32 devices in a mesh: rep: 2 (over y), sec: 4 (over x, core), tp: 4 (over z).
Axes of the slice: x: 2, y: 2, z: 4, core: 2. Of those that a mesh axis runs over, the one named last changes fastest.
Arguments:
- resid: bfloat16 [96, 5120], P(('rep', 'tp'), 'sec'), parts along dimension 0, may hold values from -6 to 6
- query: bfloat16 [96, 5120], P(('rep', 'tp'), 'sec'), parts along dimension 0, may hold values from -120 to 120
- new_kv: bfloat16 [96, 2048], P(('rep', 'tp'), 'sec'), parts along dimension 0, may hold values from -4 to 4
- key_cache: bfloat16 [96, 224, 1024], P(('rep', 'sec', 'tp')), parts along dimension 0, may hold values from -4 to 4
- cached_value_rows: bfloat16 [96, 224, 1024], P(('rep', 'sec', 'tp')), parts along dimension 0, may hold values from -6 to 6
- cache_len: int32 [96], P(('rep', 'sec', 'tp')), parts along dimension 0, may hold values from 1 to 224, as said below
- assign: int32 [96], P('rep'), parts along dimension 0, may hold values from 0 to 11, as said below
- out_weight: bfloat16 [5120, 5120], P('tp', 'sec'), may hold values from -0.078125 to 0.078125
- norm_gain: bfloat16 [5120], P('sec'), may hold values from 0.099609375 to 1.8984375
- gate_weight: bfloat16 [5120, 16384], P('sec', 'tp'), may hold values from -0.078125 to 0.078125
- up_weight: bfloat16 [5120, 16384], P('sec', 'tp'), may hold values from -0.078125 to 0.078125
- down_weight: bfloat16 [16384, 5120], P('tp', 'sec'), may hold values from -0.046875 to 0.046875
Outputs:
- layer_out: bfloat16 [96, 5120], P(('rep', 'tp'), 'sec'), parts along dimension 0
The draws below stay inside these ranges and needn't reach their ends.
There are 2 independent parts, one for each index of `rep`. The reference program is written for one: setup_inputs(seed, part) draws one part's arguments, and reference() takes and returns one part's arrays. A program takes and returns all parts, laid end to end along the dimension named above; an argument that names none is the same for every part. Nothing has to cross between parts.
Inputs may be any that keep to these rules, and one draw needn't show every extreme that they name: `assign`: each block of 12 consecutive requests names every slot 0 to 11 exactly once. `cache_len`: some cache slot has all 224 positions valid.
All inputs are finite; a program needn't handle non-finite values.
Results may differ from the reference program's by a relative error of at most 0.025.
Values may be sent and summed in bfloat16 or wider, within the bound.
A program may use at most 64 MiB of HBM per device.

```python
import math
import jax
import jax.numpy as jnp
from jax import lax

D = 5120
QUERY_HEADS = 40
KEY_VALUE_HEADS = 8
HEAD_WIDTH = 128
FFW = 16384
CACHE_SLOTS = 224
REQ_DEV = 3
GROUP = 12
REQUEST_COUNT = 48
N_SEC = 4
N_TP = 4


def clipped_normal_sample(key, array_shape):
    return jax.random.truncated_normal(key, -4.0, 4.0, array_shape, jnp.float32)


def newest_pairs(key):
    return clipped_normal_sample(jax.random.fold_in(key, 101), (REQUEST_COUNT, KEY_VALUE_HEADS, 2, HEAD_WIDTH))


def slot_table(key):
    groups = REQUEST_COUNT // GROUP
    group_keys = jax.random.split(jax.random.fold_in(key, 7), groups)
    orders = jax.vmap(lambda group_key: jax.random.permutation(group_key, GROUP))(group_keys)
    return orders.reshape(REQUEST_COUNT).astype(jnp.int32)


def draw_assign(key, part):
    return slot_table(key)


def draw_new_kv(key, part):
    key_value_pairs = newest_pairs(key)
    return key_value_pairs.reshape(REQUEST_COUNT, 2 * KEY_VALUE_HEADS * HEAD_WIDTH).astype(jnp.bfloat16)


def draw_query(key, part):
    group_query = QUERY_HEADS // KEY_VALUE_HEADS
    incoming_keys = newest_pairs(key)[:, :, 0]
    array_shape = (REQUEST_COUNT, KEY_VALUE_HEADS, group_query, HEAD_WIDTH)
    result = clipped_normal_sample(jax.random.fold_in(key, 102), array_shape) + 0.3 * incoming_keys[:, :, None, :]
    return result.reshape(REQUEST_COUNT, QUERY_HEADS * HEAD_WIDTH).astype(jnp.bfloat16)


def draw_key_cache(key, part):
    array_shape = (REQUEST_COUNT, CACHE_SLOTS, KEY_VALUE_HEADS * HEAD_WIDTH)
    base = clipped_normal_sample(jax.random.fold_in(key, 103), array_shape)
    return base.astype(jnp.bfloat16)


def draw_cache_len(key, part):
    lengths = jax.random.randint(jax.random.fold_in(key, 9), (REQUEST_COUNT,), 1, CACHE_SLOTS + 1, jnp.int32)
    longest = jax.random.randint(jax.random.fold_in(key, 10), (), 0, REQUEST_COUNT, jnp.int32)
    return lengths.at[longest].set(CACHE_SLOTS)


def level_of(rng, shape, shards, smallest, high):
    level = 1.0
    for dim, parts in shards:
        heights = jax.random.uniform(jax.random.fold_in(jax.random.fold_in(rng, 6), dim), (parts,), jnp.float32, smallest / len(shards), high / len(shards))
        level = level * jnp.repeat(jnp.exp(heights), shape[dim] // parts).reshape((-1,) + (1,) * (len(shape) - 1 - dim))
    return level


def normal_values(own_key, shape, scale, limit, shards=(), kind=jnp.bfloat16):
    values = jax.random.normal(own_key, shape, jnp.float32) * scale
    if len(shards) > 0:
        values = level_of(own_key, shape, shards, -0.22, 0.18) * values
    return jnp.clip(values, min=-limit, max=limit).astype(kind)


def setup_inputs(seed: int = 0, part: int = 0) -> dict:
    seeds = jax.random.split(jax.random.key(seed), 13)
    part_splits = jax.random.split(jax.random.fold_in(seeds[12], part), 13)
    resid = normal_values(part_splits[0], (REQUEST_COUNT, D), 1.0, 6.0, ((0, 4), (1, 4)))
    query = draw_query(jax.random.fold_in(jax.random.fold_in(seeds[12], part), 71), part)
    new_kv = draw_new_kv(jax.random.fold_in(jax.random.fold_in(seeds[12], part), 71), part)
    key_cache = draw_key_cache(jax.random.fold_in(jax.random.fold_in(seeds[12], part), 71), part)
    cached_value_rows = normal_values(part_splits[4], (REQUEST_COUNT, CACHE_SLOTS, KEY_VALUE_HEADS * HEAD_WIDTH), 1.0, 6.0, ((0, 16),))
    cache_len = draw_cache_len(jax.random.fold_in(jax.random.fold_in(seeds[12], part), 71), part)
    assign = draw_assign(jax.random.fold_in(jax.random.fold_in(seeds[12], part), 71), part)
    out_weight = normal_values(seeds[7], (QUERY_HEADS * HEAD_WIDTH, D), (QUERY_HEADS * HEAD_WIDTH) ** -0.5, 0.078125, ((0, 4), (1, 4)))
    norm_gain = jnp.clip(1.0 + 0.18 * jax.random.normal(seeds[8], (D,), jnp.float32), 0.099609375, 1.8984375).astype(jnp.bfloat16)
    gate_weight = normal_values(seeds[9], (D, FFW), D ** -0.5, 0.078125, ((0, 4), (1, 4)))
    up_weight = normal_values(seeds[10], (D, FFW), D ** -0.5, 0.078125, ((0, 4), (1, 4)))
    down_weight = normal_values(seeds[11], (FFW, D), FFW ** -0.5, 0.046875, ((0, 4), (1, 4)))
    return {"resid": resid, "query": query, "new_kv": new_kv, "key_cache": key_cache, "cached_value_rows": cached_value_rows, "cache_len": cache_len, "assign": assign, "out_weight": out_weight, "norm_gain": norm_gain, "gate_weight": gate_weight, "up_weight": up_weight, "down_weight": down_weight}


def attend_block(query_rows, key_value_pairs, stored_keys, stored_values, lengths):
    cache_slots = query_rows.shape[0]
    group_query = QUERY_HEADS // KEY_VALUE_HEADS
    query_head_rows = query_rows.astype(jnp.float32).reshape(cache_slots, KEY_VALUE_HEADS, group_query, HEAD_WIDTH)
    paired_heads = key_value_pairs.astype(jnp.float32).reshape(cache_slots, KEY_VALUE_HEADS, 2, HEAD_WIDTH)
    fresh_keys = paired_heads[:, :, 0]
    fresh_values = paired_heads[:, :, 1]
    earlier_keys = stored_keys.astype(jnp.float32).reshape(cache_slots, CACHE_SLOTS, KEY_VALUE_HEADS, HEAD_WIDTH)
    earlier_values = stored_values.astype(jnp.float32).reshape(cache_slots, CACHE_SLOTS, KEY_VALUE_HEADS, HEAD_WIDTH)
    scaling = 1.0 / math.sqrt(HEAD_WIDTH)
    past_scores = jnp.einsum('rkgd,rlkd->rkgl', query_head_rows, earlier_keys) * scaling
    fresh_scores = jnp.einsum('rkgd,rkd->rkg', query_head_rows, fresh_keys) * scaling
    valid = jnp.arange(CACHE_SLOTS, dtype=jnp.int32)[None, :] < lengths[:, None]
    past_scores = jnp.where(valid[:, None, None, :], past_scores, -1e+30)
    highest = jnp.maximum(lax.optimization_barrier(jnp.max(past_scores, axis=-1)), fresh_scores)
    past_exp = jnp.exp(past_scores - highest[..., None])
    fresh_exp = jnp.exp(fresh_scores - highest)
    denominator = lax.optimization_barrier(jnp.sum(past_exp, axis=-1)) + fresh_exp
    past_weights = lax.optimization_barrier((past_exp / denominator[..., None]).astype(jnp.bfloat16)).astype(jnp.float32)
    fresh_weights = lax.optimization_barrier((fresh_exp / denominator).astype(jnp.bfloat16)).astype(jnp.float32)
    mixed = jnp.einsum('rkgl,rlkd->rkgd', past_weights, earlier_values)
    mixed = mixed + fresh_weights[..., None] * fresh_values[:, :, None, :]
    return mixed.reshape(cache_slots, QUERY_HEADS * HEAD_WIDTH).astype(jnp.bfloat16)

def block_sum(left, right, pieces):
    width = left.shape[1] // pieces

    def add_block(index, total):
        lhs = lax.dynamic_slice_in_dim(left, index * width, width, 1)
        rhs = lax.dynamic_slice_in_dim(right, index * width, width, 0)
        term = jnp.dot(lhs, rhs, preferred_element_type=jnp.float32)
        term = lax.optimization_barrier(term.astype(jnp.bfloat16)).astype(jnp.float32)
        return total + term
    start_total = jnp.zeros((left.shape[0], right.shape[1]), jnp.float32)
    return lax.fori_loop(0, pieces, add_block, start_total)

def reference(resid, query, new_kv, key_cache, cached_value_rows, cache_len, assign, out_weight, norm_gain, gate_weight, up_weight, down_weight):
    request_ids = jnp.arange(REQUEST_COUNT, dtype=jnp.int32)
    slot_row = (assign // REQ_DEV * N_TP + request_ids // GROUP) * REQ_DEV + assign % REQ_DEV
    blocks = REQUEST_COUNT // GROUP

    def one_block(index):
        first = (index * GROUP).astype(jnp.int32)
        chosen = lax.dynamic_slice_in_dim(slot_row, first, GROUP)
        query_rows = lax.dynamic_slice_in_dim(query, first, GROUP, 0)
        key_value_pairs = lax.dynamic_slice_in_dim(new_kv, first, GROUP, 0)
        return attend_block(query_rows, key_value_pairs, key_cache[chosen], cached_value_rows[chosen], cache_len[chosen])
    attended = lax.map(one_block, jnp.arange(blocks, dtype=jnp.int32)).reshape(REQUEST_COUNT, QUERY_HEADS * HEAD_WIDTH)
    attn_out = block_sum(attended, out_weight, N_TP)
    stream = resid.astype(jnp.float32) + attn_out
    inverse = lax.rsqrt(lax.optimization_barrier(jnp.mean(stream * stream, axis=1)) + 1e-06)
    normed = (stream * inverse[:, None] * norm_gain.astype(jnp.float32)[None, :]).astype(jnp.bfloat16)
    gate = block_sum(normed, gate_weight, N_SEC)
    upper = block_sum(normed, up_weight, N_SEC)
    hidden = (jax.nn.silu(gate) * upper).astype(jnp.bfloat16)
    ff_out = block_sum(hidden, down_weight, N_TP)
    return (stream + ff_out).astype(jnp.bfloat16)
```

```python
import functools
import math

import jax
import jax.numpy as jnp
from jax import lax
from jax.experimental import pallas as pl
from jax.experimental.pallas import tpu as pltpu
from jax.sharding import PartitionSpec as P

D = 5120
QUERY_HEADS = 40
KEY_VALUE_HEADS = 8
HEAD_WIDTH = 128
CACHE_SLOTS = 224


def attend_slots(query_rows, key_value_pairs, stored_keys, stored_values, lengths):
    cache_slots = query_rows.shape[0]
    group_query = QUERY_HEADS // KEY_VALUE_HEADS
    query_head_rows = query_rows.reshape(cache_slots, KEY_VALUE_HEADS, group_query, HEAD_WIDTH)
    paired_heads = key_value_pairs.reshape(cache_slots, KEY_VALUE_HEADS, 2, HEAD_WIDTH)
    fresh_keys = paired_heads[:, :, 0]
    fresh_values = paired_heads[:, :, 1]
    earlier_keys = stored_keys.reshape(cache_slots, CACHE_SLOTS, KEY_VALUE_HEADS, HEAD_WIDTH)
    earlier_values = stored_values.reshape(cache_slots, CACHE_SLOTS, KEY_VALUE_HEADS, HEAD_WIDTH)
    scaling = 1.0 / math.sqrt(HEAD_WIDTH)
    past_scores = (
        jnp.einsum(
            "rkgd,rlkd->rkgl", query_head_rows, earlier_keys, preferred_element_type=jnp.float32
        )
        * scaling
    )
    fresh_scores = (
        jnp.einsum("rkgd,rkd->rkg", query_head_rows, fresh_keys, preferred_element_type=jnp.float32)
        * scaling
    )
    valid = lax.broadcasted_iota(jnp.int32, (cache_slots, CACHE_SLOTS), 1) < lengths[:, None]
    past_scores = jnp.where(valid[:, None, None, :], past_scores, -1e30)
    highest = jnp.maximum(jnp.max(past_scores, axis=-1), fresh_scores)
    past_exp = jnp.exp(past_scores - highest[..., None])
    fresh_exp = jnp.exp(fresh_scores - highest)
    denominator = jnp.sum(past_exp, axis=-1) + fresh_exp
    past_weights = (past_exp / denominator[..., None]).astype(jnp.bfloat16)
    fresh_weights = (fresh_exp / denominator).astype(jnp.bfloat16)
    mixed = jnp.einsum(
        "rkgl,rlkd->rkgd", past_weights, earlier_values, preferred_element_type=jnp.float32
    )
    mixed = (
        mixed
        + fresh_weights.astype(jnp.float32)[..., None]
        * fresh_values.astype(jnp.float32)[:, :, None, :]
    )
    return mixed.reshape(cache_slots, QUERY_HEADS * HEAD_WIDTH).astype(jnp.bfloat16)


def gated_units(values, width):
    return (jax.nn.silu(values[:, :width]) * values[:, width:]).astype(jnp.bfloat16)


MESH = pl.DeviceIdType.MESH
ROWS16 = 16


def up_to(count, multiple):
    return -(-count // multiple) * multiple


def fits_kernel(shapes):
    group, per_device, head_cols, width, sec, tp = shapes
    return (
        sec % 2 == 0
        and width % (sec * 256) == 0
        and head_cols % (256) == 0
        and (D // sec) % 256 == 0
        and QUERY_HEADS % tp == 0
        and QUERY_HEADS % sec == 0
        and per_device <= 8
        and per_device * sec == group
        and (group * tp) % 16 == 0
        and group * tp <= 128
    )


def fused_kernel(
    dims,
    resid_hbm,
    query_hbm,
    new_kv_hbm,
    assign_hbm,
    gain_hbm,
    lengths_hbm,
    keys,
    values,
    w_out,
    w_gate,
    w_up,
    w_down,
    out,
    resid,
    query,
    new_kv,
    assign,
    gain,
    lengths,
    kbuf,
    vbuf,
    wo,
    wg,
    wu,
    wd,
    a_q,
    a_kv,
    a_q_in,
    a_kv_in,
    qheads,
    oheads,
    slot_rows,
    b1,
    b1_in,
    b2_in,
    ord_buf,
    c_out,
    c_in,
    d_in,
    q_in,
    x_buf,
    s_in,
    e_out,
    pair_in,
    e_in,
    f_in,
    acc,
    g_out,
    g_in,
    stream_buf,
    local_sem,
    sec_send,
    sec_recv,
    tp_send,
    tp_recv,
    hop_send,
    hop_recv,
):
    S, T, G, R = dims
    N = G * T
    TR = T * R
    TRP = up_to(TR, ROWS16)
    Dl = resid.shape[1]
    Hl = w_out.shape[0]
    F = w_gate.shape[1]
    Fs = F // S
    f32, bf16 = jnp.float32, jnp.bfloat16
    s = lax.axis_index("sec")
    t = lax.axis_index("tp")
    sx, sc = s // 2, s % 2
    half = S // 2
    steps = [(dx, dc) for dx in list(range(1, half)) + [0] for dc in (0, 1) if dx or dc]
    sec_peers = [((sx + dx) % half) * 2 + (sc + dc) % 2 for dx, dc in steps]
    tp_peers = [(t + k) % T for k in sorted(range(1, T), key=lambda k: -min(k, T - k))]

    barrier = pltpu.get_barrier_semaphore()
    for c in sec_peers:
        pl.semaphore_signal(barrier, inc=1, device_id={"sec": c}, device_id_type=MESH)
    for c in tp_peers:
        pl.semaphore_signal(barrier, inc=1, device_id={"tp": c}, device_id_type=MESH)

    copies = {}
    count = [0]

    def fetch(name, src, dst):
        copy = pltpu.make_async_copy(src, dst, local_sem.at[count[0]])
        count[0] += 1
        copy.start()
        copies[name] = copy

    fetch("assign", assign_hbm, assign)
    fetch("query", query_hbm, query)
    fetch("new_kv", new_kv_hbm, new_kv)
    fetch("lengths", lengths_hbm, lengths)
    fetch("resid", resid_hbm, resid)
    fetch("gain", gain_hbm, gain)
    for r in range(R):
        fetch(("k", r), keys.at[r], kbuf.at[r])
        fetch(("v", r), values.at[r], vbuf.at[r])
    def at_step(dx, dc):
        return ((sx + dx) % half) * 2 + (sc + dc) % 2

    order = [(dx, dc) for dx in list(range(1, half)) + [0] for dc in (1, 0)]

    hs = QUERY_HEADS // S
    ht = QUERY_HEADS // T
    HW = HEAD_WIDTH
    GQ = QUERY_HEADS // KEY_VALUE_HEADS
    GP = up_to(G, ROWS16)
    RQ = a_q.shape[1]
    copies["assign"].wait()
    row_a = assign[...].astype(f32)
    ii = lax.broadcasted_iota(jnp.int32, (N, N), 0)
    jj = lax.broadcasted_iota(jnp.int32, (N, N), 1)
    col_a = jnp.sum(jnp.where(ii == jj, jnp.broadcast_to(row_a, (N, N)), 0.0), axis=1, keepdims=True)

    def own_slots(width):
        pi = lax.broadcasted_iota(jnp.int32, (N, width), 0)
        pj = lax.broadcasted_iota(jnp.int32, (N, width), 1)
        hit = pi == pj + t * G
        if width > G:
            stripe = jnp.zeros((N, width), jnp.int32)
            for j in range(1, width // GP):
                stripe = stripe + jnp.where(pj >= j * GP, GP, 0)
            hit = pi == pj - stripe + t * G
            hit = hit & (pj - stripe < G)
        return jnp.sum(
            jnp.where(hit, jnp.broadcast_to(col_a, (N, width)), 0.0)
            + jnp.where(hit, 1.0, 0.0),
            axis=0,
            keepdims=True,
        ) - 1.0

    pr = lax.broadcasted_iota(jnp.int32, (S * 8, 1), 0)
    slot = jnp.full((S * 8, 1), -2.0, f32)
    for c in range(S):
        for r in range(R):
            slot = jnp.where(pr == c * 8 + r, float(c * R + r), slot)
    picker = jnp.where(
        jnp.broadcast_to(slot, (S * 8, G)) == jnp.broadcast_to(own_slots(G), (S * 8, G)), 1.0, 0.0
    ).astype(bf16)
    qr = lax.broadcasted_iota(jnp.int32, (S * RQ, 1), 0)
    block = jnp.zeros((S * RQ, 1), jnp.int32)
    for c in range(1, S):
        block = block + jnp.where(qr >= c * RQ, 1, 0)
    place = qr - block * RQ
    turn = jnp.zeros((S * RQ, 1), jnp.int32)
    for r in range(1, R):
        turn = turn + jnp.where(place >= r * hs, 1, 0)
    qc = lax.broadcasted_iota(jnp.int32, (1, hs * GP), 1)
    stripe = jnp.zeros((1, hs * GP), jnp.int32)
    for j in range(1, hs):
        stripe = stripe + jnp.where(qc >= j * GP, 1, 0)
    wanted = jnp.where(place < R * hs, block * R + turn, -2).astype(f32)
    q_picker = jnp.where(
        (jnp.broadcast_to(wanted, (S * RQ, hs * GP)) == jnp.broadcast_to(own_slots(hs * GP), (S * RQ, hs * GP)))
        & (jnp.broadcast_to(place - turn * hs, (S * RQ, hs * GP)) == jnp.broadcast_to(stripe, (S * RQ, hs * GP))),
        1.0,
        0.0,
    ).astype(bf16)
    copies["query"].wait()
    tall = query[...].astype(f32)
    if GP > G:
        tall = jnp.concatenate([tall, jnp.zeros((GP - G, Dl), f32)], axis=0)
    stacked = jnp.concatenate([tall[:, j * HW : (j + 1) * HW] for j in range(hs)], axis=0).astype(bf16)
    picked_q = jnp.dot(q_picker, stacked, preferred_element_type=f32).astype(bf16)
    for c in range(S):
        a_q[c] = picked_q[c * RQ : (c + 1) * RQ]
    copies["new_kv"].wait()
    picked_kv = jnp.dot(picker, new_kv[...], preferred_element_type=f32)
    for c in range(S):
        a_kv[c] = picked_kv[c * 8 : c * 8 + 8].astype(bf16)
    pl.semaphore_wait(barrier, len(sec_peers) + len(tp_peers))

    started = []

    def sec_push(phase, i, src, dst):
        copy = pltpu.make_async_remote_copy(
            src_ref=src,
            dst_ref=dst,
            send_sem=sec_send.at[phase, i],
            recv_sem=sec_recv.at[phase, i],
            device_id={"sec": sec_peers[i]},
            device_id_type=MESH,
        )
        copy.start()
        started.append(copy)
        return copy

    def tp_push(phase, i, src, dst):
        copy = pltpu.make_async_remote_copy(
            src_ref=src,
            dst_ref=dst,
            send_sem=tp_send.at[phase, i],
            recv_sem=tp_recv.at[phase, i],
            device_id={"tp": tp_peers[i]},
            device_id_type=MESH,
        )
        copy.start()
        started.append(copy)
        return copy

    SP, TP = len(sec_peers), len(tp_peers)
    pend = []
    for i in range(SP):
        pend.append(sec_push(0, i, a_q.at[sec_peers[i]], a_q_in.at[s]))
        pend.append(sec_push(1, i, a_kv.at[sec_peers[i]], a_kv_in.at[s]))
    a_q_in[s] = a_q[s]
    a_kv_in[s] = a_kv[s]
    oheads[...] = jnp.zeros(oheads.shape, f32)
    slot_rows[...] = jnp.zeros(slot_rows.shape, f32)
    for copy in pend:
        copy.wait_recv()

    fetch("wo", w_out, wo)
    for step in order:
        c = at_step(*step)
        cols = pl.ds(pl.multiple_of(c * Fs, Fs), Fs)
        fetch(("g", step), w_gate.at[:, cols], wg.at[c])
        fetch(("u", step), w_up.at[:, cols], wu.at[c])

    copies["lengths"].wait()
    for r in range(R):
        copies[("k", r)].wait()
        copies[("v", r)].wait()
    for c in range(S):
        blk = a_q_in[c].astype(f32)
        for r in range(R):
            qheads[r, c * hs : (c + 1) * hs, :] = blk[r * hs : (r + 1) * hs, :]
    pairs = jnp.concatenate([a_kv_in[c].astype(f32) for c in range(S)], axis=1)
    new_k = jnp.concatenate(
        [pairs[:, 2 * k * HW : (2 * k + 1) * HW] for k in range(KEY_VALUE_HEADS)], axis=1
    )
    new_v = jnp.concatenate(
        [pairs[:, (2 * k + 1) * HW : (2 * k + 2) * HW] for k in range(KEY_VALUE_HEADS)], axis=1
    )
    KW = KEY_VALUE_HEADS * HW
    hrow = lax.broadcasted_iota(jnp.int32, (QUERY_HEADS, KW), 0)
    hcol = lax.broadcasted_iota(jnp.int32, (QUERY_HEADS, KW), 1)
    low = jnp.zeros((QUERY_HEADS, KW), jnp.int32)
    for k in range(1, KEY_VALUE_HEADS):
        low = low + jnp.where(hcol >= k * HW, 1, 0)
    diag = (hrow >= low * GQ) & (hrow < low * GQ + GQ)
    scaling = 1.0 / math.sqrt(HW)
    slots = keys.shape[1]
    each = range(R)
    wide_q = [
        jnp.where(diag, jnp.concatenate([qheads[r]] * KEY_VALUE_HEADS, axis=1), 0.0) for r in each
    ]
    past = [
        lax.dot_general(
            wide_q[r].astype(bf16),
            kbuf[r],
            (((1,), (1,)), ((), ())),
            preferred_element_type=f32,
        )
        * scaling
        for r in each
    ]
    fresh = [
        jnp.sum(wide_q[r] * new_k[r : r + 1, :], axis=1, keepdims=True) * scaling for r in each
    ]
    position = lax.broadcasted_iota(jnp.int32, (QUERY_HEADS, slots), 1)
    past = [jnp.where(position < lengths[r], past[r], -1e30) for r in each]
    highest = [jnp.maximum(jnp.max(past[r], axis=1, keepdims=True), fresh[r]) for r in each]
    past_exp = [jnp.exp(past[r] - highest[r]) for r in each]
    fresh_exp = [jnp.exp(fresh[r] - highest[r]) for r in each]
    total = [jnp.sum(past_exp[r], axis=1, keepdims=True) + fresh_exp[r] for r in each]
    past_w = [(past_exp[r] / total[r]).astype(bf16) for r in each]
    fresh_w = [(fresh_exp[r] / total[r]).astype(bf16).astype(f32) for r in each]
    mixed = [jnp.dot(past_w[r], vbuf[r], preferred_element_type=f32) for r in each]
    for r in each:
        spread = jnp.where(diag, mixed[r] + fresh_w[r] * new_v[r : r + 1, :], 0.0)
        small = spread[:, 0:HW]
        for k in range(1, KEY_VALUE_HEADS):
            small = small + spread[:, k * HW : (k + 1) * HW]
        for c in range(T):
            oheads[c, r * ht : (r + 1) * ht, :] = small[c * ht : (c + 1) * ht, :]
    for c in range(T):
        b1[c] = oheads[c].astype(bf16)
    pend = [tp_push(0, i, b1.at[tp_peers[i]], b1_in.at[t]) for i in range(TP)]
    b1_in[t] = b1[t]
    for step in reversed(order):
        c = at_step(*step)
        rows = pl.ds(pl.multiple_of(c * Fs, Fs), Fs)
        fetch(("d", step), w_down.at[rows, :], wd.at[c])

    def fold(value):
        return jnp.concatenate([value[:, : Dl // 2], value[:, Dl // 2 :]], axis=0).astype(bf16)

    def unfold(value):
        return jnp.concatenate([value[:G], value[G:]], axis=1)

    pos = jnp.zeros((1, N), f32)
    for a in range(G):
        pos = pos + jnp.where(row_a == float(a), float((a // R) * TRP + a % R), 0.0)
    lane = lax.broadcasted_iota(jnp.int32, (1, N), 1)
    for g in range(1, T):
        pos = pos + jnp.where(lane >= g * G, float(R), 0.0)
    pos_col = jnp.sum(jnp.where(ii == jj, pos, 0.0), axis=1, keepdims=True)
    oj = lax.broadcasted_iota(jnp.int32, (N, S * TRP), 1).astype(f32)
    reorder = jnp.where(oj == pos_col, 1.0, 0.0).astype(bf16)
    for copy in pend:
        copy.wait_recv()
    for c in range(T):
        blk = b1_in[c].astype(f32)
        for r in range(R):
            for j in range(ht):
                slot_rows[c * R + r : c * R + r + 1, j * HW : (j + 1) * HW] = blk[
                    r * ht + j : r * ht + j + 1, :
                ]
    b2_in[s] = slot_rows[...].astype(bf16)
    pend = [sec_push(2, i, b2_in.at[s], b2_in.at[s]) for i in range(SP)]
    copies["wo"].wait()
    for copy in pend:
        copy.wait_recv()
    rows = jnp.concatenate([b2_in[c] for c in range(S)], axis=0)
    ord_buf[...] = jnp.dot(reorder, rows, preferred_element_type=f32).astype(bf16)

    def project(i, carry):
        cols = pl.ds(pl.multiple_of(i * 256, 256), 256)
        acc[:, cols] = jnp.dot(ord_buf[...], wo[:, cols], preferred_element_type=f32)
        return carry

    lax.fori_loop(0, Dl // 256, project, 0, unroll=True)
    for g in range(T):
        c_out[g] = fold(acc[g * G : (g + 1) * G, :])
    pend = [tp_push(1, i, c_out.at[tp_peers[i]], c_in.at[t]) for i in range(TP)]
    c_in[t] = c_out[t]
    for copy in pend:
        copy.wait_recv()
    attn = c_in[0].astype(f32)
    for g in range(1, T):
        attn = attn + c_in[g].astype(f32)
    copies["resid"].wait()
    copies["gain"].wait()
    stream = resid[...].astype(f32) + unfold(attn)
    stream_buf[...] = stream
    d_in[t] = fold(stream * gain[...].astype(f32).reshape(1, Dl))
    squares = jnp.sum(stream * stream, axis=1, keepdims=True)
    qi = lax.broadcasted_iota(jnp.int32, (G, 128), 0)
    qj = lax.broadcasted_iota(jnp.int32, (G, 128), 1)
    squares = jnp.where(qj == qi + t * G, squares, 0.0)
    q_in[t] = jnp.broadcast_to(jnp.sum(squares, axis=0, keepdims=True), (8, 128))
    pend = [tp_push(2, i, d_in.at[t], d_in.at[t]) for i in range(TP)]
    pend_q = [tp_push(3, i, q_in.at[t], q_in.at[t]) for i in range(TP)]
    for copy in pend:
        copy.wait_recv()
    for g in range(T):
        acc[g * G : (g + 1) * G, :] = unfold(d_in[g].astype(f32))
    x_buf[...] = acc[...].astype(bf16)

    mate = at_step(0, 1)
    pushed = [0]

    def push(dest, src, dst):
        copy = pltpu.make_async_remote_copy(
            src_ref=src,
            dst_ref=dst,
            send_sem=hop_send.at[pushed[0]],
            recv_sem=hop_recv.at[pushed[0]],
            device_id={"sec": dest},
            device_id_type=MESH,
        )
        pushed[0] += 1
        copy.start()
        started.append(copy)
        return copy

    def widen(step, part):
        c = at_step(*step)
        copies[("gu"[part], step)].wait()
        weight = (wg, wu)[part]

        def tile(j, carry):
            cols = pl.ds(pl.multiple_of(j * 256, 256), 256)
            into = pl.ds(pl.multiple_of(part * Fs + j * 256, 256), 256)
            e_out[c, :, into] = jnp.dot(
                x_buf[...], weight[c, :, cols], preferred_element_type=f32
            ).astype(bf16)
            return carry

        lax.fori_loop(0, Fs // 256, tile, 0, unroll=True)
        return c

    parts = [pl.ds(0, Fs), pl.ds(Fs, Fs)]
    far_sums = []
    for dx in range(1, half):
        fx = (sx + dx) % half
        pair = []
        for part in (0, 1):
            c = widen((dx, 1), part)
            pair.append(push(mate, e_out.at[c, :, parts[part]], pair_in.at[fx, :, parts[part]]))
        for part in (0, 1):
            c = widen((dx, 0), part)
            pair[part].wait_recv()
            e_out[c, :, parts[part]] = (
                e_out[c, :, parts[part]].astype(f32) + pair_in[fx, :, parts[part]].astype(f32)
            ).astype(bf16)
            far_sums.append(push(c, e_out.at[c, :, parts[part]], e_in.at[sx, :, parts[part]]))
    for copy in pend_q:
        copy.wait_recv()
    squares = q_in[0]
    for g in range(1, T):
        squares = squares + q_in[g]
    s_in[s] = squares
    pend_s = [sec_push(4, k, s_in.at[s], s_in.at[s]) for k in range(SP)]
    pair = []
    for part in (0, 1):
        c = widen((0, 1), part)
        pair.append(push(mate, e_out.at[c, :, parts[part]], pair_in.at[sx, :, parts[part]]))
    for part in (0, 1):
        widen((0, 0), part)
    for copy in pend_s:
        copy.wait_recv()
    squares = s_in[0]
    for c in range(1, S):
        squares = squares + s_in[c]
    inverse = lax.rsqrt(squares[0:1, :] / D + 1e-06)
    ni = lax.broadcasted_iota(jnp.int32, (N, 128), 0)
    nj = lax.broadcasted_iota(jnp.int32, (N, 128), 1)
    inverse = jnp.sum(jnp.where(ni == nj, inverse, 0.0), axis=1, keepdims=True)
    for copy in pair + far_sums:
        copy.wait_recv()
    halves = [pl.ds(0, Fs // 2), pl.ds(Fs // 2, Fs // 2)]
    to_mate, from_far = [], {}
    for h in (0, 1):
        for j in range(Fs // 256):
            lo, hi = h * (Fs // 2) + j * 128, h * (Fs // 2) + (j + 1) * 128

            def total(lo, hi):
                value = e_out[s, :, lo:hi].astype(f32) + pair_in[sx, :, lo:hi].astype(f32)
                for dx in range(1, half):
                    value = value + e_in[(sx + dx) % half, :, lo:hi].astype(f32)
                return value * inverse

            gate, upper = total(lo, hi), total(Fs + lo, Fs + hi)
            f_in[s, :, lo:hi] = (gate / (1.0 + jnp.exp(-gate)) * upper).astype(bf16)
        piece = f_in.at[s, :, halves[h]]
        for dx in range(1, half):
            from_far[(half - dx, h)] = push(at_step(dx, 0), piece, piece)
        to_mate.append(push(mate, piece, piece))

    def lower(step, first=False):
        c = at_step(*step)
        copies[("d", step)].wait()

        def tile(j, carry):
            cols = pl.ds(pl.multiple_of(j * 256, 256), 256)
            part = jnp.dot(f_in[c], wd[c, :, cols], preferred_element_type=f32)
            if not first:
                part = part + acc[:, cols]
            acc[:, cols] = part
            return carry

        lax.fori_loop(0, Dl // 256, tile, 0, unroll=True)

    lower((0, 0), True)
    for copy in to_mate:
        copy.wait_recv()
    lower((0, 1))
    for dx in range(1, half):
        relayed = []
        for h in (0, 1):
            from_far[(dx, h)].wait_recv()
            piece = f_in.at[at_step(dx, 0), :, halves[h]]
            relayed.append(push(mate, piece, piece))
        lower((dx, 0))
        for copy in relayed:
            copy.wait_recv()
        lower((dx, 1))
    for g in range(T):
        g_out[g] = fold(acc[g * G : (g + 1) * G, :])
    pend = [tp_push(4, i, g_out.at[tp_peers[i]], g_in.at[t]) for i in range(TP)]
    g_in[t] = g_out[t]
    for copy in pend:
        copy.wait_recv()
    total = stream_buf[...]
    ff = g_in[0].astype(f32)
    for g in range(1, T):
        ff = ff + g_in[g].astype(f32)
    out[...] = (total + unfold(ff)).astype(bf16)
    for copy in started:
        copy.wait_send()


def local(
    resid,
    query,
    new_kv,
    key_cache,
    cached_value_rows,
    cache_len,
    assign,
    out_weight,
    norm_gain,
    gate_weight,
    up_weight,
    down_weight,
):
    group = query.shape[0]
    per_device = key_cache.shape[0]
    tp_index = lax.axis_index("tp")
    sec_index = lax.axis_index("sec")
    tp_count = lax.axis_size("tp")
    local_slots = lax.dynamic_slice_in_dim(assign, tp_index * group, group)
    full_query, full_pairs = (
        lax.all_gather(query, "sec", axis=1, tiled=True),
        lax.all_gather(new_kv, "sec", axis=1, tiled=True),
    )
    wanted = sec_index * per_device + lax.iota(jnp.int32, per_device)
    picker = (local_slots[None, :] == wanted[:, None]).astype(jnp.bfloat16)
    my_query = jnp.dot(picker, full_query, preferred_element_type=jnp.float32).astype(jnp.bfloat16)
    my_pairs = jnp.dot(picker, full_pairs, preferred_element_type=jnp.float32).astype(jnp.bfloat16)
    attended = attend_slots(my_query, my_pairs, key_cache, cached_value_rows, cache_len)
    request_ids = lax.iota(jnp.int32, group * tp_count)
    slot_block = lax.all_gather(attended, "sec", axis=0, tiled=True)
    received = lax.all_to_all(slot_block, "tp", split_axis=1, concat_axis=0, tiled=True)
    position = request_ids // group * group + assign
    ordered = jnp.take(received, position, axis=0)
    block = ordered
    attn_out = lax.psum_scatter(
        jnp.dot(block, out_weight, preferred_element_type=jnp.float32).astype(jnp.bfloat16),
        "tp",
        scatter_dimension=0,
        tiled=True,
    ).astype(jnp.float32)
    stream = resid.astype(jnp.float32) + attn_out
    squares = lax.psum(jnp.sum(stream * stream, axis=1), "sec")
    inverse = lax.rsqrt(squares / D + 1e-06)
    normed = (stream * inverse[:, None] * norm_gain.astype(jnp.float32)[None, :]).astype(
        jnp.bfloat16
    )
    piece = lax.all_gather(normed, "tp", axis=0, tiled=True)
    gate_part = jnp.dot(piece, gate_weight, preferred_element_type=jnp.float32)
    up_part = jnp.dot(piece, up_weight, preferred_element_type=jnp.float32)
    projected = jnp.concatenate([gate_part, up_part], axis=1)
    width = gate_weight.shape[1]
    share = lax.psum_scatter(
        projected.astype(jnp.bfloat16), "sec", scatter_dimension=0, tiled=True
    ).astype(jnp.float32)
    hidden = lax.all_gather(gated_units(share, width), "sec", axis=0, tiled=True)
    block = hidden
    ff_out = lax.psum_scatter(
        jnp.dot(block, down_weight, preferred_element_type=jnp.float32).astype(jnp.bfloat16),
        "tp",
        scatter_dimension=0,
        tiled=True,
    ).astype(jnp.float32)
    return (stream + ff_out).astype(jnp.bfloat16)


def fused(
    resid,
    query,
    new_kv,
    key_cache,
    cached_value_rows,
    cache_len,
    assign,
    out_weight,
    norm_gain,
    gate_weight,
    up_weight,
    down_weight,
):
    S, T = lax.axis_size("sec"), lax.axis_size("tp")
    G, R = query.shape[0], key_cache.shape[0]
    N = G * T
    RH = up_to(R * (QUERY_HEADS // T), ROWS16)
    RQ = up_to(R * (QUERY_HEADS // S), ROWS16)
    TRP = up_to(T * R, ROWS16)
    Dl, Hl, F, kvl = resid.shape[1], out_weight.shape[0], gate_weight.shape[1], new_kv.shape[1]
    Fs = F // S
    bf16, f32 = jnp.bfloat16, jnp.float32
    V = pltpu.VMEM
    vm = pl.BlockSpec(memory_space=pltpu.VMEM)
    hbm = pl.BlockSpec(memory_space=pl.ANY)
    scratch = [
        V(resid.shape, bf16),
        V(query.shape, bf16),
        V(new_kv.shape, bf16),
        V((1, N), jnp.int32),
        V(norm_gain.shape, bf16),
        pltpu.SMEM(cache_len.shape, jnp.int32),
        V(key_cache.shape, bf16),
        V(cached_value_rows.shape, bf16),
        V((Hl, Dl), bf16),
        V((S, Dl, Fs), bf16),
        V((S, Dl, Fs), bf16),
        V((S, Fs, Dl), bf16),
        V((S, RQ, HEAD_WIDTH), bf16),
        V((S, 8, kvl), bf16),
        V((S, RQ, HEAD_WIDTH), bf16),
        V((S, 8, kvl), bf16),
        V((R, QUERY_HEADS, HEAD_WIDTH), f32),
        V((T, RH, HEAD_WIDTH), f32),
        V((TRP, Hl), f32),
        V((T, RH, HEAD_WIDTH), bf16),
        V((T, RH, HEAD_WIDTH), bf16),
        V((S, TRP, Hl), bf16),
        V((N, Hl), bf16),
        V((T, 2 * G, Dl // 2), bf16),
        V((T, 2 * G, Dl // 2), bf16),
        V((T, 2 * G, Dl // 2), bf16),
        V((T, 8, 128), f32),
        V((N, Dl), bf16),
        V((S, 8, 128), f32),
        V((S, N, 2 * Fs), bf16),
        V((S // 2, N, 2 * Fs), bf16),
        V((S // 2, N, 2 * Fs), bf16),
        V((S, N, Fs), bf16),
        V((N, Dl), f32),
        V((T, 2 * G, Dl // 2), bf16),
        V((T, 2 * G, Dl // 2), bf16),
        V((G, Dl), f32),
        pltpu.SemaphoreType.DMA((2 * R + 7 + 3 * S,)),
        pltpu.SemaphoreType.DMA((6, S - 1)),
        pltpu.SemaphoreType.DMA((6, S - 1)),
        pltpu.SemaphoreType.DMA((5, T - 1)),
        pltpu.SemaphoreType.DMA((5, T - 1)),
        pltpu.SemaphoreType.DMA((5 * S,)),
        pltpu.SemaphoreType.DMA((5 * S,)),
    ]
    return pl.pallas_call(
        functools.partial(fused_kernel, (S, T, G, R)),
        out_shape=pltpu.VMEM(resid.shape, bf16),
        in_specs=[hbm] * 12,
        out_specs=vm,
        scratch_shapes=scratch,
        compiler_params=pltpu.CompilerParams(
            collective_id=0, has_side_effects=True, vmem_limit_bytes=54 * 2**20
        ),
    )(
        resid,
        query,
        new_kv,
        assign.reshape(1, N),
        norm_gain,
        cache_len,
        key_cache,
        cached_value_rows,
        out_weight,
        gate_weight,
        up_weight,
        down_weight,
    )


def layer(*args):
    query, key_cache, out_weight, gate_weight = args[1], args[3], args[7], args[9]
    shapes = (
        query.shape[0],
        key_cache.shape[0],
        out_weight.shape[0],
        gate_weight.shape[1],
        lax.axis_size("sec"),
        lax.axis_size("tp"),
    )
    return fused(*args) if fits_kernel(shapes) else local(*args)


def solution(mesh):
    return jax.shard_map(
        layer,
        mesh=mesh,
        in_specs=(
            P(("rep", "tp"), "sec"),
            P(("rep", "tp"), "sec"),
            P(("rep", "tp"), "sec"),
            P(("rep", "sec", "tp"), None, None),
            P(("rep", "sec", "tp"), None, None),
            P(("rep", "sec", "tp")),
            P("rep"),
            P("tp", "sec"),
            P("sec"),
            P("sec", "tp"),
            P("sec", "tp"),
            P("tp", "sec"),
        ),
        out_specs=P(("rep", "tp"), "sec"),
        check_vma=False,
    )
```

```python
import functools
import math

import jax
import jax.numpy as jnp
from jax import lax
from jax.experimental import pallas as pl
from jax.experimental.pallas import tpu as pltpu
from jax.sharding import PartitionSpec as P

D = 5120
QUERY_HEADS = 40
KEY_VALUE_HEADS = 8
HEAD_WIDTH = 128
CACHE_SLOTS = 224


def attend_slots(query_rows, key_value_pairs, stored_keys, stored_values, lengths):
    cache_slots = query_rows.shape[0]
    group_query = QUERY_HEADS // KEY_VALUE_HEADS
    query_head_rows = query_rows.reshape(cache_slots, KEY_VALUE_HEADS, group_query, HEAD_WIDTH)
    paired_heads = key_value_pairs.reshape(cache_slots, KEY_VALUE_HEADS, 2, HEAD_WIDTH)
    fresh_keys = paired_heads[:, :, 0]
    fresh_values = paired_heads[:, :, 1]
    earlier_keys = stored_keys.reshape(cache_slots, CACHE_SLOTS, KEY_VALUE_HEADS, HEAD_WIDTH)
    earlier_values = stored_values.reshape(cache_slots, CACHE_SLOTS, KEY_VALUE_HEADS, HEAD_WIDTH)
    scaling = 1.0 / math.sqrt(HEAD_WIDTH)
    past_scores = (
        jnp.einsum(
            "rkgd,rlkd->rkgl", query_head_rows, earlier_keys, preferred_element_type=jnp.float32
        )
        * scaling
    )
    fresh_scores = (
        jnp.einsum("rkgd,rkd->rkg", query_head_rows, fresh_keys, preferred_element_type=jnp.float32)
        * scaling
    )
    valid = lax.broadcasted_iota(jnp.int32, (cache_slots, CACHE_SLOTS), 1) < lengths[:, None]
    past_scores = jnp.where(valid[:, None, None, :], past_scores, -1e30)
    highest = jnp.maximum(jnp.max(past_scores, axis=-1), fresh_scores)
    past_exp = jnp.exp(past_scores - highest[..., None])
    fresh_exp = jnp.exp(fresh_scores - highest)
    denominator = jnp.sum(past_exp, axis=-1) + fresh_exp
    past_weights = (past_exp / denominator[..., None]).astype(jnp.bfloat16)
    fresh_weights = (fresh_exp / denominator).astype(jnp.bfloat16)
    mixed = jnp.einsum(
        "rkgl,rlkd->rkgd", past_weights, earlier_values, preferred_element_type=jnp.float32
    )
    mixed = (
        mixed
        + fresh_weights.astype(jnp.float32)[..., None]
        * fresh_values.astype(jnp.float32)[:, :, None, :]
    )
    return mixed.reshape(cache_slots, QUERY_HEADS * HEAD_WIDTH).astype(jnp.bfloat16)


def gated_units(values, width):
    return (jax.nn.silu(values[:, :width]) * values[:, width:]).astype(jnp.bfloat16)


MESH = pl.DeviceIdType.MESH
ROWS16 = 16
HIDDEN_PARTS = 2


def up_to(count, multiple):
    return -(-count // multiple) * multiple


def fits_kernel(shapes):
    group, per_device, head_cols, width, sec, tp = shapes
    return (
        sec % 2 == 0
        and sec >= 4
        and width % (sec * 256 * HIDDEN_PARTS) == 0
        and width % (sec * 256) == 0
        and head_cols % (256) == 0
        and (D // sec) % 256 == 0
        and D // sec >= 512
        and QUERY_HEADS % tp == 0
        and QUERY_HEADS % sec == 0
        and per_device <= 8
        and tp >= 2
        and per_device * sec == group
        and (group * tp) % 16 == 0
        and group * tp <= 128
    )


def fused_kernel(
    dims,
    resid_hbm,
    query_hbm,
    new_kv_hbm,
    assign_hbm,
    gain_hbm,
    lengths_hbm,
    keys,
    values,
    w_out,
    w_gate,
    w_up,
    w_down,
    out,
    resid,
    query,
    new_kv,
    assign,
    gain,
    lengths,
    kbuf,
    vbuf,
    wo,
    wg,
    wu,
    wd,
    a_q,
    a_kv,
    a_q_in,
    a_kv_in,
    qheads,
    oheads,
    b1,
    b2_in,
    pick_buf,
    ord_buf,
    c_out,
    c_in,
    d_in,
    q_in,
    x_buf,
    s_in,
    e_out,
    pair_in,
    e_in,
    f_in,
    acc,
    far_acc,
    near_acc,
    g_out,
    g_in,
    stream_buf,
    local_sem,
    send_sem,
    recv_sem,
):
    S, T, G, R, NH = dims
    N = G * T
    RH = b1.shape[1]
    Dl = resid.shape[1]
    F = w_gate.shape[1]
    Fs = F // S
    f32, bf16 = jnp.float32, jnp.bfloat16
    s = lax.axis_index("sec")
    t = lax.axis_index("tp")
    sx, sc = s // 2, s % 2
    half = S // 2
    steps = [(dx, dc) for dx in list(range(1, half)) + [0] for dc in (0, 1) if dx or dc]
    sec_peers = [((sx + dx) % half) * 2 + (sc + dc) % 2 for dx, dc in steps]
    tp_peers = [(t + k) % T for k in sorted(range(1, T), key=lambda k: -min(k, T - k))]

    twin = sx * 2 + (1 - sc)
    barrier = pltpu.get_barrier_semaphore()
    for c in sec_peers:
        pl.semaphore_signal(barrier, inc=1, device_id={"sec": c}, device_id_type=MESH)
    for c in tp_peers:
        pl.semaphore_signal(barrier, inc=1, device_id={"tp": c}, device_id_type=MESH)
        pl.semaphore_signal(
            barrier, inc=1, device_id={"sec": twin, "tp": c}, device_id_type=MESH
        )

    copies = {}
    count = [0]

    def fetch(name, src, dst):
        copy = pltpu.make_async_copy(src, dst, local_sem.at[count[0]])
        count[0] += 1
        copy.start()
        copies[name] = copy

    fetch("assign", assign_hbm, assign)
    fetch("query", query_hbm, query)
    fetch("new_kv", new_kv_hbm, new_kv)
    fetch("lengths", lengths_hbm, lengths)
    fetch("resid", resid_hbm, resid)
    fetch("gain", gain_hbm, gain)
    for r in range(R):
        fetch(("k", r), keys.at[r], kbuf.at[r])
        fetch(("v", r), values.at[r], vbuf.at[r])
    def at_step(dx, dc):
        return ((sx + dx) % half) * 2 + (sc + dc) % 2

    order = [(dx, dc) for dx in list(range(1, half)) + [0] for dc in (1, 0)]

    hs = QUERY_HEADS // S
    ht = QUERY_HEADS // T
    HW = HEAD_WIDTH
    GQ = QUERY_HEADS // KEY_VALUE_HEADS
    GP = up_to(G, ROWS16)
    RQ = a_q.shape[1]
    copies["assign"].wait()
    row_a = assign[...].astype(f32)
    ii = lax.broadcasted_iota(jnp.int32, (N, N), 0)
    jj = lax.broadcasted_iota(jnp.int32, (N, N), 1)
    col_a = jnp.sum(jnp.where(ii == jj, jnp.broadcast_to(row_a, (N, N)), 0.0), axis=1, keepdims=True)

    def own_slots(width):
        pi = lax.broadcasted_iota(jnp.int32, (N, width), 0)
        pj = lax.broadcasted_iota(jnp.int32, (N, width), 1)
        hit = pi == pj + t * G
        if width > G:
            stripe = jnp.zeros((N, width), jnp.int32)
            for j in range(1, width // GP):
                stripe = stripe + jnp.where(pj >= j * GP, GP, 0)
            hit = pi == pj - stripe + t * G
            hit = hit & (pj - stripe < G)
        return jnp.sum(
            jnp.where(hit, jnp.broadcast_to(col_a, (N, width)), 0.0)
            + jnp.where(hit, 1.0, 0.0),
            axis=0,
            keepdims=True,
        ) - 1.0

    pr = lax.broadcasted_iota(jnp.int32, (S * 8, 1), 0)
    slot = jnp.full((S * 8, 1), -2.0, f32)
    for c in range(S):
        for r in range(R):
            slot = jnp.where(pr == c * 8 + r, float(c * R + r), slot)
    picker = jnp.where(
        jnp.broadcast_to(slot, (S * 8, G)) == jnp.broadcast_to(own_slots(G), (S * 8, G)), 1.0, 0.0
    ).astype(bf16)
    qr = lax.broadcasted_iota(jnp.int32, (S * RQ, 1), 0)
    block = jnp.zeros((S * RQ, 1), jnp.int32)
    for c in range(1, S):
        block = block + jnp.where(qr >= c * RQ, 1, 0)
    place = qr - block * RQ
    turn = jnp.zeros((S * RQ, 1), jnp.int32)
    for r in range(1, R):
        turn = turn + jnp.where(place >= r * hs, 1, 0)
    qc = lax.broadcasted_iota(jnp.int32, (1, hs * GP), 1)
    stripe = jnp.zeros((1, hs * GP), jnp.int32)
    for j in range(1, hs):
        stripe = stripe + jnp.where(qc >= j * GP, 1, 0)
    wanted = jnp.where(place < R * hs, block * R + turn, -2).astype(f32)
    q_picker = jnp.where(
        (jnp.broadcast_to(wanted, (S * RQ, hs * GP)) == jnp.broadcast_to(own_slots(hs * GP), (S * RQ, hs * GP)))
        & (jnp.broadcast_to(place - turn * hs, (S * RQ, hs * GP)) == jnp.broadcast_to(stripe, (S * RQ, hs * GP))),
        1.0,
        0.0,
    ).astype(bf16)
    copies["query"].wait()
    tall = query[...].astype(f32)
    if GP > G:
        tall = jnp.concatenate([tall, jnp.zeros((GP - G, Dl), f32)], axis=0)
    stacked = jnp.concatenate([tall[:, j * HW : (j + 1) * HW] for j in range(hs)], axis=0).astype(bf16)
    picked_q = jnp.dot(q_picker, stacked, preferred_element_type=f32).astype(bf16)
    for c in range(S):
        a_q[c] = picked_q[c * RQ : (c + 1) * RQ]
    copies["new_kv"].wait()
    picked_kv = jnp.dot(picker, new_kv[...], preferred_element_type=f32)
    for c in range(S):
        a_kv[c] = picked_kv[c * 8 : c * 8 + 8].astype(bf16)
    pl.semaphore_wait(barrier, len(sec_peers) + 2 * len(tp_peers))

    started = []

    def push(dest, src, dst):
        copy = pltpu.make_async_remote_copy(
            src_ref=src,
            dst_ref=dst,
            send_sem=send_sem.at[len(started)],
            recv_sem=recv_sem.at[len(started)],
            device_id=dest,
            device_id_type=MESH,
        )
        copy.start()
        started.append(copy)
        return copy

    def arrived(pending):
        for copy in pending:
            copy.wait_recv()

    pend = []
    for c in sec_peers:
        pend.append(push({"sec": c}, a_q.at[c], a_q_in.at[s]))
    for c in sec_peers:
        pend.append(push({"sec": c}, a_kv.at[c], a_kv_in.at[s]))
    a_q_in[s] = a_q[s]
    a_kv_in[s] = a_kv[s]
    oheads[...] = jnp.zeros(oheads.shape, f32)
    for copy in pend:
        copy.wait_recv()

    fetch("wo", w_out, wo)
    for step in order:
        c = at_step(*step)
        cols = pl.ds(pl.multiple_of(c * Fs, Fs), Fs)
        fetch(("g", step), w_gate.at[:, cols], wg.at[c])
        fetch(("u", step), w_up.at[:, cols], wu.at[c])

    copies["lengths"].wait()
    for r in range(R):
        copies[("k", r)].wait()
        copies[("v", r)].wait()
    for c in range(S):
        blk = a_q_in[c].astype(f32)
        for r in range(R):
            qheads[r, c * hs : (c + 1) * hs, :] = blk[r * hs : (r + 1) * hs, :]
    pairs = jnp.concatenate([a_kv_in[c].astype(f32) for c in range(S)], axis=1)
    new_k = jnp.concatenate(
        [pairs[:, 2 * k * HW : (2 * k + 1) * HW] for k in range(KEY_VALUE_HEADS)], axis=1
    )
    new_v = jnp.concatenate(
        [pairs[:, (2 * k + 1) * HW : (2 * k + 2) * HW] for k in range(KEY_VALUE_HEADS)], axis=1
    )
    KW = KEY_VALUE_HEADS * HW
    hrow = lax.broadcasted_iota(jnp.int32, (QUERY_HEADS, KW), 0)
    hcol = lax.broadcasted_iota(jnp.int32, (QUERY_HEADS, KW), 1)
    low = jnp.zeros((QUERY_HEADS, KW), jnp.int32)
    for k in range(1, KEY_VALUE_HEADS):
        low = low + jnp.where(hcol >= k * HW, 1, 0)
    diag = (hrow >= low * GQ) & (hrow < low * GQ + GQ)
    scaling = 1.0 / math.sqrt(HW)
    slots = keys.shape[1]
    each = range(R)
    wide_q = [
        jnp.where(diag, jnp.concatenate([qheads[r]] * KEY_VALUE_HEADS, axis=1), 0.0) for r in each
    ]
    past = [
        lax.dot_general(
            wide_q[r].astype(bf16),
            kbuf[r],
            (((1,), (1,)), ((), ())),
            preferred_element_type=f32,
        )
        * scaling
        for r in each
    ]
    fresh = [
        jnp.sum(wide_q[r] * new_k[r : r + 1, :], axis=1, keepdims=True) * scaling for r in each
    ]
    position = lax.broadcasted_iota(jnp.int32, (QUERY_HEADS, slots), 1)
    past = [jnp.where(position < lengths[r], past[r], -1e30) for r in each]
    highest = [jnp.maximum(jnp.max(past[r], axis=1, keepdims=True), fresh[r]) for r in each]
    past_exp = [jnp.exp(past[r] - highest[r]) for r in each]
    fresh_exp = [jnp.exp(fresh[r] - highest[r]) for r in each]
    total = [jnp.sum(past_exp[r], axis=1, keepdims=True) + fresh_exp[r] for r in each]
    past_w = [(past_exp[r] / total[r]).astype(bf16) for r in each]
    fresh_w = [(fresh_exp[r] / total[r]).astype(bf16).astype(f32) for r in each]
    mixed = [jnp.dot(past_w[r], vbuf[r], preferred_element_type=f32) for r in each]
    for r in each:
        spread = jnp.where(diag, mixed[r] + fresh_w[r] * new_v[r : r + 1, :], 0.0)
        small = spread[:, 0:HW]
        for k in range(1, KEY_VALUE_HEADS):
            small = small + spread[:, k * HW : (k + 1) * HW]
        for c in range(T):
            oheads[c, r * ht : (r + 1) * ht, :] = small[c * ht : (c + 1) * ht, :]
    for c in range(T):
        b1[c] = oheads[c].astype(bf16)
    pend = [push({"sec": twin, "tp": c}, b1.at[c], b2_in.at[twin, t]) for c in tp_peers]
    pend.append(push({"sec": twin}, b1.at[t], b2_in.at[twin, t]))
    for step in reversed(order):
        c = at_step(*step)
        rows = pl.ds(pl.multiple_of(c * Fs, Fs), Fs)
        fetch(("d", step), w_down.at[rows, :], wd.at[c])

    tiles = Dl // 256
    cut = (tiles + 1) // 2
    spans = [(0, cut), (cut, tiles)]

    def fold(value):
        return jnp.concatenate(
            [
                jnp.concatenate([value[:, i : i + 128], value[:, i + 128 : i + 256]], axis=0)
                for i in range(0, value.shape[1], 256)
            ],
            axis=1,
        )

    def unfold(value):
        rows = value.shape[0] // 2
        return jnp.concatenate(
            [
                part
                for i in range(0, value.shape[1], 128)
                for part in (value[:rows, i : i + 128], value[rows:, i : i + 128])
            ],
            axis=1,
        )

    def lanes(span):
        return slice(span[0] * 128, span[1] * 128)

    copies["resid"].wait()
    copies["gain"].wait()
    stream_buf[...] = fold(resid[...].astype(f32))
    gain_rows = fold(jnp.broadcast_to(gain[...].astype(f32).reshape(1, Dl), (G, Dl)))

    pos = jnp.zeros((1, N), f32)
    for a in range(G):
        c, r = a // R, a % R
        held = c + 1 - 2 * (c % 2)
        pos = pos + jnp.where(row_a == float(a), float(held * T * RH + r * ht), 0.0)
    lane = lax.broadcasted_iota(jnp.int32, (1, N), 1)
    for g in range(1, T):
        pos = pos + jnp.where(lane >= g * G, float(RH), 0.0)
    pos_col = jnp.sum(jnp.where(ii == jj, pos, 0.0), axis=1, keepdims=True)
    spot = lax.broadcasted_iota(jnp.int32, (N, S * T * RH), 1).astype(f32)
    for j in range(ht):
        pick_buf[j * N : (j + 1) * N, :] = jnp.where(spot == pos_col + float(j), 1.0, 0.0).astype(bf16)
    arrived(pend)
    pend = [push({"sec": c}, b2_in.at[s], b2_in.at[s]) for c in sec_peers]
    copies["wo"].wait()
    arrived(pend)
    rows = jnp.concatenate([b2_in[c, g] for c in range(S) for g in range(T)], axis=0)
    placed = jnp.dot(pick_buf[...], rows, preferred_element_type=f32).astype(bf16)
    for j in range(ht):
        ord_buf[:, j * HW : (j + 1) * HW] = placed[j * N : (j + 1) * N]

    def tp_round(out_buf, in_buf, span):
        return [
            push({"tp": g}, out_buf.at[g, :, lanes(span)], in_buf.at[t, :, lanes(span)])
            for g in tp_peers
        ]

    def tp_sum(out_buf, in_buf, span):
        value = out_buf[t, :, lanes(span)].astype(f32)
        for g in tp_peers:
            value = value + in_buf[g, :, lanes(span)].astype(f32)
        return value

    def deal(out_buf, i, value):
        for g in range(T):
            out_buf[g, :, i * 128 : (i + 1) * 128] = fold(value[g * G : (g + 1) * G, :]).astype(bf16)

    pend = []
    for span in spans:
        for i in range(*span):
            deal(
                c_out,
                i,
                jnp.dot(ord_buf[...], wo[:, i * 256 : (i + 1) * 256], preferred_element_type=f32),
            )
        pend.append(tp_round(c_out, c_in, span))
    squares = jnp.zeros((G, 1), f32)
    pend_d = []
    for span, copies_in in zip(spans, pend):
        arrived(copies_in)
        stream = stream_buf[:, lanes(span)] + tp_sum(c_out, c_in, span)
        stream_buf[:, lanes(span)] = stream
        d_in[t, :, lanes(span)] = (stream * gain_rows[:, lanes(span)]).astype(bf16)
        piece = d_in.at[t, :, lanes(span)]
        pend_d.append([push({"tp": g}, piece, piece) for g in tp_peers])
        part = jnp.sum(stream * stream, axis=1, keepdims=True)
        squares = squares + part[:G] + part[G:]
    qi = lax.broadcasted_iota(jnp.int32, (G, 128), 0)
    qj = lax.broadcasted_iota(jnp.int32, (G, 128), 1)
    squares = jnp.where(qj == qi + t * G, squares, 0.0)
    q_in[t] = jnp.broadcast_to(jnp.sum(squares, axis=0, keepdims=True), (8, 128))
    pend_q = [push({"tp": g}, q_in.at[t], q_in.at[t]) for g in tp_peers]

    def take(span):
        for i in range(*span):
            blks = [d_in[g, :, i * 128 : (i + 1) * 128].astype(f32) for g in range(T)]
            for side in (0, 1):
                cols = slice(i * 256 + side * 128, i * 256 + side * 128 + 128)
                x_buf[:, cols] = jnp.concatenate(
                    [blk[side * G : side * G + G] for blk in blks], axis=0
                ).astype(bf16)

    mate = {"sec": at_step(0, 1)}
    Fh = Fs // NH
    parts = range(NH)
    ready = set()

    def need(step):
        for part in "gu":
            if (part, step) not in ready:
                copies[(part, step)].wait()
                ready.add((part, step))

    def widen(step, h, depth, base=None):
        need(step)
        c = at_step(*step)
        value = [
            jnp.dot(
                x_buf[:, depth],
                weight[c, depth, h * Fh : (h + 1) * Fh],
                preferred_element_type=f32,
            )
            for weight in (wg, wu)
        ]
        value = jnp.concatenate(value, axis=1)
        return value if base is None else base + value

    def unit_cols(h):
        return slice(h * 2 * Fh, (h + 1) * 2 * Fh)

    first, second = [slice(lo * 256, hi * 256) for lo, hi in spans]
    whole = slice(0, Dl)
    far = list(range(1, half))
    arrived(pend_d[0])
    take(spans[0])
    for n, dx in enumerate(far):
        for dc in (0, 1):
            for h in parts:
                far_acc[2 * n + dc, :, unit_cols(h)] = widen((dx, dc), h, first)
    arrived(pend_d[1])
    take(spans[1])
    arrived(pend_q)
    squares = q_in[0]
    for g in range(1, T):
        squares = squares + q_in[g]
    s_in[s] = squares
    pend_s = [push({"sec": c}, s_in.at[s], s_in.at[s]) for c in sec_peers]
    pair, far_sums = {}, {}
    for n, dx in enumerate(far):
        fx = (sx + dx) % half
        c = at_step(dx, 0)
        for h in parts:
            e_out[c, :, unit_cols(h)] = widen(
                (dx, 0), h, second, far_acc[2 * n, :, unit_cols(h)]
            ).astype(bf16)
            pair[(dx, h)] = push(
                mate, e_out.at[c, :, unit_cols(h)], pair_in.at[fx, :, unit_cols(h)]
            )
        for h in parts:
            far_acc[2 * n + 1, :, unit_cols(h)] = widen(
                (dx, 1), h, second, far_acc[2 * n + 1, :, unit_cols(h)]
            )

    def near_mate(h):
        c = at_step(0, 1)
        e_out[c, :, unit_cols(h)] = widen((0, 1), h, whole).astype(bf16)
        pair[(0, h)] = push(mate, e_out.at[c, :, unit_cols(h)], pair_in.at[sx, :, unit_cols(h)])

    near_mate(0)
    for h in parts:
        for n, dx in enumerate(far):
            fx = (sx + dx) % half
            c = at_step(dx, 1)
            pair[(dx, h)].wait_recv()
            e_out[c, :, unit_cols(h)] = (
                far_acc[2 * n + 1, :, unit_cols(h)] + pair_in[fx, :, unit_cols(h)].astype(f32)
            ).astype(bf16)
            far_sums[(dx, h)] = push(
                {"sec": c}, e_out.at[c, :, unit_cols(h)], e_in.at[sx, :, unit_cols(h)]
            )
    for h in parts[1:]:
        near_mate(h)
    for h in parts:
        near_acc[:, unit_cols(h)] = widen((0, 0), h, whole)
    arrived(pend_s)
    squares = s_in[0]
    for c in range(1, S):
        squares = squares + s_in[c]
    inverse = lax.rsqrt(squares[0:1, :] / D + 1e-06)
    ni = lax.broadcasted_iota(jnp.int32, (N, 128), 0)
    nj = lax.broadcasted_iota(jnp.int32, (N, 128), 1)
    inverse = jnp.sum(jnp.where(ni == nj, inverse, 0.0), axis=1, keepdims=True)
    to_mate, from_far = [], {}
    for h in parts:
        pair[(0, h)].wait_recv()
        for dx in far:
            far_sums[(dx, h)].wait_recv()
        for j in range(0, Fh, 128):
            both = []
            for lo in (h * 2 * Fh + j, h * 2 * Fh + Fh + j):
                value = near_acc[:, lo : lo + 128] + pair_in[sx, :, lo : lo + 128].astype(f32)
                for dx in far:
                    value = value + e_in[(sx + dx) % half, :, lo : lo + 128].astype(f32)
                both.append(value * inverse)
            gate, upper = both
            f_in[s, :, h * Fh + j : h * Fh + j + 128] = (
                gate / (1.0 + jnp.exp(-gate)) * upper
            ).astype(bf16)
        piece = f_in.at[s, :, h * Fh : (h + 1) * Fh]
        for dx in far:
            from_far[(half - dx, h)] = push({"sec": at_step(dx, 1)}, piece, piece)
        to_mate.append(push(mate, piece, piece))

    def lower(step, units, first=False):
        c = at_step(*step)
        for i in range(tiles):
            cols = slice(i * 256, (i + 1) * 256)
            value = jnp.dot(f_in[c, :, units], wd[c, units, cols], preferred_element_type=f32)
            acc[:, cols] = value if first else acc[:, cols] + value

    for step in order:
        copies[("d", step)].wait()
    all_units = slice(0, Fs)
    lower((0, 0), all_units, True)
    arrived(to_mate)
    lower((0, 1), all_units)
    relayed = {}
    for h in parts:
        for dx in far:
            from_far[(dx, h)].wait_recv()
            piece = f_in.at[at_step(dx, 1), :, h * Fh : (h + 1) * Fh]
            relayed[(dx, h)] = push(mate, piece, piece)
    for dx in far:
        lower((dx, 1), all_units)
    early = slice(0, (NH - 1) * Fh)
    late = slice((NH - 1) * Fh, Fs)
    for dx in far:
        for h in parts[:-1]:
            relayed[(dx, h)].wait_recv()
        lower((dx, 0), early)
    for dx in far[:-1]:
        relayed[(dx, NH - 1)].wait_recv()
        lower((dx, 0), late)
    relayed[(far[-1], NH - 1)].wait_recv()
    c = at_step(far[-1], 0)
    pend = []
    for span in spans:
        for i in range(*span):
            cols = slice(i * 256, (i + 1) * 256)
            value = jnp.dot(f_in[c, :, late], wd[c, late, cols], preferred_element_type=f32)
            deal(g_out, i, acc[:, cols] + value)
        pend.append(tp_round(g_out, g_in, span))
    for span, copies_in in zip(spans, pend):
        arrived(copies_in)
        total = stream_buf[:, lanes(span)] + tp_sum(g_out, g_in, span)
        out[:, span[0] * 256 : span[1] * 256] = unfold(total).astype(bf16)
    for copy in started:
        copy.wait_send()


def local(
    resid,
    query,
    new_kv,
    key_cache,
    cached_value_rows,
    cache_len,
    assign,
    out_weight,
    norm_gain,
    gate_weight,
    up_weight,
    down_weight,
):
    group = query.shape[0]
    per_device = key_cache.shape[0]
    tp_index = lax.axis_index("tp")
    sec_index = lax.axis_index("sec")
    tp_count = lax.axis_size("tp")
    local_slots = lax.dynamic_slice_in_dim(assign, tp_index * group, group)
    full_query, full_pairs = (
        lax.all_gather(query, "sec", axis=1, tiled=True),
        lax.all_gather(new_kv, "sec", axis=1, tiled=True),
    )
    wanted = sec_index * per_device + lax.iota(jnp.int32, per_device)
    picker = (local_slots[None, :] == wanted[:, None]).astype(jnp.bfloat16)
    my_query = jnp.dot(picker, full_query, preferred_element_type=jnp.float32).astype(jnp.bfloat16)
    my_pairs = jnp.dot(picker, full_pairs, preferred_element_type=jnp.float32).astype(jnp.bfloat16)
    attended = attend_slots(my_query, my_pairs, key_cache, cached_value_rows, cache_len)
    request_ids = lax.iota(jnp.int32, group * tp_count)
    slot_block = lax.all_gather(attended, "sec", axis=0, tiled=True)
    received = lax.all_to_all(slot_block, "tp", split_axis=1, concat_axis=0, tiled=True)
    position = request_ids // group * group + assign
    ordered = jnp.take(received, position, axis=0)
    block = ordered
    attn_out = lax.psum_scatter(
        jnp.dot(block, out_weight, preferred_element_type=jnp.float32).astype(jnp.bfloat16),
        "tp",
        scatter_dimension=0,
        tiled=True,
    ).astype(jnp.float32)
    stream = resid.astype(jnp.float32) + attn_out
    squares = lax.psum(jnp.sum(stream * stream, axis=1), "sec")
    inverse = lax.rsqrt(squares / D + 1e-06)
    normed = (stream * inverse[:, None] * norm_gain.astype(jnp.float32)[None, :]).astype(
        jnp.bfloat16
    )
    piece = lax.all_gather(normed, "tp", axis=0, tiled=True)
    gate_part = jnp.dot(piece, gate_weight, preferred_element_type=jnp.float32)
    up_part = jnp.dot(piece, up_weight, preferred_element_type=jnp.float32)
    projected = jnp.concatenate([gate_part, up_part], axis=1)
    width = gate_weight.shape[1]
    share = lax.psum_scatter(
        projected.astype(jnp.bfloat16), "sec", scatter_dimension=0, tiled=True
    ).astype(jnp.float32)
    hidden = lax.all_gather(gated_units(share, width), "sec", axis=0, tiled=True)
    block = hidden
    ff_out = lax.psum_scatter(
        jnp.dot(block, down_weight, preferred_element_type=jnp.float32).astype(jnp.bfloat16),
        "tp",
        scatter_dimension=0,
        tiled=True,
    ).astype(jnp.float32)
    return (stream + ff_out).astype(jnp.bfloat16)


def fused(
    resid,
    query,
    new_kv,
    key_cache,
    cached_value_rows,
    cache_len,
    assign,
    out_weight,
    norm_gain,
    gate_weight,
    up_weight,
    down_weight,
):
    S, T = lax.axis_size("sec"), lax.axis_size("tp")
    G, R = query.shape[0], key_cache.shape[0]
    N = G * T
    RH = up_to(R * (QUERY_HEADS // T), ROWS16)
    RQ = up_to(R * (QUERY_HEADS // S), ROWS16)
    Dl, Hl, F, kvl = resid.shape[1], out_weight.shape[0], gate_weight.shape[1], new_kv.shape[1]
    Fs = F // S
    NH = HIDDEN_PARTS
    remote = 4 * (S - 1) + 10 * (T - 1) + (3 * S // 2 + 2) * NH
    bf16, f32 = jnp.bfloat16, jnp.float32
    V = pltpu.VMEM
    vm = pl.BlockSpec(memory_space=pltpu.VMEM)
    hbm = pl.BlockSpec(memory_space=pl.ANY)
    scratch = [
        V(resid.shape, bf16),
        V(query.shape, bf16),
        V(new_kv.shape, bf16),
        V((1, N), jnp.int32),
        V(norm_gain.shape, bf16),
        pltpu.SMEM(cache_len.shape, jnp.int32),
        V(key_cache.shape, bf16),
        V(cached_value_rows.shape, bf16),
        V((Hl, Dl), bf16),
        V((S, Dl, Fs), bf16),
        V((S, Dl, Fs), bf16),
        V((S, Fs, Dl), bf16),
        V((S, RQ, HEAD_WIDTH), bf16),
        V((S, 8, kvl), bf16),
        V((S, RQ, HEAD_WIDTH), bf16),
        V((S, 8, kvl), bf16),
        V((R, QUERY_HEADS, HEAD_WIDTH), f32),
        V((T, RH, HEAD_WIDTH), f32),
        V((T, RH, HEAD_WIDTH), bf16),
        V((S, T, RH, HEAD_WIDTH), bf16),
        V((QUERY_HEADS // T * N, S * T * RH), bf16),
        V((N, Hl), bf16),
        V((T, 2 * G, Dl // 2), bf16),
        V((T, 2 * G, Dl // 2), bf16),
        V((T, 2 * G, Dl // 2), bf16),
        V((T, 8, 128), f32),
        V((N, Dl), bf16),
        V((S, 8, 128), f32),
        V((S, N, 2 * Fs), bf16),
        V((S // 2, N, 2 * Fs), bf16),
        V((S // 2, N, 2 * Fs), bf16),
        V((S, N, Fs), bf16),
        V((N, Dl), f32),
        V((2 * (S // 2 - 1), N, 2 * Fs), f32),
        V((N, 2 * Fs), f32),
        V((T, 2 * G, Dl // 2), bf16),
        V((T, 2 * G, Dl // 2), bf16),
        V((2 * G, Dl // 2), f32),
        pltpu.SemaphoreType.DMA((2 * R + 7 + 3 * S,)),
        pltpu.SemaphoreType.DMA((remote,)),
        pltpu.SemaphoreType.DMA((remote,)),
    ]
    return pl.pallas_call(
        functools.partial(fused_kernel, (S, T, G, R, NH)),
        out_shape=pltpu.VMEM(resid.shape, bf16),
        in_specs=[hbm] * 12,
        out_specs=vm,
        scratch_shapes=scratch,
        compiler_params=pltpu.CompilerParams(
            collective_id=0, has_side_effects=True, vmem_limit_bytes=54 * 2**20
        ),
    )(
        resid,
        query,
        new_kv,
        assign.reshape(1, N),
        norm_gain,
        cache_len,
        key_cache,
        cached_value_rows,
        out_weight,
        gate_weight,
        up_weight,
        down_weight,
    )


def layer(*args):
    query, key_cache, out_weight, gate_weight = args[1], args[3], args[7], args[9]
    shapes = (
        query.shape[0],
        key_cache.shape[0],
        out_weight.shape[0],
        gate_weight.shape[1],
        lax.axis_size("sec"),
        lax.axis_size("tp"),
    )
    return fused(*args) if fits_kernel(shapes) else local(*args)


def solution(mesh):
    return jax.shard_map(
        layer,
        mesh=mesh,
        in_specs=(
            P(("rep", "tp"), "sec"),
            P(("rep", "tp"), "sec"),
            P(("rep", "tp"), "sec"),
            P(("rep", "sec", "tp"), None, None),
            P(("rep", "sec", "tp"), None, None),
            P(("rep", "sec", "tp")),
            P("rep"),
            P("tp", "sec"),
            P("sec"),
            P("sec", "tp"),
            P("sec", "tp"),
            P("tp", "sec"),
        ),
        out_specs=P(("rep", "tp"), "sec"),
        check_vma=False,
    )
```

```python
import functools
import math

import jax
import jax.numpy as jnp
from jax import lax
from jax.experimental import pallas as pl
from jax.experimental.pallas import tpu as pltpu
from jax.sharding import PartitionSpec as P

D = 5120
QUERY_HEADS = 40
KEY_VALUE_HEADS = 8
HEAD_WIDTH = 128
CACHE_SLOTS = 224


def attend_slots(query_rows, key_value_pairs, stored_keys, stored_values, lengths):
    cache_slots = query_rows.shape[0]
    group_query = QUERY_HEADS // KEY_VALUE_HEADS
    query_head_rows = query_rows.reshape(cache_slots, KEY_VALUE_HEADS, group_query, HEAD_WIDTH)
    paired_heads = key_value_pairs.reshape(cache_slots, KEY_VALUE_HEADS, 2, HEAD_WIDTH)
    fresh_keys = paired_heads[:, :, 0]
    fresh_values = paired_heads[:, :, 1]
    earlier_keys = stored_keys.reshape(cache_slots, CACHE_SLOTS, KEY_VALUE_HEADS, HEAD_WIDTH)
    earlier_values = stored_values.reshape(cache_slots, CACHE_SLOTS, KEY_VALUE_HEADS, HEAD_WIDTH)
    scaling = 1.0 / math.sqrt(HEAD_WIDTH)
    past_scores = (
        jnp.einsum(
            "rkgd,rlkd->rkgl", query_head_rows, earlier_keys, preferred_element_type=jnp.float32
        )
        * scaling
    )
    fresh_scores = (
        jnp.einsum("rkgd,rkd->rkg", query_head_rows, fresh_keys, preferred_element_type=jnp.float32)
        * scaling
    )
    valid = lax.broadcasted_iota(jnp.int32, (cache_slots, CACHE_SLOTS), 1) < lengths[:, None]
    past_scores = jnp.where(valid[:, None, None, :], past_scores, -1e30)
    highest = jnp.maximum(jnp.max(past_scores, axis=-1), fresh_scores)
    past_exp = jnp.exp(past_scores - highest[..., None])
    fresh_exp = jnp.exp(fresh_scores - highest)
    denominator = jnp.sum(past_exp, axis=-1) + fresh_exp
    past_weights = (past_exp / denominator[..., None]).astype(jnp.bfloat16)
    fresh_weights = (fresh_exp / denominator).astype(jnp.bfloat16)
    mixed = jnp.einsum(
        "rkgl,rlkd->rkgd", past_weights, earlier_values, preferred_element_type=jnp.float32
    )
    mixed = (
        mixed
        + fresh_weights.astype(jnp.float32)[..., None]
        * fresh_values.astype(jnp.float32)[:, :, None, :]
    )
    return mixed.reshape(cache_slots, QUERY_HEADS * HEAD_WIDTH).astype(jnp.bfloat16)


def gated_units(values, width):
    return (jax.nn.silu(values[:, :width]) * values[:, width:]).astype(jnp.bfloat16)


MESH = pl.DeviceIdType.MESH
ROWS16 = 16
HIDDEN_PARTS = 2


def up_to(count, multiple):
    return -(-count // multiple) * multiple


def fits_kernel(shapes):
    group, per_device, head_cols, width, sec, tp = shapes
    return (
        sec % 2 == 0
        and sec >= 4
        and width % (sec * 256 * HIDDEN_PARTS) == 0
        and width % (sec * 256) == 0
        and head_cols % (256) == 0
        and (D // sec) % 256 == 0
        and D // sec >= 512
        and QUERY_HEADS % tp == 0
        and QUERY_HEADS % sec == 0
        and per_device <= 8
        and tp >= 2
        and per_device * sec == group
        and (group * tp) % 16 == 0
        and group * tp <= 128
    )


def fused_kernel(
    dims,
    resid_hbm,
    query_hbm,
    new_kv_hbm,
    assign_hbm,
    gain_hbm,
    lengths_hbm,
    keys,
    values,
    w_out,
    w_gate,
    w_up,
    w_down,
    out,
    resid,
    query,
    new_kv,
    assign,
    gain,
    lengths,
    kbuf,
    vbuf,
    wo,
    wg,
    wu,
    wd,
    a_q,
    a_kv,
    a_q_in,
    a_kv_in,
    qheads,
    oheads,
    b1,
    b2_in,
    pick_buf,
    ord_buf,
    c_out,
    c_in,
    d_in,
    q_in,
    x_buf,
    s_in,
    e_out,
    pair_in,
    e_in,
    f_in,
    acc,
    far_acc,
    near_acc,
    g_out,
    g_in,
    stream_buf,
    local_sem,
    send_sem,
    recv_sem,
):
    S, T, G, R, NH = dims
    N = G * T
    RH = b1.shape[1]
    Dl = resid.shape[1]
    F = w_gate.shape[1]
    Fs = F // S
    f32, bf16 = jnp.float32, jnp.bfloat16
    s = lax.axis_index("sec")
    t = lax.axis_index("tp")
    sx, sc = s // 2, s % 2
    half = S // 2
    steps = [(dx, dc) for dx in list(range(1, half)) + [0] for dc in (0, 1) if dx or dc]
    sec_peers = [((sx + dx) % half) * 2 + (sc + dc) % 2 for dx, dc in steps]
    tp_peers = [(t + k) % T for k in sorted(range(1, T), key=lambda k: -min(k, T - k))]
    if T == 4:
        tp_peers = [T - 1 - t, (t + 2) % T, t + 1 - 2 * (t % 2)]

    twin = sx * 2 + (1 - sc)
    barrier = pltpu.get_barrier_semaphore()
    for c in sec_peers:
        pl.semaphore_signal(barrier, inc=1, device_id={"sec": c}, device_id_type=MESH)
    for c in tp_peers:
        pl.semaphore_signal(barrier, inc=1, device_id={"tp": c}, device_id_type=MESH)
        pl.semaphore_signal(
            barrier, inc=1, device_id={"sec": twin, "tp": c}, device_id_type=MESH
        )

    copies = {}
    count = [0]

    def fetch(name, src, dst):
        copy = pltpu.make_async_copy(src, dst, local_sem.at[count[0]])
        count[0] += 1
        copy.start()
        copies[name] = copy

    fetch("assign", assign_hbm, assign)
    fetch("query", query_hbm, query)
    fetch("new_kv", new_kv_hbm, new_kv)
    fetch("lengths", lengths_hbm, lengths)
    fetch("resid", resid_hbm, resid)
    fetch("gain", gain_hbm, gain)
    for r in range(R):
        fetch(("k", r), keys.at[r], kbuf.at[r])
        fetch(("v", r), values.at[r], vbuf.at[r])
    def at_step(dx, dc):
        return ((sx + dx) % half) * 2 + (sc + dc) % 2

    order = [(dx, dc) for dx in list(range(1, half)) + [0] for dc in (1, 0)]

    hs = QUERY_HEADS // S
    ht = QUERY_HEADS // T
    HW = HEAD_WIDTH
    GQ = QUERY_HEADS // KEY_VALUE_HEADS
    GP = up_to(G, ROWS16)
    RQ = a_q.shape[1]
    copies["assign"].wait()
    row_a = assign[...].astype(f32)
    ii = lax.broadcasted_iota(jnp.int32, (N, N), 0)
    jj = lax.broadcasted_iota(jnp.int32, (N, N), 1)
    col_a = jnp.sum(jnp.where(ii == jj, jnp.broadcast_to(row_a, (N, N)), 0.0), axis=1, keepdims=True)

    def own_slots(width):
        pi = lax.broadcasted_iota(jnp.int32, (N, width), 0)
        pj = lax.broadcasted_iota(jnp.int32, (N, width), 1)
        hit = pi == pj + t * G
        if width > G:
            stripe = jnp.zeros((N, width), jnp.int32)
            for j in range(1, width // GP):
                stripe = stripe + jnp.where(pj >= j * GP, GP, 0)
            hit = pi == pj - stripe + t * G
            hit = hit & (pj - stripe < G)
        return jnp.sum(
            jnp.where(hit, jnp.broadcast_to(col_a, (N, width)), 0.0)
            + jnp.where(hit, 1.0, 0.0),
            axis=0,
            keepdims=True,
        ) - 1.0

    pr = lax.broadcasted_iota(jnp.int32, (S * 8, 1), 0)
    slot = jnp.full((S * 8, 1), -2.0, f32)
    for c in range(S):
        for r in range(R):
            slot = jnp.where(pr == c * 8 + r, float(c * R + r), slot)
    picker = jnp.where(
        jnp.broadcast_to(slot, (S * 8, G)) == jnp.broadcast_to(own_slots(G), (S * 8, G)), 1.0, 0.0
    ).astype(bf16)
    qr = lax.broadcasted_iota(jnp.int32, (S * RQ, 1), 0)
    block = jnp.zeros((S * RQ, 1), jnp.int32)
    for c in range(1, S):
        block = block + jnp.where(qr >= c * RQ, 1, 0)
    place = qr - block * RQ
    turn = jnp.zeros((S * RQ, 1), jnp.int32)
    for r in range(1, R):
        turn = turn + jnp.where(place >= r * hs, 1, 0)
    qc = lax.broadcasted_iota(jnp.int32, (1, hs * GP), 1)
    stripe = jnp.zeros((1, hs * GP), jnp.int32)
    for j in range(1, hs):
        stripe = stripe + jnp.where(qc >= j * GP, 1, 0)
    wanted = jnp.where(place < R * hs, block * R + turn, -2).astype(f32)
    q_picker = jnp.where(
        (jnp.broadcast_to(wanted, (S * RQ, hs * GP)) == jnp.broadcast_to(own_slots(hs * GP), (S * RQ, hs * GP)))
        & (jnp.broadcast_to(place - turn * hs, (S * RQ, hs * GP)) == jnp.broadcast_to(stripe, (S * RQ, hs * GP))),
        1.0,
        0.0,
    ).astype(bf16)
    copies["query"].wait()
    tall = query[...].astype(f32)
    if GP > G:
        tall = jnp.concatenate([tall, jnp.zeros((GP - G, Dl), f32)], axis=0)
    stacked = jnp.concatenate([tall[:, j * HW : (j + 1) * HW] for j in range(hs)], axis=0).astype(bf16)
    picked_q = jnp.dot(q_picker, stacked, preferred_element_type=f32).astype(bf16)
    for c in range(S):
        a_q[c] = picked_q[c * RQ : (c + 1) * RQ]
    copies["new_kv"].wait()
    picked_kv = jnp.dot(picker, new_kv[...], preferred_element_type=f32)
    for c in range(S):
        a_kv[c] = picked_kv[c * 8 : c * 8 + 8].astype(bf16)
    pl.semaphore_wait(barrier, len(sec_peers) + 2 * len(tp_peers))

    started = []

    def push(dest, src, dst):
        copy = pltpu.make_async_remote_copy(
            src_ref=src,
            dst_ref=dst,
            send_sem=send_sem.at[len(started)],
            recv_sem=recv_sem.at[len(started)],
            device_id=dest,
            device_id_type=MESH,
        )
        copy.start()
        started.append(copy)
        return copy

    def arrived(pending):
        for copy in pending:
            copy.wait_recv()

    pend = []
    for c in sec_peers:
        pend.append(push({"sec": c}, a_q.at[c], a_q_in.at[s]))
    for c in sec_peers:
        pend.append(push({"sec": c}, a_kv.at[c], a_kv_in.at[s]))
    a_q_in[s] = a_q[s]
    a_kv_in[s] = a_kv[s]
    oheads[...] = jnp.zeros(oheads.shape, f32)
    for copy in pend:
        copy.wait_recv()

    fetch("wo", w_out, wo)
    for step in order:
        c = at_step(*step)
        cols = pl.ds(pl.multiple_of(c * Fs, Fs), Fs)
        fetch(("g", step), w_gate.at[:, cols], wg.at[c])
        fetch(("u", step), w_up.at[:, cols], wu.at[c])

    copies["lengths"].wait()
    for r in range(R):
        copies[("k", r)].wait()
        copies[("v", r)].wait()
    for c in range(S):
        blk = a_q_in[c].astype(f32)
        for r in range(R):
            qheads[r, c * hs : (c + 1) * hs, :] = blk[r * hs : (r + 1) * hs, :]
    pairs = jnp.concatenate([a_kv_in[c].astype(f32) for c in range(S)], axis=1)
    new_k = jnp.concatenate(
        [pairs[:, 2 * k * HW : (2 * k + 1) * HW] for k in range(KEY_VALUE_HEADS)], axis=1
    )
    new_v = jnp.concatenate(
        [pairs[:, (2 * k + 1) * HW : (2 * k + 2) * HW] for k in range(KEY_VALUE_HEADS)], axis=1
    )
    KW = KEY_VALUE_HEADS * HW
    hrow = lax.broadcasted_iota(jnp.int32, (QUERY_HEADS, KW), 0)
    hcol = lax.broadcasted_iota(jnp.int32, (QUERY_HEADS, KW), 1)
    low = jnp.zeros((QUERY_HEADS, KW), jnp.int32)
    for k in range(1, KEY_VALUE_HEADS):
        low = low + jnp.where(hcol >= k * HW, 1, 0)
    diag = (hrow >= low * GQ) & (hrow < low * GQ + GQ)
    scaling = 1.0 / math.sqrt(HW)
    slots = keys.shape[1]
    each = range(R)
    wide_q = [
        jnp.where(diag, jnp.concatenate([qheads[r]] * KEY_VALUE_HEADS, axis=1), 0.0) for r in each
    ]
    past = [
        lax.dot_general(
            wide_q[r].astype(bf16),
            kbuf[r],
            (((1,), (1,)), ((), ())),
            preferred_element_type=f32,
        )
        * scaling
        for r in each
    ]
    fresh = [
        jnp.sum(wide_q[r] * new_k[r : r + 1, :], axis=1, keepdims=True) * scaling for r in each
    ]
    position = lax.broadcasted_iota(jnp.int32, (QUERY_HEADS, slots), 1)
    past = [jnp.where(position < lengths[r], past[r], -1e30) for r in each]
    highest = [jnp.maximum(jnp.max(past[r], axis=1, keepdims=True), fresh[r]) for r in each]
    past_exp = [jnp.exp(past[r] - highest[r]) for r in each]
    fresh_exp = [jnp.exp(fresh[r] - highest[r]) for r in each]
    total = [jnp.sum(past_exp[r], axis=1, keepdims=True) + fresh_exp[r] for r in each]
    past_w = [(past_exp[r] / total[r]).astype(bf16) for r in each]
    fresh_w = [(fresh_exp[r] / total[r]).astype(bf16).astype(f32) for r in each]
    mixed = [jnp.dot(past_w[r], vbuf[r], preferred_element_type=f32) for r in each]
    for r in each:
        spread = jnp.where(diag, mixed[r] + fresh_w[r] * new_v[r : r + 1, :], 0.0)
        small = spread[:, 0:HW]
        for k in range(1, KEY_VALUE_HEADS):
            small = small + spread[:, k * HW : (k + 1) * HW]
        for c in range(T):
            oheads[c, r * ht : (r + 1) * ht, :] = small[c * ht : (c + 1) * ht, :]
    for c in range(T):
        b1[c] = oheads[c].astype(bf16)
    pend = [push({"sec": twin, "tp": c}, b1.at[c], b2_in.at[twin, t]) for c in tp_peers]
    pend.append(push({"sec": twin}, b1.at[t], b2_in.at[twin, t]))
    for step in reversed(order):
        c = at_step(*step)
        rows = pl.ds(pl.multiple_of(c * Fs, Fs), Fs)
        fetch(("d", step), w_down.at[rows, :], wd.at[c])

    tiles = Dl // 256
    cut = (tiles + 1) // 2
    spans = [(0, cut), (cut, tiles)]

    def fold(value):
        return jnp.concatenate(
            [
                jnp.concatenate([value[:, i : i + 128], value[:, i + 128 : i + 256]], axis=0)
                for i in range(0, value.shape[1], 256)
            ],
            axis=1,
        )

    def unfold(value):
        rows = value.shape[0] // 2
        return jnp.concatenate(
            [
                part
                for i in range(0, value.shape[1], 128)
                for part in (value[:rows, i : i + 128], value[rows:, i : i + 128])
            ],
            axis=1,
        )

    def lanes(span):
        return slice(span[0] * 128, span[1] * 128)

    copies["resid"].wait()
    copies["gain"].wait()
    stream_buf[...] = fold(resid[...].astype(f32))
    gain_rows = fold(jnp.broadcast_to(gain[...].astype(f32).reshape(1, Dl), (G, Dl)))

    pos = jnp.zeros((1, N), f32)
    for a in range(G):
        c, r = a // R, a % R
        held = c + 1 - 2 * (c % 2)
        pos = pos + jnp.where(row_a == float(a), float(held * T * RH + r * ht), 0.0)
    lane = lax.broadcasted_iota(jnp.int32, (1, N), 1)
    for g in range(1, T):
        pos = pos + jnp.where(lane >= g * G, float(RH), 0.0)
    pos_col = jnp.sum(jnp.where(ii == jj, pos, 0.0), axis=1, keepdims=True)
    spot = lax.broadcasted_iota(jnp.int32, (N, S * T * RH), 1).astype(f32)
    for j in range(ht):
        pick_buf[j * N : (j + 1) * N, :] = jnp.where(spot == pos_col + float(j), 1.0, 0.0).astype(bf16)
    arrived(pend)
    pend = [push({"sec": c}, b2_in.at[s], b2_in.at[s]) for c in sec_peers]
    copies["wo"].wait()
    arrived(pend)
    rows = jnp.concatenate([b2_in[c, g] for c in range(S) for g in range(T)], axis=0)
    placed = jnp.dot(pick_buf[...], rows, preferred_element_type=f32).astype(bf16)
    for j in range(ht):
        ord_buf[:, j * HW : (j + 1) * HW] = placed[j * N : (j + 1) * N]

    def tp_round(out_buf, in_buf, span):
        return [
            push({"tp": g}, out_buf.at[g, :, lanes(span)], in_buf.at[t, :, lanes(span)])
            for g in tp_peers
        ]

    def tp_sum(out_buf, in_buf, span):
        value = out_buf[t, :, lanes(span)].astype(f32)
        for g in tp_peers:
            value = value + in_buf[g, :, lanes(span)].astype(f32)
        return value

    def deal(out_buf, i, value):
        for g in range(T):
            out_buf[g, :, i * 128 : (i + 1) * 128] = fold(value[g * G : (g + 1) * G, :]).astype(bf16)

    pend = []
    for span in spans:
        for i in range(*span):
            deal(
                c_out,
                i,
                jnp.dot(ord_buf[...], wo[:, i * 256 : (i + 1) * 256], preferred_element_type=f32),
            )
        pend.append(tp_round(c_out, c_in, span))
    squares = jnp.zeros((G, 1), f32)
    pend_d = []
    for span, copies_in in zip(spans, pend):
        arrived(copies_in)
        stream = stream_buf[:, lanes(span)] + tp_sum(c_out, c_in, span)
        stream_buf[:, lanes(span)] = stream
        d_in[t, :, lanes(span)] = (stream * gain_rows[:, lanes(span)]).astype(bf16)
        piece = d_in.at[t, :, lanes(span)]
        pend_d.append([push({"tp": g}, piece, piece) for g in tp_peers])
        part = jnp.sum(stream * stream, axis=1, keepdims=True)
        squares = squares + part[:G] + part[G:]
    qi = lax.broadcasted_iota(jnp.int32, (G, 128), 0)
    qj = lax.broadcasted_iota(jnp.int32, (G, 128), 1)
    squares = jnp.where(qj == qi + t * G, squares, 0.0)
    q_in[t] = jnp.broadcast_to(jnp.sum(squares, axis=0, keepdims=True), (8, 128))
    pend_q = [push({"tp": g}, q_in.at[t], q_in.at[t]) for g in tp_peers]

    def take(span):
        for i in range(*span):
            blks = [d_in[g, :, i * 128 : (i + 1) * 128].astype(f32) for g in range(T)]
            for side in (0, 1):
                cols = slice(i * 256 + side * 128, i * 256 + side * 128 + 128)
                x_buf[:, cols] = jnp.concatenate(
                    [blk[side * G : side * G + G] for blk in blks], axis=0
                ).astype(bf16)

    mate = {"sec": at_step(0, 1)}
    Fh = Fs // NH
    parts = range(NH)
    ready = set()

    def need(step):
        for part in "gu":
            if (part, step) not in ready:
                copies[(part, step)].wait()
                ready.add((part, step))

    def widen(step, h, depth, base=None):
        need(step)
        c = at_step(*step)
        value = [
            jnp.dot(
                x_buf[:, depth],
                weight[c, depth, h * Fh : (h + 1) * Fh],
                preferred_element_type=f32,
            )
            for weight in (wg, wu)
        ]
        value = jnp.concatenate(value, axis=1)
        return value if base is None else base + value

    def unit_cols(h):
        return slice(h * 2 * Fh, (h + 1) * 2 * Fh)

    first, second = [slice(lo * 256, hi * 256) for lo, hi in spans]
    whole = slice(0, Dl)
    far = list(range(1, half))
    arrived(pend_d[0])
    take(spans[0])
    for n, dx in enumerate(far):
        for dc in (0, 1):
            for h in parts:
                far_acc[2 * n + dc, :, unit_cols(h)] = widen((dx, dc), h, first)
    arrived(pend_d[1])
    take(spans[1])
    arrived(pend_q)
    squares = q_in[0]
    for g in range(1, T):
        squares = squares + q_in[g]
    s_in[s] = squares
    pend_s = [push({"sec": c}, s_in.at[s], s_in.at[s]) for c in sec_peers]
    pair, far_sums = {}, {}
    for n, dx in enumerate(far):
        fx = (sx + dx) % half
        c = at_step(dx, 0)
        for h in parts:
            e_out[c, :, unit_cols(h)] = widen(
                (dx, 0), h, second, far_acc[2 * n, :, unit_cols(h)]
            ).astype(bf16)
            pair[(dx, h)] = push(
                mate, e_out.at[c, :, unit_cols(h)], pair_in.at[fx, :, unit_cols(h)]
            )
        for h in parts:
            far_acc[2 * n + 1, :, unit_cols(h)] = widen(
                (dx, 1), h, second, far_acc[2 * n + 1, :, unit_cols(h)]
            )

    def near_mate(h):
        c = at_step(0, 1)
        e_out[c, :, unit_cols(h)] = widen((0, 1), h, whole).astype(bf16)
        pair[(0, h)] = push(mate, e_out.at[c, :, unit_cols(h)], pair_in.at[sx, :, unit_cols(h)])

    near_mate(0)
    for h in parts:
        for n, dx in enumerate(far):
            fx = (sx + dx) % half
            c = at_step(dx, 1)
            pair[(dx, h)].wait_recv()
            e_out[c, :, unit_cols(h)] = (
                far_acc[2 * n + 1, :, unit_cols(h)] + pair_in[fx, :, unit_cols(h)].astype(f32)
            ).astype(bf16)
            far_sums[(dx, h)] = push(
                {"sec": c}, e_out.at[c, :, unit_cols(h)], e_in.at[sx, :, unit_cols(h)]
            )
    for h in parts[1:]:
        near_mate(h)
    for h in parts:
        near_acc[:, unit_cols(h)] = widen((0, 0), h, whole)
    arrived(pend_s)
    squares = s_in[0]
    for c in range(1, S):
        squares = squares + s_in[c]
    inverse = lax.rsqrt(squares[0:1, :] / D + 1e-06)
    ni = lax.broadcasted_iota(jnp.int32, (N, 128), 0)
    nj = lax.broadcasted_iota(jnp.int32, (N, 128), 1)
    inverse = jnp.sum(jnp.where(ni == nj, inverse, 0.0), axis=1, keepdims=True)
    to_mate, from_far = [], {}
    for h in parts:
        pair[(0, h)].wait_recv()
        for dx in far:
            far_sums[(dx, h)].wait_recv()
        for j in range(0, Fh, 128):
            both = []
            for lo in (h * 2 * Fh + j, h * 2 * Fh + Fh + j):
                value = near_acc[:, lo : lo + 128] + pair_in[sx, :, lo : lo + 128].astype(f32)
                for dx in far:
                    value = value + e_in[(sx + dx) % half, :, lo : lo + 128].astype(f32)
                both.append(value * inverse)
            gate, upper = both
            f_in[s, :, h * Fh + j : h * Fh + j + 128] = (
                gate / (1.0 + jnp.exp(-gate)) * upper
            ).astype(bf16)
        piece = f_in.at[s, :, h * Fh : (h + 1) * Fh]
        for dx in far:
            from_far[(half - dx, h)] = push({"sec": at_step(dx, 1)}, piece, piece)
        to_mate.append(push(mate, piece, piece))

    def lower(step, units, first=False):
        c = at_step(*step)
        for i in range(tiles):
            cols = slice(i * 256, (i + 1) * 256)
            value = jnp.dot(f_in[c, :, units], wd[c, units, cols], preferred_element_type=f32)
            acc[:, cols] = value if first else acc[:, cols] + value

    for step in order:
        copies[("d", step)].wait()
    all_units = slice(0, Fs)
    lower((0, 0), all_units, True)
    arrived(to_mate)
    lower((0, 1), all_units)
    relayed = {}
    for h in parts:
        for dx in far:
            from_far[(dx, h)].wait_recv()
            piece = f_in.at[at_step(dx, 1), :, h * Fh : (h + 1) * Fh]
            relayed[(dx, h)] = push(mate, piece, piece)
    for dx in far:
        lower((dx, 1), all_units)
    early = slice(0, (NH - 1) * Fh)
    late = slice((NH - 1) * Fh, Fs)
    for dx in far:
        for h in parts[:-1]:
            relayed[(dx, h)].wait_recv()
        lower((dx, 0), early)
    for dx in far[:-1]:
        relayed[(dx, NH - 1)].wait_recv()
        lower((dx, 0), late)
    relayed[(far[-1], NH - 1)].wait_recv()
    c = at_step(far[-1], 0)
    pend = []
    for span in spans:
        for i in range(*span):
            cols = slice(i * 256, (i + 1) * 256)
            value = jnp.dot(f_in[c, :, late], wd[c, late, cols], preferred_element_type=f32)
            deal(g_out, i, acc[:, cols] + value)
        pend.append(tp_round(g_out, g_in, span))
    for span, copies_in in zip(spans, pend):
        arrived(copies_in)
        total = stream_buf[:, lanes(span)] + tp_sum(g_out, g_in, span)
        out[:, span[0] * 256 : span[1] * 256] = unfold(total).astype(bf16)
    for copy in started:
        copy.wait_send()


def local(
    resid,
    query,
    new_kv,
    key_cache,
    cached_value_rows,
    cache_len,
    assign,
    out_weight,
    norm_gain,
    gate_weight,
    up_weight,
    down_weight,
):
    group = query.shape[0]
    per_device = key_cache.shape[0]
    tp_index = lax.axis_index("tp")
    sec_index = lax.axis_index("sec")
    tp_count = lax.axis_size("tp")
    local_slots = lax.dynamic_slice_in_dim(assign, tp_index * group, group)
    full_query, full_pairs = (
        lax.all_gather(query, "sec", axis=1, tiled=True),
        lax.all_gather(new_kv, "sec", axis=1, tiled=True),
    )
    wanted = sec_index * per_device + lax.iota(jnp.int32, per_device)
    picker = (local_slots[None, :] == wanted[:, None]).astype(jnp.bfloat16)
    my_query = jnp.dot(picker, full_query, preferred_element_type=jnp.float32).astype(jnp.bfloat16)
    my_pairs = jnp.dot(picker, full_pairs, preferred_element_type=jnp.float32).astype(jnp.bfloat16)
    attended = attend_slots(my_query, my_pairs, key_cache, cached_value_rows, cache_len)
    request_ids = lax.iota(jnp.int32, group * tp_count)
    slot_block = lax.all_gather(attended, "sec", axis=0, tiled=True)
    received = lax.all_to_all(slot_block, "tp", split_axis=1, concat_axis=0, tiled=True)
    position = request_ids // group * group + assign
    ordered = jnp.take(received, position, axis=0)
    block = ordered
    attn_out = lax.psum_scatter(
        jnp.dot(block, out_weight, preferred_element_type=jnp.float32).astype(jnp.bfloat16),
        "tp",
        scatter_dimension=0,
        tiled=True,
    ).astype(jnp.float32)
    stream = resid.astype(jnp.float32) + attn_out
    squares = lax.psum(jnp.sum(stream * stream, axis=1), "sec")
    inverse = lax.rsqrt(squares / D + 1e-06)
    normed = (stream * inverse[:, None] * norm_gain.astype(jnp.float32)[None, :]).astype(
        jnp.bfloat16
    )
    piece = lax.all_gather(normed, "tp", axis=0, tiled=True)
    gate_part = jnp.dot(piece, gate_weight, preferred_element_type=jnp.float32)
    up_part = jnp.dot(piece, up_weight, preferred_element_type=jnp.float32)
    projected = jnp.concatenate([gate_part, up_part], axis=1)
    width = gate_weight.shape[1]
    share = lax.psum_scatter(
        projected.astype(jnp.bfloat16), "sec", scatter_dimension=0, tiled=True
    ).astype(jnp.float32)
    hidden = lax.all_gather(gated_units(share, width), "sec", axis=0, tiled=True)
    block = hidden
    ff_out = lax.psum_scatter(
        jnp.dot(block, down_weight, preferred_element_type=jnp.float32).astype(jnp.bfloat16),
        "tp",
        scatter_dimension=0,
        tiled=True,
    ).astype(jnp.float32)
    return (stream + ff_out).astype(jnp.bfloat16)


def fused(
    resid,
    query,
    new_kv,
    key_cache,
    cached_value_rows,
    cache_len,
    assign,
    out_weight,
    norm_gain,
    gate_weight,
    up_weight,
    down_weight,
):
    S, T = lax.axis_size("sec"), lax.axis_size("tp")
    G, R = query.shape[0], key_cache.shape[0]
    N = G * T
    RH = up_to(R * (QUERY_HEADS // T), ROWS16)
    RQ = up_to(R * (QUERY_HEADS // S), ROWS16)
    Dl, Hl, F, kvl = resid.shape[1], out_weight.shape[0], gate_weight.shape[1], new_kv.shape[1]
    Fs = F // S
    NH = HIDDEN_PARTS
    remote = 4 * (S - 1) + 10 * (T - 1) + (3 * S // 2 + 2) * NH
    bf16, f32 = jnp.bfloat16, jnp.float32
    V = pltpu.VMEM
    vm = pl.BlockSpec(memory_space=pltpu.VMEM)
    hbm = pl.BlockSpec(memory_space=pl.ANY)
    scratch = [
        V(resid.shape, bf16),
        V(query.shape, bf16),
        V(new_kv.shape, bf16),
        V((1, N), jnp.int32),
        V(norm_gain.shape, bf16),
        pltpu.SMEM(cache_len.shape, jnp.int32),
        V(key_cache.shape, bf16),
        V(cached_value_rows.shape, bf16),
        V((Hl, Dl), bf16),
        V((S, Dl, Fs), bf16),
        V((S, Dl, Fs), bf16),
        V((S, Fs, Dl), bf16),
        V((S, RQ, HEAD_WIDTH), bf16),
        V((S, 8, kvl), bf16),
        V((S, RQ, HEAD_WIDTH), bf16),
        V((S, 8, kvl), bf16),
        V((R, QUERY_HEADS, HEAD_WIDTH), f32),
        V((T, RH, HEAD_WIDTH), f32),
        V((T, RH, HEAD_WIDTH), bf16),
        V((S, T, RH, HEAD_WIDTH), bf16),
        V((QUERY_HEADS // T * N, S * T * RH), bf16),
        V((N, Hl), bf16),
        V((T, 2 * G, Dl // 2), bf16),
        V((T, 2 * G, Dl // 2), bf16),
        V((T, 2 * G, Dl // 2), bf16),
        V((T, 8, 128), f32),
        V((N, Dl), bf16),
        V((S, 8, 128), f32),
        V((S, N, 2 * Fs), bf16),
        V((S // 2, N, 2 * Fs), bf16),
        V((S // 2, N, 2 * Fs), bf16),
        V((S, N, Fs), bf16),
        V((N, Dl), f32),
        V((2 * (S // 2 - 1), N, 2 * Fs), f32),
        V((N, 2 * Fs), f32),
        V((T, 2 * G, Dl // 2), bf16),
        V((T, 2 * G, Dl // 2), bf16),
        V((2 * G, Dl // 2), f32),
        pltpu.SemaphoreType.DMA((2 * R + 7 + 3 * S,)),
        pltpu.SemaphoreType.DMA((remote,)),
        pltpu.SemaphoreType.DMA((remote,)),
    ]
    return pl.pallas_call(
        functools.partial(fused_kernel, (S, T, G, R, NH)),
        out_shape=pltpu.VMEM(resid.shape, bf16),
        in_specs=[hbm] * 12,
        out_specs=vm,
        scratch_shapes=scratch,
        compiler_params=pltpu.CompilerParams(
            collective_id=0, has_side_effects=True, vmem_limit_bytes=54 * 2**20
        ),
    )(
        resid,
        query,
        new_kv,
        assign.reshape(1, N),
        norm_gain,
        cache_len,
        key_cache,
        cached_value_rows,
        out_weight,
        gate_weight,
        up_weight,
        down_weight,
    )


def layer(*args):
    query, key_cache, out_weight, gate_weight = args[1], args[3], args[7], args[9]
    shapes = (
        query.shape[0],
        key_cache.shape[0],
        out_weight.shape[0],
        gate_weight.shape[1],
        lax.axis_size("sec"),
        lax.axis_size("tp"),
    )
    return fused(*args) if fits_kernel(shapes) else local(*args)


def solution(mesh):
    return jax.shard_map(
        layer,
        mesh=mesh,
        in_specs=(
            P(("rep", "tp"), "sec"),
            P(("rep", "tp"), "sec"),
            P(("rep", "tp"), "sec"),
            P(("rep", "sec", "tp"), None, None),
            P(("rep", "sec", "tp"), None, None),
            P(("rep", "sec", "tp")),
            P("rep"),
            P("tp", "sec"),
            P("sec"),
            P("sec", "tp"),
            P("sec", "tp"),
            P("tp", "sec"),
        ),
        out_specs=P(("rep", "tp"), "sec"),
        check_vma=False,
    )
```

```python
import functools
import math

import jax
import jax.numpy as jnp
from jax import lax
from jax.experimental import pallas as pl
from jax.experimental.pallas import tpu as pltpu
from jax.sharding import PartitionSpec as P

D = 5120
QUERY_HEADS = 40
KEY_VALUE_HEADS = 8
HEAD_WIDTH = 128
CACHE_SLOTS = 224


def attend_slots(query_rows, key_value_pairs, stored_keys, stored_values, lengths):
    cache_slots = query_rows.shape[0]
    group_query = QUERY_HEADS // KEY_VALUE_HEADS
    query_head_rows = query_rows.reshape(cache_slots, KEY_VALUE_HEADS, group_query, HEAD_WIDTH)
    paired_heads = key_value_pairs.reshape(cache_slots, KEY_VALUE_HEADS, 2, HEAD_WIDTH)
    fresh_keys = paired_heads[:, :, 0]
    fresh_values = paired_heads[:, :, 1]
    earlier_keys = stored_keys.reshape(cache_slots, CACHE_SLOTS, KEY_VALUE_HEADS, HEAD_WIDTH)
    earlier_values = stored_values.reshape(cache_slots, CACHE_SLOTS, KEY_VALUE_HEADS, HEAD_WIDTH)
    scaling = 1.0 / math.sqrt(HEAD_WIDTH)
    past_scores = (
        jnp.einsum(
            "rkgd,rlkd->rkgl", query_head_rows, earlier_keys, preferred_element_type=jnp.float32
        )
        * scaling
    )
    fresh_scores = (
        jnp.einsum("rkgd,rkd->rkg", query_head_rows, fresh_keys, preferred_element_type=jnp.float32)
        * scaling
    )
    valid = lax.broadcasted_iota(jnp.int32, (cache_slots, CACHE_SLOTS), 1) < lengths[:, None]
    past_scores = jnp.where(valid[:, None, None, :], past_scores, -1e30)
    highest = jnp.maximum(jnp.max(past_scores, axis=-1), fresh_scores)
    past_exp = jnp.exp(past_scores - highest[..., None])
    fresh_exp = jnp.exp(fresh_scores - highest)
    denominator = jnp.sum(past_exp, axis=-1) + fresh_exp
    past_weights = (past_exp / denominator[..., None]).astype(jnp.bfloat16)
    fresh_weights = (fresh_exp / denominator).astype(jnp.bfloat16)
    mixed = jnp.einsum(
        "rkgl,rlkd->rkgd", past_weights, earlier_values, preferred_element_type=jnp.float32
    )
    mixed = (
        mixed
        + fresh_weights.astype(jnp.float32)[..., None]
        * fresh_values.astype(jnp.float32)[:, :, None, :]
    )
    return mixed.reshape(cache_slots, QUERY_HEADS * HEAD_WIDTH).astype(jnp.bfloat16)


def gated_units(values, width):
    return (jax.nn.silu(values[:, :width]) * values[:, width:]).astype(jnp.bfloat16)


MESH = pl.DeviceIdType.MESH
ROWS16 = 16
HIDDEN_PARTS = 2
SENDS = 16


def up_to(count, multiple):
    return -(-count // multiple) * multiple


def fits_kernel(shapes):
    group, per_device, head_cols, width, sec, tp = shapes
    return (
        sec % 2 == 0
        and sec >= 4
        and width % (sec * 256 * HIDDEN_PARTS) == 0
        and width % (sec * 256) == 0
        and head_cols % (256) == 0
        and (D // sec) % 256 == 0
        and D // sec >= 512
        and QUERY_HEADS % tp == 0
        and QUERY_HEADS % sec == 0
        and per_device <= 8
        and tp >= 2
        and per_device * sec == group
        and (group * tp) % 16 == 0
        and group * tp <= 128
    )


def fused_kernel(
    dims,
    resid_hbm,
    query_hbm,
    new_kv_hbm,
    assign_hbm,
    gain_hbm,
    lengths_hbm,
    keys,
    values,
    w_out,
    w_gate,
    w_up,
    w_down,
    out,
    resid,
    query,
    new_kv,
    assign,
    gain,
    lengths,
    kbuf,
    vbuf,
    wo,
    wg,
    wu,
    wd,
    a_q,
    a_kv,
    a_q_in,
    a_kv_in,
    qheads,
    oheads,
    b1,
    b2_in,
    pick_buf,
    ord_buf,
    c_out,
    c_in,
    d_in,
    q_in,
    x_buf,
    s_in,
    e_out,
    pair_in,
    e_in,
    f_in,
    acc,
    far_acc,
    near_acc,
    g_out,
    g_in,
    stream_buf,
    local_sem,
    send_sem,
    recv_sem,
):
    S, T, G, R, NH = dims
    N = G * T
    RH = b1.shape[1]
    Dl = resid.shape[1]
    F = w_gate.shape[1]
    Fs = F // S
    f32, bf16 = jnp.float32, jnp.bfloat16
    s = lax.axis_index("sec")
    t = lax.axis_index("tp")
    sx, sc = s // 2, s % 2
    half = S // 2
    steps = [(dx, dc) for dx in list(range(1, half)) + [0] for dc in (0, 1) if dx or dc]
    sec_peers = [((sx + dx) % half) * 2 + (sc + dc) % 2 for dx, dc in steps]
    tp_peers = [(t + k) % T for k in sorted(range(1, T), key=lambda k: -min(k, T - k))]
    if T == 4:
        tp_peers = [T - 1 - t, (t + 2) % T, t + 1 - 2 * (t % 2)]

    twin = sx * 2 + (1 - sc)
    barrier = pltpu.get_barrier_semaphore()
    for c in sec_peers:
        pl.semaphore_signal(barrier, inc=1, device_id={"sec": c}, device_id_type=MESH)
    for c in tp_peers:
        pl.semaphore_signal(barrier, inc=1, device_id={"tp": c}, device_id_type=MESH)
        pl.semaphore_signal(
            barrier, inc=1, device_id={"sec": twin, "tp": c}, device_id_type=MESH
        )

    copies = {}
    count, used = [0], {}

    def fetch(name, src, dst, after=None):
        if after is None:
            slot = count[0]
            count[0] += 1
        else:
            slot = used[after]
        used[name] = slot
        copy = pltpu.make_async_copy(src, dst, local_sem.at[slot])
        copy.start()
        copies[name] = copy

    fetch("assign", assign_hbm, assign)
    fetch("query", query_hbm, query)
    fetch("new_kv", new_kv_hbm, new_kv)
    fetch("lengths", lengths_hbm, lengths)
    fetch("resid", resid_hbm, resid)
    fetch("gain", gain_hbm, gain)
    for r in range(R):
        fetch(("k", r), keys.at[r], kbuf.at[r])
        fetch(("v", r), values.at[r], vbuf.at[r])
    def at_step(dx, dc):
        return ((sx + dx) % half) * 2 + (sc + dc) % 2

    order = [(dx, dc) for dx in list(range(1, half)) + [0] for dc in (1, 0)]

    hs = QUERY_HEADS // S
    ht = QUERY_HEADS // T
    HW = HEAD_WIDTH
    GQ = QUERY_HEADS // KEY_VALUE_HEADS
    GP = up_to(G, ROWS16)
    RQ = a_q.shape[1]
    copies["assign"].wait()
    row_a = assign[...].astype(f32)
    ii = lax.broadcasted_iota(jnp.int32, (N, N), 0)
    jj = lax.broadcasted_iota(jnp.int32, (N, N), 1)
    col_a = jnp.sum(jnp.where(ii == jj, jnp.broadcast_to(row_a, (N, N)), 0.0), axis=1, keepdims=True)

    def own_slots(width):
        pi = lax.broadcasted_iota(jnp.int32, (N, width), 0)
        pj = lax.broadcasted_iota(jnp.int32, (N, width), 1)
        hit = pi == pj + t * G
        if width > G:
            stripe = jnp.zeros((N, width), jnp.int32)
            for j in range(1, width // GP):
                stripe = stripe + jnp.where(pj >= j * GP, GP, 0)
            hit = pi == pj - stripe + t * G
            hit = hit & (pj - stripe < G)
        return jnp.sum(
            jnp.where(hit, jnp.broadcast_to(col_a, (N, width)), 0.0)
            + jnp.where(hit, 1.0, 0.0),
            axis=0,
            keepdims=True,
        ) - 1.0

    pr = lax.broadcasted_iota(jnp.int32, (S * 8, 1), 0)
    slot = jnp.full((S * 8, 1), -2.0, f32)
    for c in range(S):
        for r in range(R):
            slot = jnp.where(pr == c * 8 + r, float(c * R + r), slot)
    picker = jnp.where(
        jnp.broadcast_to(slot, (S * 8, G)) == jnp.broadcast_to(own_slots(G), (S * 8, G)), 1.0, 0.0
    ).astype(bf16)
    qr = lax.broadcasted_iota(jnp.int32, (S * RQ, 1), 0)
    block = jnp.zeros((S * RQ, 1), jnp.int32)
    for c in range(1, S):
        block = block + jnp.where(qr >= c * RQ, 1, 0)
    place = qr - block * RQ
    turn = jnp.zeros((S * RQ, 1), jnp.int32)
    for r in range(1, R):
        turn = turn + jnp.where(place >= r * hs, 1, 0)
    qc = lax.broadcasted_iota(jnp.int32, (1, hs * GP), 1)
    stripe = jnp.zeros((1, hs * GP), jnp.int32)
    for j in range(1, hs):
        stripe = stripe + jnp.where(qc >= j * GP, 1, 0)
    wanted = jnp.where(place < R * hs, block * R + turn, -2).astype(f32)
    q_picker = jnp.where(
        (jnp.broadcast_to(wanted, (S * RQ, hs * GP)) == jnp.broadcast_to(own_slots(hs * GP), (S * RQ, hs * GP)))
        & (jnp.broadcast_to(place - turn * hs, (S * RQ, hs * GP)) == jnp.broadcast_to(stripe, (S * RQ, hs * GP))),
        1.0,
        0.0,
    ).astype(bf16)
    copies["query"].wait()
    tall = query[...].astype(f32)
    if GP > G:
        tall = jnp.concatenate([tall, jnp.zeros((GP - G, Dl), f32)], axis=0)
    stacked = jnp.concatenate([tall[:, j * HW : (j + 1) * HW] for j in range(hs)], axis=0).astype(bf16)
    picked_q = jnp.dot(q_picker, stacked, preferred_element_type=f32).astype(bf16)
    for c in range(S):
        a_q[c] = picked_q[c * RQ : (c + 1) * RQ]
    copies["new_kv"].wait()
    picked_kv = jnp.dot(picker, new_kv[...], preferred_element_type=f32)
    for c in range(S):
        a_kv[c] = picked_kv[c * 8 : c * 8 + 8].astype(bf16)
    pl.semaphore_wait(barrier, len(sec_peers) + 2 * len(tp_peers))

    started = []

    sends = send_sem.shape[0]
    taken = [0]

    def fresh(amount):
        taken[0] += amount
        return list(range(taken[0] - amount, taken[0]))

    query_slots, kv_slots = fresh(S - 1), fresh(S - 1)
    head_slots, gather_slots = fresh(T), fresh(S - 1)
    sum_slots = fresh(2 * (T - 1))
    spread_slots = kv_slots + head_slots + gather_slots
    spread_slots = spread_slots + fresh(max(0, 3 * (T - 1) - len(spread_slots)))
    list_query, list_kv, list_head = list(query_slots), list(kv_slots), list(head_slots)
    list_gather, list_sum = list(gather_slots), list(sum_slots)
    hop_slots = fresh(NH * (4 * (half - 1) + 2))

    def push(dest, src, dst, slots):
        turn = len(started)
        if turn >= sends:
            started[turn - sends].wait_send()
        copy = pltpu.make_async_remote_copy(
            src_ref=src,
            dst_ref=dst,
            send_sem=send_sem.at[turn % sends],
            recv_sem=recv_sem.at[slots.pop(0)],
            device_id=dest,
            device_id_type=MESH,
        )
        copy.start()
        started.append(copy)
        return copy

    def arrived(pending):
        for copy in pending:
            copy.wait_recv()

    pend = []
    for c in sec_peers:
        pend.append(push({"sec": c}, a_q.at[c], a_q_in.at[s], list_query))
    for c in sec_peers:
        pend.append(push({"sec": c}, a_kv.at[c], a_kv_in.at[s], list_kv))
    a_q_in[s] = a_q[s]
    a_kv_in[s] = a_kv[s]
    oheads[...] = jnp.zeros(oheads.shape, f32)
    for copy in pend:
        copy.wait_recv()

    fetch("wo", w_out, wo, "assign")
    for step in order:
        c = at_step(*step)
        cols = pl.ds(pl.multiple_of(c * Fs, Fs), Fs)
        fetch(("g", step), w_gate.at[:, cols], wg.at[c])
        fetch(("u", step), w_up.at[:, cols], wu.at[c])

    copies["lengths"].wait()
    for r in range(R):
        copies[("k", r)].wait()
        copies[("v", r)].wait()
    for c in range(S):
        blk = a_q_in[c].astype(f32)
        for r in range(R):
            qheads[r, c * hs : (c + 1) * hs, :] = blk[r * hs : (r + 1) * hs, :]
    pairs = jnp.concatenate([a_kv_in[c].astype(f32) for c in range(S)], axis=1)
    new_k = jnp.concatenate(
        [pairs[:, 2 * k * HW : (2 * k + 1) * HW] for k in range(KEY_VALUE_HEADS)], axis=1
    )
    new_v = jnp.concatenate(
        [pairs[:, (2 * k + 1) * HW : (2 * k + 2) * HW] for k in range(KEY_VALUE_HEADS)], axis=1
    )
    KW = KEY_VALUE_HEADS * HW
    hrow = lax.broadcasted_iota(jnp.int32, (QUERY_HEADS, KW), 0)
    hcol = lax.broadcasted_iota(jnp.int32, (QUERY_HEADS, KW), 1)
    low = jnp.zeros((QUERY_HEADS, KW), jnp.int32)
    for k in range(1, KEY_VALUE_HEADS):
        low = low + jnp.where(hcol >= k * HW, 1, 0)
    diag = (hrow >= low * GQ) & (hrow < low * GQ + GQ)
    scaling = 1.0 / math.sqrt(HW)
    slots = keys.shape[1]
    each = range(R)
    wide_q = [
        jnp.where(diag, jnp.concatenate([qheads[r]] * KEY_VALUE_HEADS, axis=1), 0.0) for r in each
    ]
    past = [
        lax.dot_general(
            wide_q[r].astype(bf16),
            kbuf[r],
            (((1,), (1,)), ((), ())),
            preferred_element_type=f32,
        )
        * scaling
        for r in each
    ]
    fresh = [
        jnp.sum(wide_q[r] * new_k[r : r + 1, :], axis=1, keepdims=True) * scaling for r in each
    ]
    position = lax.broadcasted_iota(jnp.int32, (QUERY_HEADS, slots), 1)
    past = [jnp.where(position < lengths[r], past[r], -1e30) for r in each]
    highest = [jnp.maximum(jnp.max(past[r], axis=1, keepdims=True), fresh[r]) for r in each]
    past_exp = [jnp.exp(past[r] - highest[r]) for r in each]
    fresh_exp = [jnp.exp(fresh[r] - highest[r]) for r in each]
    total = [jnp.sum(past_exp[r], axis=1, keepdims=True) + fresh_exp[r] for r in each]
    past_w = [(past_exp[r] / total[r]).astype(bf16) for r in each]
    fresh_w = [(fresh_exp[r] / total[r]).astype(bf16).astype(f32) for r in each]
    mixed = [jnp.dot(past_w[r], vbuf[r], preferred_element_type=f32) for r in each]
    for r in each:
        spread = jnp.where(diag, mixed[r] + fresh_w[r] * new_v[r : r + 1, :], 0.0)
        small = spread[:, 0:HW]
        for k in range(1, KEY_VALUE_HEADS):
            small = small + spread[:, k * HW : (k + 1) * HW]
        for c in range(T):
            oheads[c, r * ht : (r + 1) * ht, :] = small[c * ht : (c + 1) * ht, :]
    for c in range(T):
        b1[c] = oheads[c].astype(bf16)
    pend = [push({"sec": twin, "tp": c}, b1.at[c], b2_in.at[twin, t], list_head) for c in tp_peers]
    pend.append(push({"sec": twin}, b1.at[t], b2_in.at[twin, t], list_head))
    spare = [(part, r) for part in "kv" for r in range(R)]
    for step in reversed(order):
        c = at_step(*step)
        rows = pl.ds(pl.multiple_of(c * Fs, Fs), Fs)
        fetch(("d", step), w_down.at[rows, :], wd.at[c], spare.pop(0) if spare else None)

    tiles = Dl // 256
    cut = (tiles + 1) // 2
    spans = [(0, cut), (cut, tiles)]

    def fold(value):
        return jnp.concatenate(
            [
                jnp.concatenate([value[:, i : i + 128], value[:, i + 128 : i + 256]], axis=0)
                for i in range(0, value.shape[1], 256)
            ],
            axis=1,
        )

    def unfold(value):
        rows = value.shape[0] // 2
        return jnp.concatenate(
            [
                part
                for i in range(0, value.shape[1], 128)
                for part in (value[:rows, i : i + 128], value[rows:, i : i + 128])
            ],
            axis=1,
        )

    def lanes(span):
        return slice(span[0] * 128, span[1] * 128)

    copies["resid"].wait()
    copies["gain"].wait()
    stream_buf[...] = fold(resid[...].astype(f32))
    gain_rows = fold(jnp.broadcast_to(gain[...].astype(f32).reshape(1, Dl), (G, Dl)))

    pos = jnp.zeros((1, N), f32)
    for a in range(G):
        c, r = a // R, a % R
        held = c + 1 - 2 * (c % 2)
        pos = pos + jnp.where(row_a == float(a), float(held * T * RH + r * ht), 0.0)
    lane = lax.broadcasted_iota(jnp.int32, (1, N), 1)
    for g in range(1, T):
        pos = pos + jnp.where(lane >= g * G, float(RH), 0.0)
    pos_col = jnp.sum(jnp.where(ii == jj, pos, 0.0), axis=1, keepdims=True)
    spot = lax.broadcasted_iota(jnp.int32, (N, S * T * RH), 1).astype(f32)
    for j in range(ht):
        pick_buf[j * N : (j + 1) * N, :] = jnp.where(spot == pos_col + float(j), 1.0, 0.0).astype(bf16)
    arrived(pend)
    pend = [push({"sec": c}, b2_in.at[s], b2_in.at[s], list_gather) for c in sec_peers]
    copies["wo"].wait()
    arrived(pend)
    rows = jnp.concatenate([b2_in[c, g] for c in range(S) for g in range(T)], axis=0)
    placed = jnp.dot(pick_buf[...], rows, preferred_element_type=f32).astype(bf16)
    for j in range(ht):
        ord_buf[:, j * HW : (j + 1) * HW] = placed[j * N : (j + 1) * N]

    def tp_round(out_buf, in_buf, span, slots):
        return [
            push({"tp": g}, out_buf.at[g, :, lanes(span)], in_buf.at[t, :, lanes(span)], slots)
            for g in tp_peers
        ]

    def tp_sum(out_buf, in_buf, span):
        value = out_buf[t, :, lanes(span)].astype(f32)
        for g in tp_peers:
            value = value + in_buf[g, :, lanes(span)].astype(f32)
        return value

    def deal(out_buf, i, value):
        for g in range(T):
            out_buf[g, :, i * 128 : (i + 1) * 128] = fold(value[g * G : (g + 1) * G, :]).astype(bf16)

    pend = []
    for span in spans:
        for i in range(*span):
            deal(
                c_out,
                i,
                jnp.dot(ord_buf[...], wo[:, i * 256 : (i + 1) * 256], preferred_element_type=f32),
            )
        pend.append(tp_round(c_out, c_in, span, list_sum))
    squares = jnp.zeros((G, 1), f32)
    pend_d = []
    for span, copies_in in zip(spans, pend):
        arrived(copies_in)
        stream = stream_buf[:, lanes(span)] + tp_sum(c_out, c_in, span)
        stream_buf[:, lanes(span)] = stream
        d_in[t, :, lanes(span)] = (stream * gain_rows[:, lanes(span)]).astype(bf16)
        piece = d_in.at[t, :, lanes(span)]
        pend_d.append([push({"tp": g}, piece, piece, spread_slots) for g in tp_peers])
        part = jnp.sum(stream * stream, axis=1, keepdims=True)
        squares = squares + part[:G] + part[G:]
    qi = lax.broadcasted_iota(jnp.int32, (G, 128), 0)
    qj = lax.broadcasted_iota(jnp.int32, (G, 128), 1)
    squares = jnp.where(qj == qi + t * G, squares, 0.0)
    q_in[t] = jnp.broadcast_to(jnp.sum(squares, axis=0, keepdims=True), (8, 128))
    pend_q = [push({"tp": g}, q_in.at[t], q_in.at[t], spread_slots) for g in tp_peers]

    def take(span):
        for i in range(*span):
            blks = [d_in[g, :, i * 128 : (i + 1) * 128].astype(f32) for g in range(T)]
            for side in (0, 1):
                cols = slice(i * 256 + side * 128, i * 256 + side * 128 + 128)
                x_buf[:, cols] = jnp.concatenate(
                    [blk[side * G : side * G + G] for blk in blks], axis=0
                ).astype(bf16)

    mate = {"sec": at_step(0, 1)}
    Fh = Fs // NH
    parts = range(NH)
    ready = set()

    def need(step):
        for part in "gu":
            if (part, step) not in ready:
                copies[(part, step)].wait()
                ready.add((part, step))

    def widen(step, h, depth, base=None):
        need(step)
        c = at_step(*step)
        value = [
            jnp.dot(
                x_buf[:, depth],
                weight[c, depth, h * Fh : (h + 1) * Fh],
                preferred_element_type=f32,
            )
            for weight in (wg, wu)
        ]
        value = jnp.concatenate(value, axis=1)
        return value if base is None else base + value

    def unit_cols(h):
        return slice(h * 2 * Fh, (h + 1) * 2 * Fh)

    first, second = [slice(lo * 256, hi * 256) for lo, hi in spans]
    whole = slice(0, Dl)
    far = list(range(1, half))
    arrived(pend_d[0])
    take(spans[0])
    for n, dx in enumerate(far):
        for dc in (0, 1):
            for h in parts:
                far_acc[2 * n + dc, :, unit_cols(h)] = widen((dx, dc), h, first)
    arrived(pend_d[1])
    take(spans[1])
    arrived(pend_q)
    squares = q_in[0]
    for g in range(1, T):
        squares = squares + q_in[g]
    s_in[s] = squares
    pend_s = [push({"sec": c}, s_in.at[s], s_in.at[s], query_slots) for c in sec_peers]
    pair, far_sums = {}, {}
    for n, dx in enumerate(far):
        fx = (sx + dx) % half
        c = at_step(dx, 0)
        for h in parts:
            e_out[c, :, unit_cols(h)] = widen(
                (dx, 0), h, second, far_acc[2 * n, :, unit_cols(h)]
            ).astype(bf16)
            pair[(dx, h)] = push(
                mate, e_out.at[c, :, unit_cols(h)], pair_in.at[fx, :, unit_cols(h)], hop_slots
            )
        for h in parts:
            far_acc[2 * n + 1, :, unit_cols(h)] = widen(
                (dx, 1), h, second, far_acc[2 * n + 1, :, unit_cols(h)]
            )

    def near_mate(h):
        c = at_step(0, 1)
        e_out[c, :, unit_cols(h)] = widen((0, 1), h, whole).astype(bf16)
        pair[(0, h)] = push(mate, e_out.at[c, :, unit_cols(h)], pair_in.at[sx, :, unit_cols(h)], hop_slots)

    near_mate(0)
    for h in parts:
        for n, dx in enumerate(far):
            fx = (sx + dx) % half
            c = at_step(dx, 1)
            pair[(dx, h)].wait_recv()
            e_out[c, :, unit_cols(h)] = (
                far_acc[2 * n + 1, :, unit_cols(h)] + pair_in[fx, :, unit_cols(h)].astype(f32)
            ).astype(bf16)
            far_sums[(dx, h)] = push(
                {"sec": c}, e_out.at[c, :, unit_cols(h)], e_in.at[sx, :, unit_cols(h)], hop_slots
            )
    for h in parts[1:]:
        near_mate(h)
    for h in parts:
        near_acc[:, unit_cols(h)] = widen((0, 0), h, whole)
    arrived(pend_s)
    squares = s_in[0]
    for c in range(1, S):
        squares = squares + s_in[c]
    inverse = lax.rsqrt(squares[0:1, :] / D + 1e-06)
    ni = lax.broadcasted_iota(jnp.int32, (N, 128), 0)
    nj = lax.broadcasted_iota(jnp.int32, (N, 128), 1)
    inverse = jnp.sum(jnp.where(ni == nj, inverse, 0.0), axis=1, keepdims=True)
    to_mate, from_far = [], {}
    for h in parts:
        pair[(0, h)].wait_recv()
        for dx in far:
            far_sums[(dx, h)].wait_recv()
        for j in range(0, Fh, 128):
            both = []
            for lo in (h * 2 * Fh + j, h * 2 * Fh + Fh + j):
                value = near_acc[:, lo : lo + 128] + pair_in[sx, :, lo : lo + 128].astype(f32)
                for dx in far:
                    value = value + e_in[(sx + dx) % half, :, lo : lo + 128].astype(f32)
                both.append(value * inverse)
            gate, upper = both
            f_in[s, :, h * Fh + j : h * Fh + j + 128] = (
                gate / (1.0 + jnp.exp(-gate)) * upper
            ).astype(bf16)
        piece = f_in.at[s, :, h * Fh : (h + 1) * Fh]
        for dx in far:
            from_far[(half - dx, h)] = push({"sec": at_step(dx, 1)}, piece, piece, hop_slots)
        to_mate.append(push(mate, piece, piece, hop_slots))

    def lower(step, units, first=False):
        c = at_step(*step)
        for i in range(tiles):
            cols = slice(i * 256, (i + 1) * 256)
            value = jnp.dot(f_in[c, :, units], wd[c, units, cols], preferred_element_type=f32)
            acc[:, cols] = value if first else acc[:, cols] + value

    for step in order:
        copies[("d", step)].wait()
    all_units = slice(0, Fs)
    lower((0, 0), all_units, True)
    arrived(to_mate)
    lower((0, 1), all_units)
    relayed = {}
    for h in parts:
        for dx in far:
            from_far[(dx, h)].wait_recv()
            piece = f_in.at[at_step(dx, 1), :, h * Fh : (h + 1) * Fh]
            relayed[(dx, h)] = push(mate, piece, piece, hop_slots)
    for dx in far:
        lower((dx, 1), all_units)
    early = slice(0, (NH - 1) * Fh)
    late = slice((NH - 1) * Fh, Fs)
    for dx in far:
        for h in parts[:-1]:
            relayed[(dx, h)].wait_recv()
        lower((dx, 0), early)
    for dx in far[:-1]:
        relayed[(dx, NH - 1)].wait_recv()
        lower((dx, 0), late)
    relayed[(far[-1], NH - 1)].wait_recv()
    c = at_step(far[-1], 0)
    pend = []
    for span in spans:
        for i in range(*span):
            cols = slice(i * 256, (i + 1) * 256)
            value = jnp.dot(f_in[c, :, late], wd[c, late, cols], preferred_element_type=f32)
            deal(g_out, i, acc[:, cols] + value)
        pend.append(tp_round(g_out, g_in, span, sum_slots))
    for span, copies_in in zip(spans, pend):
        arrived(copies_in)
        total = stream_buf[:, lanes(span)] + tp_sum(g_out, g_in, span)
        out[:, span[0] * 256 : span[1] * 256] = unfold(total).astype(bf16)
    for copy in started[-sends:]:
        copy.wait_send()


def local(
    resid,
    query,
    new_kv,
    key_cache,
    cached_value_rows,
    cache_len,
    assign,
    out_weight,
    norm_gain,
    gate_weight,
    up_weight,
    down_weight,
):
    group = query.shape[0]
    per_device = key_cache.shape[0]
    tp_index = lax.axis_index("tp")
    sec_index = lax.axis_index("sec")
    tp_count = lax.axis_size("tp")
    local_slots = lax.dynamic_slice_in_dim(assign, tp_index * group, group)
    full_query, full_pairs = (
        lax.all_gather(query, "sec", axis=1, tiled=True),
        lax.all_gather(new_kv, "sec", axis=1, tiled=True),
    )
    wanted = sec_index * per_device + lax.iota(jnp.int32, per_device)
    picker = (local_slots[None, :] == wanted[:, None]).astype(jnp.bfloat16)
    my_query = jnp.dot(picker, full_query, preferred_element_type=jnp.float32).astype(jnp.bfloat16)
    my_pairs = jnp.dot(picker, full_pairs, preferred_element_type=jnp.float32).astype(jnp.bfloat16)
    attended = attend_slots(my_query, my_pairs, key_cache, cached_value_rows, cache_len)
    request_ids = lax.iota(jnp.int32, group * tp_count)
    slot_block = lax.all_gather(attended, "sec", axis=0, tiled=True)
    received = lax.all_to_all(slot_block, "tp", split_axis=1, concat_axis=0, tiled=True)
    position = request_ids // group * group + assign
    ordered = jnp.take(received, position, axis=0)
    block = ordered
    attn_out = lax.psum_scatter(
        jnp.dot(block, out_weight, preferred_element_type=jnp.float32).astype(jnp.bfloat16),
        "tp",
        scatter_dimension=0,
        tiled=True,
    ).astype(jnp.float32)
    stream = resid.astype(jnp.float32) + attn_out
    squares = lax.psum(jnp.sum(stream * stream, axis=1), "sec")
    inverse = lax.rsqrt(squares / D + 1e-06)
    normed = (stream * inverse[:, None] * norm_gain.astype(jnp.float32)[None, :]).astype(
        jnp.bfloat16
    )
    piece = lax.all_gather(normed, "tp", axis=0, tiled=True)
    gate_part = jnp.dot(piece, gate_weight, preferred_element_type=jnp.float32)
    up_part = jnp.dot(piece, up_weight, preferred_element_type=jnp.float32)
    projected = jnp.concatenate([gate_part, up_part], axis=1)
    width = gate_weight.shape[1]
    share = lax.psum_scatter(
        projected.astype(jnp.bfloat16), "sec", scatter_dimension=0, tiled=True
    ).astype(jnp.float32)
    hidden = lax.all_gather(gated_units(share, width), "sec", axis=0, tiled=True)
    block = hidden
    ff_out = lax.psum_scatter(
        jnp.dot(block, down_weight, preferred_element_type=jnp.float32).astype(jnp.bfloat16),
        "tp",
        scatter_dimension=0,
        tiled=True,
    ).astype(jnp.float32)
    return (stream + ff_out).astype(jnp.bfloat16)


def fused(
    resid,
    query,
    new_kv,
    key_cache,
    cached_value_rows,
    cache_len,
    assign,
    out_weight,
    norm_gain,
    gate_weight,
    up_weight,
    down_weight,
):
    S, T = lax.axis_size("sec"), lax.axis_size("tp")
    G, R = query.shape[0], key_cache.shape[0]
    N = G * T
    RH = up_to(R * (QUERY_HEADS // T), ROWS16)
    RQ = up_to(R * (QUERY_HEADS // S), ROWS16)
    Dl, Hl, F, kvl = resid.shape[1], out_weight.shape[0], gate_weight.shape[1], new_kv.shape[1]
    Fs = F // S
    NH = HIDDEN_PARTS
    landed = 4 * (S - 1) - (S - 1) + T + 2 * (T - 1) + NH * (2 * S - 2)
    landed = landed + max(0, 3 * (T - 1) - 2 * (S - 1) - T)
    bf16, f32 = jnp.bfloat16, jnp.float32
    V = pltpu.VMEM
    vm = pl.BlockSpec(memory_space=pltpu.VMEM)
    hbm = pl.BlockSpec(memory_space=pl.ANY)
    scratch = [
        V(resid.shape, bf16),
        V(query.shape, bf16),
        V(new_kv.shape, bf16),
        V((1, N), jnp.int32),
        V(norm_gain.shape, bf16),
        pltpu.SMEM(cache_len.shape, jnp.int32),
        V(key_cache.shape, bf16),
        V(cached_value_rows.shape, bf16),
        V((Hl, Dl), bf16),
        V((S, Dl, Fs), bf16),
        V((S, Dl, Fs), bf16),
        V((S, Fs, Dl), bf16),
        V((S, RQ, HEAD_WIDTH), bf16),
        V((S, 8, kvl), bf16),
        V((S, RQ, HEAD_WIDTH), bf16),
        V((S, 8, kvl), bf16),
        V((R, QUERY_HEADS, HEAD_WIDTH), f32),
        V((T, RH, HEAD_WIDTH), f32),
        V((T, RH, HEAD_WIDTH), bf16),
        V((S, T, RH, HEAD_WIDTH), bf16),
        V((QUERY_HEADS // T * N, S * T * RH), bf16),
        V((N, Hl), bf16),
        V((T, 2 * G, Dl // 2), bf16),
        V((T, 2 * G, Dl // 2), bf16),
        V((T, 2 * G, Dl // 2), bf16),
        V((T, 8, 128), f32),
        V((N, Dl), bf16),
        V((S, 8, 128), f32),
        V((S, N, 2 * Fs), bf16),
        V((S // 2, N, 2 * Fs), bf16),
        V((S // 2, N, 2 * Fs), bf16),
        V((S, N, Fs), bf16),
        V((N, Dl), f32),
        V((2 * (S // 2 - 1), N, 2 * Fs), f32),
        V((N, 2 * Fs), f32),
        V((T, 2 * G, Dl // 2), bf16),
        V((T, 2 * G, Dl // 2), bf16),
        V((2 * G, Dl // 2), f32),
        pltpu.SemaphoreType.DMA((2 * R + 6 + 2 * S + max(0, S - 2 * R),)),
        pltpu.SemaphoreType.DMA((SENDS,)),
        pltpu.SemaphoreType.DMA((landed,)),
    ]
    return pl.pallas_call(
        functools.partial(fused_kernel, (S, T, G, R, NH)),
        out_shape=pltpu.VMEM(resid.shape, bf16),
        in_specs=[hbm] * 12,
        out_specs=vm,
        scratch_shapes=scratch,
        compiler_params=pltpu.CompilerParams(
            collective_id=0, has_side_effects=True, vmem_limit_bytes=54 * 2**20
        ),
    )(
        resid,
        query,
        new_kv,
        assign.reshape(1, N),
        norm_gain,
        cache_len,
        key_cache,
        cached_value_rows,
        out_weight,
        gate_weight,
        up_weight,
        down_weight,
    )


def layer(*args):
    query, key_cache, out_weight, gate_weight = args[1], args[3], args[7], args[9]
    shapes = (
        query.shape[0],
        key_cache.shape[0],
        out_weight.shape[0],
        gate_weight.shape[1],
        lax.axis_size("sec"),
        lax.axis_size("tp"),
    )
    return fused(*args) if fits_kernel(shapes) else local(*args)


def solution(mesh):
    return jax.shard_map(
        layer,
        mesh=mesh,
        in_specs=(
            P(("rep", "tp"), "sec"),
            P(("rep", "tp"), "sec"),
            P(("rep", "tp"), "sec"),
            P(("rep", "sec", "tp"), None, None),
            P(("rep", "sec", "tp"), None, None),
            P(("rep", "sec", "tp")),
            P("rep"),
            P("tp", "sec"),
            P("sec"),
            P("sec", "tp"),
            P("sec", "tp"),
            P("tp", "sec"),
        ),
        out_specs=P(("rep", "tp"), "sec"),
        check_vma=False,
    )
```

```python
import functools
import math

import jax
import jax.numpy as jnp
from jax import lax
from jax.experimental import pallas as pl
from jax.experimental.pallas import tpu as pltpu
from jax.sharding import PartitionSpec as P

D = 5120
QUERY_HEADS = 40
KEY_VALUE_HEADS = 8
HEAD_WIDTH = 128
CACHE_SLOTS = 224


def attend_slots(query_rows, key_value_pairs, stored_keys, stored_values, lengths):
    cache_slots = query_rows.shape[0]
    group_query = QUERY_HEADS // KEY_VALUE_HEADS
    query_head_rows = query_rows.reshape(cache_slots, KEY_VALUE_HEADS, group_query, HEAD_WIDTH)
    paired_heads = key_value_pairs.reshape(cache_slots, KEY_VALUE_HEADS, 2, HEAD_WIDTH)
    fresh_keys = paired_heads[:, :, 0]
    fresh_values = paired_heads[:, :, 1]
    earlier_keys = stored_keys.reshape(cache_slots, CACHE_SLOTS, KEY_VALUE_HEADS, HEAD_WIDTH)
    earlier_values = stored_values.reshape(cache_slots, CACHE_SLOTS, KEY_VALUE_HEADS, HEAD_WIDTH)
    scaling = 1.0 / math.sqrt(HEAD_WIDTH)
    past_scores = (
        jnp.einsum(
            "rkgd,rlkd->rkgl", query_head_rows, earlier_keys, preferred_element_type=jnp.float32
        )
        * scaling
    )
    fresh_scores = (
        jnp.einsum("rkgd,rkd->rkg", query_head_rows, fresh_keys, preferred_element_type=jnp.float32)
        * scaling
    )
    valid = lax.broadcasted_iota(jnp.int32, (cache_slots, CACHE_SLOTS), 1) < lengths[:, None]
    past_scores = jnp.where(valid[:, None, None, :], past_scores, -1e30)
    highest = jnp.maximum(jnp.max(past_scores, axis=-1), fresh_scores)
    past_exp = jnp.exp(past_scores - highest[..., None])
    fresh_exp = jnp.exp(fresh_scores - highest)
    denominator = jnp.sum(past_exp, axis=-1) + fresh_exp
    past_weights = (past_exp / denominator[..., None]).astype(jnp.bfloat16)
    fresh_weights = (fresh_exp / denominator).astype(jnp.bfloat16)
    mixed = jnp.einsum(
        "rkgl,rlkd->rkgd", past_weights, earlier_values, preferred_element_type=jnp.float32
    )
    mixed = (
        mixed
        + fresh_weights.astype(jnp.float32)[..., None]
        * fresh_values.astype(jnp.float32)[:, :, None, :]
    )
    return mixed.reshape(cache_slots, QUERY_HEADS * HEAD_WIDTH).astype(jnp.bfloat16)


def gated_units(values, width):
    return (jax.nn.silu(values[:, :width]) * values[:, width:]).astype(jnp.bfloat16)


MESH = pl.DeviceIdType.MESH
ROWS16 = 16
HIDDEN_PARTS = 4
SENDS = 10


def up_to(count, multiple):
    return -(-count // multiple) * multiple


def fits_kernel(shapes):
    group, per_device, head_cols, width, sec, tp = shapes
    return (
        sec % 2 == 0
        and sec >= 4
        and width % (sec * 256 * HIDDEN_PARTS) == 0
        and width % (sec * 256) == 0
        and head_cols % (256) == 0
        and (D // sec) % 256 == 0
        and D // sec >= 512
        and QUERY_HEADS % tp == 0
        and QUERY_HEADS % sec == 0
        and per_device <= 8
        and tp >= 2
        and per_device * sec == group
        and (group * tp) % 16 == 0
        and group * tp <= 128
    )


def fused_kernel(
    dims,
    resid_hbm,
    query_hbm,
    new_kv_hbm,
    assign_hbm,
    gain_hbm,
    lengths_hbm,
    keys,
    values,
    w_out,
    w_gate,
    w_up,
    w_down,
    out,
    resid,
    query,
    new_kv,
    assign,
    gain,
    lengths,
    kbuf,
    vbuf,
    wo,
    wg,
    wu,
    wd,
    a_q,
    a_kv,
    a_q_in,
    a_kv_in,
    qheads,
    oheads,
    b1,
    b2_in,
    pick_buf,
    ord_buf,
    c_out,
    c_in,
    d_in,
    q_in,
    x_buf,
    s_in,
    e_out,
    pair_in,
    e_in,
    f_in,
    acc,
    far_acc,
    near_acc,
    g_out,
    g_in,
    stream_buf,
    local_sem,
    send_sem,
    recv_sem,
):
    S, T, G, R, NH = dims
    N = G * T
    RH = b1.shape[1]
    Dl = resid.shape[1]
    F = w_gate.shape[1]
    Fs = F // S
    f32, bf16 = jnp.float32, jnp.bfloat16
    s = lax.axis_index("sec")
    t = lax.axis_index("tp")
    sx, sc = s // 2, s % 2
    half = S // 2
    steps = [(dx, dc) for dx in list(range(1, half)) + [0] for dc in (0, 1) if dx or dc]
    sec_peers = [((sx + dx) % half) * 2 + (sc + dc) % 2 for dx, dc in steps]
    tp_peers = [(t + k) % T for k in sorted(range(1, T), key=lambda k: -min(k, T - k))]
    if T == 4:
        tp_peers = [T - 1 - t, (t + 2) % T, t + 1 - 2 * (t % 2)]

    twin = sx * 2 + (1 - sc)
    barrier = pltpu.get_barrier_semaphore()
    for c in sec_peers:
        pl.semaphore_signal(barrier, inc=1, device_id={"sec": c}, device_id_type=MESH)
    for c in tp_peers:
        pl.semaphore_signal(barrier, inc=1, device_id={"tp": c}, device_id_type=MESH)
        pl.semaphore_signal(
            barrier, inc=1, device_id={"sec": twin, "tp": c}, device_id_type=MESH
        )

    copies = {}
    count, used = [0], {}

    def fetch(name, src, dst, after=None):
        if after is None:
            slot = count[0]
            count[0] += 1
        else:
            slot = used[after]
        used[name] = slot
        copy = pltpu.make_async_copy(src, dst, local_sem.at[slot])
        copy.start()
        copies[name] = copy

    fetch("assign", assign_hbm, assign)
    fetch("query", query_hbm, query)
    fetch("new_kv", new_kv_hbm, new_kv)
    fetch("lengths", lengths_hbm, lengths)
    fetch("resid", resid_hbm, resid)
    fetch("gain", gain_hbm, gain)
    for r in range(R):
        fetch(("k", r), keys.at[r], kbuf.at[r])
        fetch(("v", r), values.at[r], vbuf.at[r])
    def at_step(dx, dc):
        return ((sx + dx) % half) * 2 + (sc + dc) % 2

    order = [(dx, dc) for dx in list(range(1, half)) + [0] for dc in (1, 0)]

    hs = QUERY_HEADS // S
    ht = QUERY_HEADS // T
    HW = HEAD_WIDTH
    GQ = QUERY_HEADS // KEY_VALUE_HEADS
    GP = up_to(G, ROWS16)
    RQ = a_q.shape[1]
    copies["assign"].wait()
    row_a = assign[...].astype(f32)
    ii = lax.broadcasted_iota(jnp.int32, (N, N), 0)
    jj = lax.broadcasted_iota(jnp.int32, (N, N), 1)
    col_a = jnp.sum(jnp.where(ii == jj, jnp.broadcast_to(row_a, (N, N)), 0.0), axis=1, keepdims=True)

    def own_slots(width):
        pi = lax.broadcasted_iota(jnp.int32, (N, width), 0)
        pj = lax.broadcasted_iota(jnp.int32, (N, width), 1)
        hit = pi == pj + t * G
        if width > G:
            stripe = jnp.zeros((N, width), jnp.int32)
            for j in range(1, width // GP):
                stripe = stripe + jnp.where(pj >= j * GP, GP, 0)
            hit = pi == pj - stripe + t * G
            hit = hit & (pj - stripe < G)
        return jnp.sum(
            jnp.where(hit, jnp.broadcast_to(col_a, (N, width)), 0.0)
            + jnp.where(hit, 1.0, 0.0),
            axis=0,
            keepdims=True,
        ) - 1.0

    pr = lax.broadcasted_iota(jnp.int32, (S * 8, 1), 0)
    slot = jnp.full((S * 8, 1), -2.0, f32)
    for c in range(S):
        for r in range(R):
            slot = jnp.where(pr == c * 8 + r, float(c * R + r), slot)
    picker = jnp.where(
        jnp.broadcast_to(slot, (S * 8, G)) == jnp.broadcast_to(own_slots(G), (S * 8, G)), 1.0, 0.0
    ).astype(bf16)
    qr = lax.broadcasted_iota(jnp.int32, (S * RQ, 1), 0)
    block = jnp.zeros((S * RQ, 1), jnp.int32)
    for c in range(1, S):
        block = block + jnp.where(qr >= c * RQ, 1, 0)
    place = qr - block * RQ
    turn = jnp.zeros((S * RQ, 1), jnp.int32)
    for r in range(1, R):
        turn = turn + jnp.where(place >= r * hs, 1, 0)
    qc = lax.broadcasted_iota(jnp.int32, (1, hs * GP), 1)
    stripe = jnp.zeros((1, hs * GP), jnp.int32)
    for j in range(1, hs):
        stripe = stripe + jnp.where(qc >= j * GP, 1, 0)
    wanted = jnp.where(place < R * hs, block * R + turn, -2).astype(f32)
    q_picker = jnp.where(
        (jnp.broadcast_to(wanted, (S * RQ, hs * GP)) == jnp.broadcast_to(own_slots(hs * GP), (S * RQ, hs * GP)))
        & (jnp.broadcast_to(place - turn * hs, (S * RQ, hs * GP)) == jnp.broadcast_to(stripe, (S * RQ, hs * GP))),
        1.0,
        0.0,
    ).astype(bf16)
    copies["query"].wait()
    tall = query[...].astype(f32)
    if GP > G:
        tall = jnp.concatenate([tall, jnp.zeros((GP - G, Dl), f32)], axis=0)
    stacked = jnp.concatenate([tall[:, j * HW : (j + 1) * HW] for j in range(hs)], axis=0).astype(bf16)
    picked_q = jnp.dot(q_picker, stacked, preferred_element_type=f32).astype(bf16)
    for c in range(S):
        a_q[c] = picked_q[c * RQ : (c + 1) * RQ]
    copies["new_kv"].wait()
    picked_kv = jnp.dot(picker, new_kv[...], preferred_element_type=f32)
    for c in range(S):
        a_kv[c] = picked_kv[c * 8 : c * 8 + 8].astype(bf16)
    pl.semaphore_wait(barrier, len(sec_peers) + 2 * len(tp_peers))

    started = []

    sends = send_sem.shape[0]
    taken = [0]

    def fresh(amount):
        taken[0] += amount
        return list(range(taken[0] - amount, taken[0]))

    query_slots, kv_slots = fresh(S - 1), fresh(S - 1)
    head_slots, gather_slots = fresh(T), fresh(S - 1)
    sum_slots = fresh(2 * (T - 1))
    spread_slots = kv_slots + head_slots + gather_slots
    spread_slots = spread_slots + fresh(max(0, 3 * (T - 1) - len(spread_slots)))
    list_query, list_kv, list_head = list(query_slots), list(kv_slots), list(head_slots)
    list_gather, list_sum = list(gather_slots), list(sum_slots)
    hops = NH * (2 * half - 1)
    hop_slots = fresh(hops)
    unit_slots = list(spread_slots) + fresh(max(0, hops - len(spread_slots)))

    def push(dest, src, dst, slots):
        turn = len(started)
        if turn >= sends:
            started[turn - sends].wait_send()
        copy = pltpu.make_async_remote_copy(
            src_ref=src,
            dst_ref=dst,
            send_sem=send_sem.at[turn % sends],
            recv_sem=recv_sem.at[slots.pop(0)],
            device_id=dest,
            device_id_type=MESH,
        )
        copy.start()
        started.append(copy)
        return copy

    def arrived(pending):
        for copy in pending:
            copy.wait_recv()

    pend = []
    for c in sec_peers:
        pend.append(push({"sec": c}, a_q.at[c], a_q_in.at[s], list_query))
    for c in sec_peers:
        pend.append(push({"sec": c}, a_kv.at[c], a_kv_in.at[s], list_kv))
    a_q_in[s] = a_q[s]
    a_kv_in[s] = a_kv[s]
    oheads[...] = jnp.zeros(oheads.shape, f32)
    for copy in pend:
        copy.wait_recv()

    fetch("wo", w_out, wo, "assign")
    for step in order:
        c = at_step(*step)
        cols = pl.ds(pl.multiple_of(c * Fs, Fs), Fs)
        first = step == order[0]
        fetch(("g", step), w_gate.at[:, cols], wg.at[c], "query" if first else None)
        fetch(("u", step), w_up.at[:, cols], wu.at[c], "new_kv" if first else None)

    copies["lengths"].wait()
    for r in range(R):
        copies[("k", r)].wait()
        copies[("v", r)].wait()
    for c in range(S):
        blk = a_q_in[c].astype(f32)
        for r in range(R):
            qheads[r, c * hs : (c + 1) * hs, :] = blk[r * hs : (r + 1) * hs, :]
    pairs = jnp.concatenate([a_kv_in[c].astype(f32) for c in range(S)], axis=1)
    new_k = jnp.concatenate(
        [pairs[:, 2 * k * HW : (2 * k + 1) * HW] for k in range(KEY_VALUE_HEADS)], axis=1
    )
    new_v = jnp.concatenate(
        [pairs[:, (2 * k + 1) * HW : (2 * k + 2) * HW] for k in range(KEY_VALUE_HEADS)], axis=1
    )
    KW = KEY_VALUE_HEADS * HW
    hrow = lax.broadcasted_iota(jnp.int32, (QUERY_HEADS, KW), 0)
    hcol = lax.broadcasted_iota(jnp.int32, (QUERY_HEADS, KW), 1)
    low = jnp.zeros((QUERY_HEADS, KW), jnp.int32)
    for k in range(1, KEY_VALUE_HEADS):
        low = low + jnp.where(hcol >= k * HW, 1, 0)
    diag = (hrow >= low * GQ) & (hrow < low * GQ + GQ)
    scaling = 1.0 / math.sqrt(HW)
    slots = keys.shape[1]
    each = range(R)
    wide_q = [
        jnp.where(diag, jnp.concatenate([qheads[r]] * KEY_VALUE_HEADS, axis=1), 0.0) for r in each
    ]
    past = [
        lax.dot_general(
            wide_q[r].astype(bf16),
            kbuf[r],
            (((1,), (1,)), ((), ())),
            preferred_element_type=f32,
        )
        * scaling
        for r in each
    ]
    fresh = [
        jnp.sum(wide_q[r] * new_k[r : r + 1, :], axis=1, keepdims=True) * scaling for r in each
    ]
    position = lax.broadcasted_iota(jnp.int32, (QUERY_HEADS, slots), 1)
    past = [jnp.where(position < lengths[r], past[r], -1e30) for r in each]
    highest = [jnp.maximum(jnp.max(past[r], axis=1, keepdims=True), fresh[r]) for r in each]
    past_exp = [jnp.exp(past[r] - highest[r]) for r in each]
    fresh_exp = [jnp.exp(fresh[r] - highest[r]) for r in each]
    total = [jnp.sum(past_exp[r], axis=1, keepdims=True) + fresh_exp[r] for r in each]
    past_w = [(past_exp[r] / total[r]).astype(bf16) for r in each]
    fresh_w = [(fresh_exp[r] / total[r]).astype(bf16).astype(f32) for r in each]
    mixed = [jnp.dot(past_w[r], vbuf[r], preferred_element_type=f32) for r in each]
    for r in each:
        spread = jnp.where(diag, mixed[r] + fresh_w[r] * new_v[r : r + 1, :], 0.0)
        small = spread[:, 0:HW]
        for k in range(1, KEY_VALUE_HEADS):
            small = small + spread[:, k * HW : (k + 1) * HW]
        for c in range(T):
            oheads[c, r * ht : (r + 1) * ht, :] = small[c * ht : (c + 1) * ht, :]
    for c in range(T):
        b1[c] = oheads[c].astype(bf16)
    pend = [push({"sec": twin, "tp": c}, b1.at[c], b2_in.at[twin, t], list_head) for c in tp_peers]
    pend.append(push({"sec": twin}, b1.at[t], b2_in.at[twin, t], list_head))
    spare = [(part, r) for part in "kv" for r in range(R)]
    for step in reversed(order):
        c = at_step(*step)
        rows = pl.ds(pl.multiple_of(c * Fs, Fs), Fs)
        fetch(("d", step), w_down.at[rows, :], wd.at[c], spare.pop(0) if spare else None)

    tiles = Dl // 256
    cut = (tiles + 1) // 2
    spans = [(0, cut), (cut, tiles)]

    def fold(value):
        return jnp.concatenate(
            [
                jnp.concatenate([value[:, i : i + 128], value[:, i + 128 : i + 256]], axis=0)
                for i in range(0, value.shape[1], 256)
            ],
            axis=1,
        )

    def unfold(value):
        rows = value.shape[0] // 2
        return jnp.concatenate(
            [
                part
                for i in range(0, value.shape[1], 128)
                for part in (value[:rows, i : i + 128], value[rows:, i : i + 128])
            ],
            axis=1,
        )

    def lanes(span):
        return slice(span[0] * 128, span[1] * 128)

    copies["resid"].wait()
    copies["gain"].wait()
    stream_buf[...] = fold(resid[...].astype(f32))
    gain_rows = fold(jnp.broadcast_to(gain[...].astype(f32).reshape(1, Dl), (G, Dl)))

    pos = jnp.zeros((1, N), f32)
    for a in range(G):
        c, r = a // R, a % R
        held = c + 1 - 2 * (c % 2)
        pos = pos + jnp.where(row_a == float(a), float(held * T * RH + r * ht), 0.0)
    lane = lax.broadcasted_iota(jnp.int32, (1, N), 1)
    for g in range(1, T):
        pos = pos + jnp.where(lane >= g * G, float(RH), 0.0)
    pos_col = jnp.sum(jnp.where(ii == jj, pos, 0.0), axis=1, keepdims=True)
    spot = lax.broadcasted_iota(jnp.int32, (N, S * T * RH), 1).astype(f32)
    for j in range(ht):
        pick_buf[j * N : (j + 1) * N, :] = jnp.where(spot == pos_col + float(j), 1.0, 0.0).astype(bf16)
    arrived(pend)
    pend = [push({"sec": c}, b2_in.at[s], b2_in.at[s], list_gather) for c in sec_peers]
    copies["wo"].wait()
    arrived(pend)
    rows = jnp.concatenate([b2_in[c, g] for c in range(S) for g in range(T)], axis=0)
    placed = jnp.dot(pick_buf[...], rows, preferred_element_type=f32).astype(bf16)
    for j in range(ht):
        ord_buf[:, j * HW : (j + 1) * HW] = placed[j * N : (j + 1) * N]

    def tp_round(out_buf, in_buf, span, slots):
        return [
            push({"tp": g}, out_buf.at[g, :, lanes(span)], in_buf.at[t, :, lanes(span)], slots)
            for g in tp_peers
        ]

    def tp_sum(out_buf, in_buf, span):
        value = out_buf[t, :, lanes(span)].astype(f32)
        for g in tp_peers:
            value = value + in_buf[g, :, lanes(span)].astype(f32)
        return value

    def deal(out_buf, i, value):
        for g in range(T):
            out_buf[g, :, i * 128 : (i + 1) * 128] = fold(value[g * G : (g + 1) * G, :]).astype(bf16)

    pend = []
    for span in spans:
        for i in range(*span):
            deal(
                c_out,
                i,
                jnp.dot(ord_buf[...], wo[:, i * 256 : (i + 1) * 256], preferred_element_type=f32),
            )
        pend.append(tp_round(c_out, c_in, span, list_sum))
    squares = jnp.zeros((G, 1), f32)
    pend_d = []
    for span, copies_in in zip(spans, pend):
        arrived(copies_in)
        stream = stream_buf[:, lanes(span)] + tp_sum(c_out, c_in, span)
        stream_buf[:, lanes(span)] = stream
        d_in[t, :, lanes(span)] = (stream * gain_rows[:, lanes(span)]).astype(bf16)
        piece = d_in.at[t, :, lanes(span)]
        pend_d.append([push({"tp": g}, piece, piece, spread_slots) for g in tp_peers])
        part = jnp.sum(stream * stream, axis=1, keepdims=True)
        squares = squares + part[:G] + part[G:]
    qi = lax.broadcasted_iota(jnp.int32, (G, 128), 0)
    qj = lax.broadcasted_iota(jnp.int32, (G, 128), 1)
    squares = jnp.where(qj == qi + t * G, squares, 0.0)
    q_in[t] = jnp.broadcast_to(jnp.sum(squares, axis=0, keepdims=True), (8, 128))
    pend_q = [push({"tp": g}, q_in.at[t], q_in.at[t], spread_slots) for g in tp_peers]

    def take(span):
        for i in range(*span):
            blks = [d_in[g, :, i * 128 : (i + 1) * 128].astype(f32) for g in range(T)]
            for side in (0, 1):
                cols = slice(i * 256 + side * 128, i * 256 + side * 128 + 128)
                x_buf[:, cols] = jnp.concatenate(
                    [blk[side * G : side * G + G] for blk in blks], axis=0
                ).astype(bf16)

    mate = {"sec": at_step(0, 1)}
    Fh = Fs // NH
    parts = range(NH)
    ready = set()

    def need(step):
        for part in "gu":
            if (part, step) not in ready:
                copies[(part, step)].wait()
                ready.add((part, step))

    def widen(step, h, depth, base=None):
        need(step)
        c = at_step(*step)
        value = [
            jnp.dot(
                x_buf[:, depth],
                weight[c, depth, h * Fh : (h + 1) * Fh],
                preferred_element_type=f32,
            )
            for weight in (wg, wu)
        ]
        value = jnp.concatenate(value, axis=1)
        return value if base is None else base + value

    def unit_cols(h):
        return slice(h * 2 * Fh, (h + 1) * 2 * Fh)

    first, second = [slice(lo * 256, hi * 256) for lo, hi in spans]
    whole = slice(0, Dl)
    far = list(range(1, half))
    arrived(pend_d[0])
    take(spans[0])
    for n, dx in enumerate(far):
        for dc in (0, 1):
            for h in parts:
                far_acc[2 * n + dc, :, unit_cols(h)] = widen((dx, dc), h, first)
    arrived(pend_d[1])
    take(spans[1])
    arrived(pend_q)
    squares = q_in[0]
    for g in range(1, T):
        squares = squares + q_in[g]
    s_in[s] = squares
    pend_s = [push({"sec": c}, s_in.at[s], s_in.at[s], query_slots) for c in sec_peers]
    pair, far_sums = {}, {}
    for n, dx in enumerate(far):
        fx = (sx + dx) % half
        c = at_step(dx, 0)
        for h in parts:
            e_out[c, :, unit_cols(h)] = widen(
                (dx, 0), h, second, far_acc[2 * n, :, unit_cols(h)]
            ).astype(bf16)
            pair[(dx, h)] = push(
                mate, e_out.at[c, :, unit_cols(h)], pair_in.at[fx, :, unit_cols(h)], hop_slots
            )
        for h in parts:
            far_acc[2 * n + 1, :, unit_cols(h)] = widen(
                (dx, 1), h, second, far_acc[2 * n + 1, :, unit_cols(h)]
            )

    def near_mate(h):
        c = at_step(0, 1)
        e_out[c, :, unit_cols(h)] = widen((0, 1), h, whole).astype(bf16)
        pair[(0, h)] = push(mate, e_out.at[c, :, unit_cols(h)], pair_in.at[sx, :, unit_cols(h)], hop_slots)

    near_mate(0)
    for h in parts:
        for n, dx in enumerate(far):
            fx = (sx + dx) % half
            c = at_step(dx, 1)
            pair[(dx, h)].wait_recv()
            e_out[c, :, unit_cols(h)] = (
                far_acc[2 * n + 1, :, unit_cols(h)] + pair_in[fx, :, unit_cols(h)].astype(f32)
            ).astype(bf16)
            far_sums[(dx, h)] = push(
                {"sec": c}, e_out.at[c, :, unit_cols(h)], e_in.at[sx, :, unit_cols(h)], hop_slots
            )
    for h in parts[1:]:
        near_mate(h)
    for h in parts:
        near_acc[:, unit_cols(h)] = widen((0, 0), h, whole)
    arrived(pend_s)
    squares = s_in[0]
    for c in range(1, S):
        squares = squares + s_in[c]
    inverse = lax.rsqrt(squares[0:1, :] / D + 1e-06)
    ni = lax.broadcasted_iota(jnp.int32, (N, 128), 0)
    nj = lax.broadcasted_iota(jnp.int32, (N, 128), 1)
    inverse = jnp.sum(jnp.where(ni == nj, inverse, 0.0), axis=1, keepdims=True)
    to_mate, from_far = [], {}
    for h in parts:
        pair[(0, h)].wait_recv()
        for dx in far:
            far_sums[(dx, h)].wait_recv()
        for j in range(0, Fh, 128):
            both = []
            for lo in (h * 2 * Fh + j, h * 2 * Fh + Fh + j):
                value = near_acc[:, lo : lo + 128] + pair_in[sx, :, lo : lo + 128].astype(f32)
                for dx in far:
                    value = value + e_in[(sx + dx) % half, :, lo : lo + 128].astype(f32)
                both.append(value * inverse)
            gate, upper = both
            f_in[s, :, h * Fh + j : h * Fh + j + 128] = (
                gate / (1.0 + jnp.exp(-gate)) * upper
            ).astype(bf16)
        piece = f_in.at[s, :, h * Fh : (h + 1) * Fh]
        for dx in far:
            from_far[(half - dx, h)] = push({"sec": at_step(dx, 1)}, piece, piece, unit_slots)
        to_mate.append(push(mate, piece, piece, unit_slots))

    def lower(step, units, first=False):
        c = at_step(*step)
        for i in range(tiles):
            cols = slice(i * 256, (i + 1) * 256)
            value = jnp.dot(f_in[c, :, units], wd[c, units, cols], preferred_element_type=f32)
            acc[:, cols] = value if first else acc[:, cols] + value

    for step in order:
        copies[("d", step)].wait()
    all_units = slice(0, Fs)
    lower((0, 0), all_units, True)
    arrived(to_mate)
    lower((0, 1), all_units)
    relayed = {}
    for h in parts:
        for dx in far:
            from_far[(dx, h)].wait_recv()
            piece = f_in.at[at_step(dx, 1), :, h * Fh : (h + 1) * Fh]
            relayed[(dx, h)] = push(mate, piece, piece, unit_slots)
    for dx in far:
        lower((dx, 1), all_units)
    early = slice(0, (NH - 1) * Fh)
    late = slice((NH - 1) * Fh, Fs)
    for dx in far:
        for h in parts[:-1]:
            relayed[(dx, h)].wait_recv()
        lower((dx, 0), early)
    for dx in far[:-1]:
        relayed[(dx, NH - 1)].wait_recv()
        lower((dx, 0), late)
    relayed[(far[-1], NH - 1)].wait_recv()
    c = at_step(far[-1], 0)
    pend = []
    for span in spans:
        for i in range(*span):
            cols = slice(i * 256, (i + 1) * 256)
            value = jnp.dot(f_in[c, :, late], wd[c, late, cols], preferred_element_type=f32)
            deal(g_out, i, acc[:, cols] + value)
        pend.append(tp_round(g_out, g_in, span, sum_slots))
    for span, copies_in in zip(spans, pend):
        arrived(copies_in)
        total = stream_buf[:, lanes(span)] + tp_sum(g_out, g_in, span)
        out[:, span[0] * 256 : span[1] * 256] = unfold(total).astype(bf16)
    for copy in started[-sends:]:
        copy.wait_send()


def local(
    resid,
    query,
    new_kv,
    key_cache,
    cached_value_rows,
    cache_len,
    assign,
    out_weight,
    norm_gain,
    gate_weight,
    up_weight,
    down_weight,
):
    group = query.shape[0]
    per_device = key_cache.shape[0]
    tp_index = lax.axis_index("tp")
    sec_index = lax.axis_index("sec")
    tp_count = lax.axis_size("tp")
    local_slots = lax.dynamic_slice_in_dim(assign, tp_index * group, group)
    full_query, full_pairs = (
        lax.all_gather(query, "sec", axis=1, tiled=True),
        lax.all_gather(new_kv, "sec", axis=1, tiled=True),
    )
    wanted = sec_index * per_device + lax.iota(jnp.int32, per_device)
    picker = (local_slots[None, :] == wanted[:, None]).astype(jnp.bfloat16)
    my_query = jnp.dot(picker, full_query, preferred_element_type=jnp.float32).astype(jnp.bfloat16)
    my_pairs = jnp.dot(picker, full_pairs, preferred_element_type=jnp.float32).astype(jnp.bfloat16)
    attended = attend_slots(my_query, my_pairs, key_cache, cached_value_rows, cache_len)
    request_ids = lax.iota(jnp.int32, group * tp_count)
    slot_block = lax.all_gather(attended, "sec", axis=0, tiled=True)
    received = lax.all_to_all(slot_block, "tp", split_axis=1, concat_axis=0, tiled=True)
    position = request_ids // group * group + assign
    ordered = jnp.take(received, position, axis=0)
    block = ordered
    attn_out = lax.psum_scatter(
        jnp.dot(block, out_weight, preferred_element_type=jnp.float32).astype(jnp.bfloat16),
        "tp",
        scatter_dimension=0,
        tiled=True,
    ).astype(jnp.float32)
    stream = resid.astype(jnp.float32) + attn_out
    squares = lax.psum(jnp.sum(stream * stream, axis=1), "sec")
    inverse = lax.rsqrt(squares / D + 1e-06)
    normed = (stream * inverse[:, None] * norm_gain.astype(jnp.float32)[None, :]).astype(
        jnp.bfloat16
    )
    piece = lax.all_gather(normed, "tp", axis=0, tiled=True)
    gate_part = jnp.dot(piece, gate_weight, preferred_element_type=jnp.float32)
    up_part = jnp.dot(piece, up_weight, preferred_element_type=jnp.float32)
    projected = jnp.concatenate([gate_part, up_part], axis=1)
    width = gate_weight.shape[1]
    share = lax.psum_scatter(
        projected.astype(jnp.bfloat16), "sec", scatter_dimension=0, tiled=True
    ).astype(jnp.float32)
    hidden = lax.all_gather(gated_units(share, width), "sec", axis=0, tiled=True)
    block = hidden
    ff_out = lax.psum_scatter(
        jnp.dot(block, down_weight, preferred_element_type=jnp.float32).astype(jnp.bfloat16),
        "tp",
        scatter_dimension=0,
        tiled=True,
    ).astype(jnp.float32)
    return (stream + ff_out).astype(jnp.bfloat16)


def fused(
    resid,
    query,
    new_kv,
    key_cache,
    cached_value_rows,
    cache_len,
    assign,
    out_weight,
    norm_gain,
    gate_weight,
    up_weight,
    down_weight,
):
    S, T = lax.axis_size("sec"), lax.axis_size("tp")
    G, R = query.shape[0], key_cache.shape[0]
    N = G * T
    RH = up_to(R * (QUERY_HEADS // T), ROWS16)
    RQ = up_to(R * (QUERY_HEADS // S), ROWS16)
    Dl, Hl, F, kvl = resid.shape[1], out_weight.shape[0], gate_weight.shape[1], new_kv.shape[1]
    Fs = F // S
    NH = HIDDEN_PARTS
    landed = 4 * (S - 1) - (S - 1) + T + 2 * (T - 1) + NH * (S - 1)
    spread = max(3 * (T - 1), 2 * (S - 1) + T)
    landed = landed + spread - 2 * (S - 1) - T + max(0, NH * (S - 1) - spread)
    bf16, f32 = jnp.bfloat16, jnp.float32
    V = pltpu.VMEM
    vm = pl.BlockSpec(memory_space=pltpu.VMEM)
    hbm = pl.BlockSpec(memory_space=pl.ANY)
    scratch = [
        V(resid.shape, bf16),
        V(query.shape, bf16),
        V(new_kv.shape, bf16),
        V((1, N), jnp.int32),
        V(norm_gain.shape, bf16),
        pltpu.SMEM(cache_len.shape, jnp.int32),
        V(key_cache.shape, bf16),
        V(cached_value_rows.shape, bf16),
        V((Hl, Dl), bf16),
        V((S, Dl, Fs), bf16),
        V((S, Dl, Fs), bf16),
        V((S, Fs, Dl), bf16),
        V((S, RQ, HEAD_WIDTH), bf16),
        V((S, 8, kvl), bf16),
        V((S, RQ, HEAD_WIDTH), bf16),
        V((S, 8, kvl), bf16),
        V((R, QUERY_HEADS, HEAD_WIDTH), f32),
        V((T, RH, HEAD_WIDTH), f32),
        V((T, RH, HEAD_WIDTH), bf16),
        V((S, T, RH, HEAD_WIDTH), bf16),
        V((QUERY_HEADS // T * N, S * T * RH), bf16),
        V((N, Hl), bf16),
        V((T, 2 * G, Dl // 2), bf16),
        V((T, 2 * G, Dl // 2), bf16),
        V((T, 2 * G, Dl // 2), bf16),
        V((T, 8, 128), f32),
        V((N, Dl), bf16),
        V((S, 8, 128), f32),
        V((S, N, 2 * Fs), bf16),
        V((S // 2, N, 2 * Fs), bf16),
        V((S // 2, N, 2 * Fs), bf16),
        V((S, N, Fs), bf16),
        V((N, Dl), f32),
        V((2 * (S // 2 - 1), N, 2 * Fs), f32),
        V((N, 2 * Fs), f32),
        V((T, 2 * G, Dl // 2), bf16),
        V((T, 2 * G, Dl // 2), bf16),
        V((2 * G, Dl // 2), f32),
        pltpu.SemaphoreType.DMA((2 * R + 4 + 2 * S + max(0, S - 2 * R),)),
        pltpu.SemaphoreType.DMA((SENDS,)),
        pltpu.SemaphoreType.DMA((landed,)),
    ]
    return pl.pallas_call(
        functools.partial(fused_kernel, (S, T, G, R, NH)),
        out_shape=pltpu.VMEM(resid.shape, bf16),
        in_specs=[hbm] * 12,
        out_specs=vm,
        scratch_shapes=scratch,
        compiler_params=pltpu.CompilerParams(
            collective_id=0, has_side_effects=True, vmem_limit_bytes=54 * 2**20
        ),
    )(
        resid,
        query,
        new_kv,
        assign.reshape(1, N),
        norm_gain,
        cache_len,
        key_cache,
        cached_value_rows,
        out_weight,
        gate_weight,
        up_weight,
        down_weight,
    )


def layer(*args):
    query, key_cache, out_weight, gate_weight = args[1], args[3], args[7], args[9]
    shapes = (
        query.shape[0],
        key_cache.shape[0],
        out_weight.shape[0],
        gate_weight.shape[1],
        lax.axis_size("sec"),
        lax.axis_size("tp"),
    )
    return fused(*args) if fits_kernel(shapes) else local(*args)


def solution(mesh):
    return jax.shard_map(
        layer,
        mesh=mesh,
        in_specs=(
            P(("rep", "tp"), "sec"),
            P(("rep", "tp"), "sec"),
            P(("rep", "tp"), "sec"),
            P(("rep", "sec", "tp"), None, None),
            P(("rep", "sec", "tp"), None, None),
            P(("rep", "sec", "tp")),
            P("rep"),
            P("tp", "sec"),
            P("sec"),
            P("sec", "tp"),
            P("sec", "tp"),
            P("tp", "sec"),
        ),
        out_specs=P(("rep", "tp"), "sec"),
        check_vma=False,
    )
```

```python
import functools
import math

import jax
import jax.numpy as jnp
from jax import lax
from jax.experimental import pallas as pl
from jax.experimental.pallas import tpu as pltpu
from jax.sharding import PartitionSpec as P

D = 5120
QUERY_HEADS = 40
KEY_VALUE_HEADS = 8
HEAD_WIDTH = 128
CACHE_SLOTS = 224


def attend_slots(query_rows, key_value_pairs, stored_keys, stored_values, lengths):
    cache_slots = query_rows.shape[0]
    group_query = QUERY_HEADS // KEY_VALUE_HEADS
    query_head_rows = query_rows.reshape(cache_slots, KEY_VALUE_HEADS, group_query, HEAD_WIDTH)
    paired_heads = key_value_pairs.reshape(cache_slots, KEY_VALUE_HEADS, 2, HEAD_WIDTH)
    fresh_keys = paired_heads[:, :, 0]
    fresh_values = paired_heads[:, :, 1]
    earlier_keys = stored_keys.reshape(cache_slots, CACHE_SLOTS, KEY_VALUE_HEADS, HEAD_WIDTH)
    earlier_values = stored_values.reshape(cache_slots, CACHE_SLOTS, KEY_VALUE_HEADS, HEAD_WIDTH)
    scaling = 1.0 / math.sqrt(HEAD_WIDTH)
    past_scores = (
        jnp.einsum(
            "rkgd,rlkd->rkgl", query_head_rows, earlier_keys, preferred_element_type=jnp.float32
        )
        * scaling
    )
    fresh_scores = (
        jnp.einsum("rkgd,rkd->rkg", query_head_rows, fresh_keys, preferred_element_type=jnp.float32)
        * scaling
    )
    valid = lax.broadcasted_iota(jnp.int32, (cache_slots, CACHE_SLOTS), 1) < lengths[:, None]
    past_scores = jnp.where(valid[:, None, None, :], past_scores, -1e30)
    highest = jnp.maximum(jnp.max(past_scores, axis=-1), fresh_scores)
    past_exp = jnp.exp(past_scores - highest[..., None])
    fresh_exp = jnp.exp(fresh_scores - highest)
    denominator = jnp.sum(past_exp, axis=-1) + fresh_exp
    past_weights = (past_exp / denominator[..., None]).astype(jnp.bfloat16)
    fresh_weights = (fresh_exp / denominator).astype(jnp.bfloat16)
    mixed = jnp.einsum(
        "rkgl,rlkd->rkgd", past_weights, earlier_values, preferred_element_type=jnp.float32
    )
    mixed = (
        mixed
        + fresh_weights.astype(jnp.float32)[..., None]
        * fresh_values.astype(jnp.float32)[:, :, None, :]
    )
    return mixed.reshape(cache_slots, QUERY_HEADS * HEAD_WIDTH).astype(jnp.bfloat16)


def gated_units(values, width):
    return (jax.nn.silu(values[:, :width]) * values[:, width:]).astype(jnp.bfloat16)


MESH = pl.DeviceIdType.MESH
ROWS16 = 16
HIDDEN_PARTS = 4
SENDS = 7


def up_to(count, multiple):
    return -(-count // multiple) * multiple


def fits_kernel(shapes):
    group, per_device, head_cols, width, sec, tp = shapes
    return (
        sec % 2 == 0
        and sec >= 4
        and width % (sec * 256 * HIDDEN_PARTS) == 0
        and width % (sec * 256) == 0
        and head_cols % (256) == 0
        and (D // sec) % 256 == 0
        and D // sec >= 512
        and QUERY_HEADS % tp == 0
        and QUERY_HEADS % sec == 0
        and per_device <= 8
        and tp >= 2
        and per_device * sec == group
        and (group * tp) % 16 == 0
        and group * tp <= 128
    )


def fused_kernel(
    dims,
    resid_hbm,
    query_hbm,
    new_kv_hbm,
    assign_hbm,
    gain_hbm,
    lengths_hbm,
    keys,
    values,
    w_out,
    w_gate,
    w_up,
    w_down,
    out,
    resid,
    query,
    new_kv,
    assign,
    gain,
    lengths,
    kbuf,
    vbuf,
    wo,
    wg,
    wu,
    wd,
    a_q,
    a_kv,
    a_q_in,
    a_kv_in,
    qheads,
    oheads,
    b1,
    b2_in,
    pick_buf,
    ord_buf,
    c_out,
    c_in,
    d_in,
    q_in,
    x_buf,
    s_in,
    e_out,
    pair_in,
    e_in,
    f_in,
    acc,
    far_acc,
    near_acc,
    g_out,
    g_in,
    stream_buf,
    local_sem,
    send_sem,
    recv_sem,
):
    S, T, G, R, NH = dims
    N = G * T
    RH = b1.shape[1]
    Dl = resid.shape[1]
    F = w_gate.shape[1]
    Fs = F // S
    f32, bf16 = jnp.float32, jnp.bfloat16
    s = lax.axis_index("sec")
    t = lax.axis_index("tp")
    sx, sc = s // 2, s % 2
    half = S // 2
    steps = [(dx, dc) for dx in list(range(1, half)) + [0] for dc in (0, 1) if dx or dc]
    sec_peers = [((sx + dx) % half) * 2 + (sc + dc) % 2 for dx, dc in steps]
    tp_peers = [(t + k) % T for k in sorted(range(1, T), key=lambda k: -min(k, T - k))]
    if T == 4:
        tp_peers = [T - 1 - t, (t + 2) % T, t + 1 - 2 * (t % 2)]

    twin = sx * 2 + (1 - sc)
    barrier = pltpu.get_barrier_semaphore()
    for c in sec_peers:
        pl.semaphore_signal(barrier, inc=1, device_id={"sec": c}, device_id_type=MESH)
    for c in tp_peers:
        pl.semaphore_signal(barrier, inc=1, device_id={"tp": c}, device_id_type=MESH)
        pl.semaphore_signal(
            barrier, inc=1, device_id={"sec": twin, "tp": c}, device_id_type=MESH
        )

    copies = {}
    count, used = [0], {}

    def fetch(name, src, dst, after=None):
        if after is None:
            slot = count[0]
            count[0] += 1
        else:
            slot = used[after]
        used[name] = slot
        copy = pltpu.make_async_copy(src, dst, local_sem.at[slot])
        copy.start()
        copies[name] = copy

    fetch("assign", assign_hbm, assign)
    fetch("query", query_hbm, query)
    fetch("new_kv", new_kv_hbm, new_kv)
    fetch("lengths", lengths_hbm, lengths)
    fetch("resid", resid_hbm, resid)
    fetch("gain", gain_hbm, gain)
    for r in range(R):
        fetch(("k", r), keys.at[r], kbuf.at[r])
        fetch(("v", r), values.at[r], vbuf.at[r])
    def at_step(dx, dc):
        return ((sx + dx) % half) * 2 + (sc + dc) % 2

    order = [(dx, dc) for dx in list(range(1, half)) + [0] for dc in (1, 0)]

    hs = QUERY_HEADS // S
    ht = QUERY_HEADS // T
    HW = HEAD_WIDTH
    GQ = QUERY_HEADS // KEY_VALUE_HEADS
    GP = up_to(G, ROWS16)
    RQ = a_q.shape[1]
    copies["assign"].wait()
    row_a = assign[...].astype(f32)
    ii = lax.broadcasted_iota(jnp.int32, (N, N), 0)
    jj = lax.broadcasted_iota(jnp.int32, (N, N), 1)
    col_a = jnp.sum(jnp.where(ii == jj, jnp.broadcast_to(row_a, (N, N)), 0.0), axis=1, keepdims=True)

    def own_slots(width):
        pi = lax.broadcasted_iota(jnp.int32, (N, width), 0)
        pj = lax.broadcasted_iota(jnp.int32, (N, width), 1)
        hit = pi == pj + t * G
        if width > G:
            stripe = jnp.zeros((N, width), jnp.int32)
            for j in range(1, width // GP):
                stripe = stripe + jnp.where(pj >= j * GP, GP, 0)
            hit = pi == pj - stripe + t * G
            hit = hit & (pj - stripe < G)
        return jnp.sum(
            jnp.where(hit, jnp.broadcast_to(col_a, (N, width)), 0.0)
            + jnp.where(hit, 1.0, 0.0),
            axis=0,
            keepdims=True,
        ) - 1.0

    pr = lax.broadcasted_iota(jnp.int32, (S * 8, 1), 0)
    slot = jnp.full((S * 8, 1), -2.0, f32)
    for c in range(S):
        for r in range(R):
            slot = jnp.where(pr == c * 8 + r, float(c * R + r), slot)
    picker = jnp.where(
        jnp.broadcast_to(slot, (S * 8, G)) == jnp.broadcast_to(own_slots(G), (S * 8, G)), 1.0, 0.0
    ).astype(bf16)
    qr = lax.broadcasted_iota(jnp.int32, (S * RQ, 1), 0)
    block = jnp.zeros((S * RQ, 1), jnp.int32)
    for c in range(1, S):
        block = block + jnp.where(qr >= c * RQ, 1, 0)
    place = qr - block * RQ
    turn = jnp.zeros((S * RQ, 1), jnp.int32)
    for r in range(1, R):
        turn = turn + jnp.where(place >= r * hs, 1, 0)
    qc = lax.broadcasted_iota(jnp.int32, (1, hs * GP), 1)
    stripe = jnp.zeros((1, hs * GP), jnp.int32)
    for j in range(1, hs):
        stripe = stripe + jnp.where(qc >= j * GP, 1, 0)
    wanted = jnp.where(place < R * hs, block * R + turn, -2).astype(f32)
    q_picker = jnp.where(
        (jnp.broadcast_to(wanted, (S * RQ, hs * GP)) == jnp.broadcast_to(own_slots(hs * GP), (S * RQ, hs * GP)))
        & (jnp.broadcast_to(place - turn * hs, (S * RQ, hs * GP)) == jnp.broadcast_to(stripe, (S * RQ, hs * GP))),
        1.0,
        0.0,
    ).astype(bf16)
    copies["query"].wait()
    tall = query[...].astype(f32)
    if GP > G:
        tall = jnp.concatenate([tall, jnp.zeros((GP - G, Dl), f32)], axis=0)
    stacked = jnp.concatenate([tall[:, j * HW : (j + 1) * HW] for j in range(hs)], axis=0).astype(bf16)
    picked_q = jnp.dot(q_picker, stacked, preferred_element_type=f32).astype(bf16)
    for c in range(S):
        a_q[c] = picked_q[c * RQ : (c + 1) * RQ]
    copies["new_kv"].wait()
    picked_kv = jnp.dot(picker, new_kv[...], preferred_element_type=f32)
    for c in range(S):
        a_kv[c] = picked_kv[c * 8 : c * 8 + 8].astype(bf16)
    pl.semaphore_wait(barrier, len(sec_peers) + 2 * len(tp_peers))

    started = []

    sends = send_sem.shape[0]
    taken = [0]

    def fresh(amount):
        taken[0] += amount
        return list(range(taken[0] - amount, taken[0]))

    query_slots, kv_slots = fresh(S - 1), fresh(S - 1)
    head_slots, gather_slots = fresh(T), fresh(S - 1)
    sum_slots = fresh(2 * (T - 1))
    spread_slots = kv_slots + head_slots + gather_slots
    spread_slots = spread_slots + fresh(max(0, 3 * (T - 1) - len(spread_slots)))
    list_query, list_kv, list_head = list(query_slots), list(kv_slots), list(head_slots)
    list_gather, list_sum = list(gather_slots), list(sum_slots)
    hops = NH * (2 * half - 1)
    hop_slots = fresh(hops)
    unit_slots = list(spread_slots) + fresh(max(0, hops - len(spread_slots)))

    def push(dest, src, dst, slots):
        turn = len(started)
        if turn >= sends:
            started[turn - sends].wait_send()
        copy = pltpu.make_async_remote_copy(
            src_ref=src,
            dst_ref=dst,
            send_sem=send_sem.at[turn % sends],
            recv_sem=recv_sem.at[slots.pop(0)],
            device_id=dest,
            device_id_type=MESH,
        )
        copy.start()
        started.append(copy)
        return copy

    def arrived(pending):
        for copy in pending:
            copy.wait_recv()

    pend = []
    for c in sec_peers:
        pend.append(push({"sec": c}, a_q.at[c], a_q_in.at[s], list_query))
    for c in sec_peers:
        pend.append(push({"sec": c}, a_kv.at[c], a_kv_in.at[s], list_kv))
    a_q_in[s] = a_q[s]
    a_kv_in[s] = a_kv[s]
    oheads[...] = jnp.zeros(oheads.shape, f32)
    for copy in pend:
        copy.wait_recv()

    fetch("wo", w_out, wo, "assign")
    for step in order:
        c = at_step(*step)
        cols = pl.ds(pl.multiple_of(c * Fs, Fs), Fs)
        first = step == order[0]
        fetch(("g", step), w_gate.at[:, cols], wg.at[c], "query" if first else None)
        fetch(("u", step), w_up.at[:, cols], wu.at[c], "new_kv" if first else None)

    copies["lengths"].wait()
    for r in range(R):
        copies[("k", r)].wait()
        copies[("v", r)].wait()
    for c in range(S):
        blk = a_q_in[c].astype(f32)
        for r in range(R):
            qheads[r, c * hs : (c + 1) * hs, :] = blk[r * hs : (r + 1) * hs, :]
    pairs = jnp.concatenate([a_kv_in[c].astype(f32) for c in range(S)], axis=1)
    new_k = jnp.concatenate(
        [pairs[:, 2 * k * HW : (2 * k + 1) * HW] for k in range(KEY_VALUE_HEADS)], axis=1
    )
    new_v = jnp.concatenate(
        [pairs[:, (2 * k + 1) * HW : (2 * k + 2) * HW] for k in range(KEY_VALUE_HEADS)], axis=1
    )
    KW = KEY_VALUE_HEADS * HW
    hrow = lax.broadcasted_iota(jnp.int32, (QUERY_HEADS, KW), 0)
    hcol = lax.broadcasted_iota(jnp.int32, (QUERY_HEADS, KW), 1)
    low = jnp.zeros((QUERY_HEADS, KW), jnp.int32)
    for k in range(1, KEY_VALUE_HEADS):
        low = low + jnp.where(hcol >= k * HW, 1, 0)
    diag = (hrow >= low * GQ) & (hrow < low * GQ + GQ)
    scaling = 1.0 / math.sqrt(HW)
    slots = keys.shape[1]
    each = range(R)
    wide_q = [
        jnp.where(diag, jnp.concatenate([qheads[r]] * KEY_VALUE_HEADS, axis=1), 0.0) for r in each
    ]
    past = [
        lax.dot_general(
            wide_q[r].astype(bf16),
            kbuf[r],
            (((1,), (1,)), ((), ())),
            preferred_element_type=f32,
        )
        * scaling
        for r in each
    ]
    fresh = [
        jnp.sum(wide_q[r] * new_k[r : r + 1, :], axis=1, keepdims=True) * scaling for r in each
    ]
    position = lax.broadcasted_iota(jnp.int32, (QUERY_HEADS, slots), 1)
    past = [jnp.where(position < lengths[r], past[r], -1e30) for r in each]
    highest = [jnp.maximum(jnp.max(past[r], axis=1, keepdims=True), fresh[r]) for r in each]
    past_exp = [jnp.exp(past[r] - highest[r]) for r in each]
    fresh_exp = [jnp.exp(fresh[r] - highest[r]) for r in each]
    total = [jnp.sum(past_exp[r], axis=1, keepdims=True) + fresh_exp[r] for r in each]
    past_w = [(past_exp[r] / total[r]).astype(bf16) for r in each]
    fresh_w = [(fresh_exp[r] / total[r]).astype(bf16).astype(f32) for r in each]
    mixed = [jnp.dot(past_w[r], vbuf[r], preferred_element_type=f32) for r in each]
    for r in each:
        spread = jnp.where(diag, mixed[r] + fresh_w[r] * new_v[r : r + 1, :], 0.0)
        small = spread[:, 0:HW]
        for k in range(1, KEY_VALUE_HEADS):
            small = small + spread[:, k * HW : (k + 1) * HW]
        for c in range(T):
            oheads[c, r * ht : (r + 1) * ht, :] = small[c * ht : (c + 1) * ht, :]
    for c in range(T):
        b1[c] = oheads[c].astype(bf16)
    pend = [push({"sec": twin, "tp": c}, b1.at[c], b2_in.at[twin, t], list_head) for c in tp_peers]
    pend.append(push({"sec": twin}, b1.at[t], b2_in.at[twin, t], list_head))
    spare = [(part, r) for part in "kv" for r in range(R)]
    for step in reversed(order):
        c = at_step(*step)
        rows = pl.ds(pl.multiple_of(c * Fs, Fs), Fs)
        fetch(("d", step), w_down.at[rows, :], wd.at[c], spare.pop(0) if spare else None)

    tiles = Dl // 256
    cut = (tiles + 1) // 2
    spans = [(0, cut), (cut, tiles)]

    def fold(value):
        return jnp.concatenate(
            [
                jnp.concatenate([value[:, i : i + 128], value[:, i + 128 : i + 256]], axis=0)
                for i in range(0, value.shape[1], 256)
            ],
            axis=1,
        )

    def unfold(value):
        rows = value.shape[0] // 2
        return jnp.concatenate(
            [
                part
                for i in range(0, value.shape[1], 128)
                for part in (value[:rows, i : i + 128], value[rows:, i : i + 128])
            ],
            axis=1,
        )

    def lanes(span):
        return slice(span[0] * 128, span[1] * 128)

    copies["resid"].wait()
    copies["gain"].wait()
    stream_buf[...] = fold(resid[...].astype(f32))
    gain_rows = fold(jnp.broadcast_to(gain[...].astype(f32).reshape(1, Dl), (G, Dl)))

    pos = jnp.zeros((1, N), f32)
    for a in range(G):
        c, r = a // R, a % R
        held = c + 1 - 2 * (c % 2)
        pos = pos + jnp.where(row_a == float(a), float(held * T * RH + r * ht), 0.0)
    lane = lax.broadcasted_iota(jnp.int32, (1, N), 1)
    for g in range(1, T):
        pos = pos + jnp.where(lane >= g * G, float(RH), 0.0)
    pos_col = jnp.sum(jnp.where(ii == jj, pos, 0.0), axis=1, keepdims=True)
    spot = lax.broadcasted_iota(jnp.int32, (N, S * T * RH), 1).astype(f32)
    for j in range(ht):
        pick_buf[j * N : (j + 1) * N, :] = jnp.where(spot == pos_col + float(j), 1.0, 0.0).astype(bf16)
    arrived(pend)
    pend = [push({"sec": c}, b2_in.at[s], b2_in.at[s], list_gather) for c in sec_peers]
    copies["wo"].wait()
    arrived(pend)
    rows = jnp.concatenate([b2_in[c, g] for c in range(S) for g in range(T)], axis=0)
    placed = jnp.dot(pick_buf[...], rows, preferred_element_type=f32).astype(bf16)
    for j in range(ht):
        ord_buf[:, j * HW : (j + 1) * HW] = placed[j * N : (j + 1) * N]

    def tp_round(out_buf, in_buf, span, slots):
        return [
            push({"tp": g}, out_buf.at[g, :, lanes(span)], in_buf.at[t, :, lanes(span)], slots)
            for g in tp_peers
        ]

    def tp_sum(out_buf, in_buf, span):
        value = out_buf[t, :, lanes(span)].astype(f32)
        for g in tp_peers:
            value = value + in_buf[g, :, lanes(span)].astype(f32)
        return value

    def deal(out_buf, i, value):
        for g in range(T):
            out_buf[g, :, i * 128 : (i + 1) * 128] = fold(value[g * G : (g + 1) * G, :]).astype(bf16)

    pend = []
    for span in spans:
        for i in range(*span):
            deal(
                c_out,
                i,
                jnp.dot(ord_buf[...], wo[:, i * 256 : (i + 1) * 256], preferred_element_type=f32),
            )
        pend.append(tp_round(c_out, c_in, span, list_sum))
    squares = jnp.zeros((G, 1), f32)
    pend_d = []
    for span, copies_in in zip(spans, pend):
        arrived(copies_in)
        stream = stream_buf[:, lanes(span)] + tp_sum(c_out, c_in, span)
        stream_buf[:, lanes(span)] = stream
        d_in[t, :, lanes(span)] = (stream * gain_rows[:, lanes(span)]).astype(bf16)
        piece = d_in.at[t, :, lanes(span)]
        pend_d.append([push({"tp": g}, piece, piece, spread_slots) for g in tp_peers])
        part = jnp.sum(stream * stream, axis=1, keepdims=True)
        squares = squares + part[:G] + part[G:]
    qi = lax.broadcasted_iota(jnp.int32, (G, 128), 0)
    qj = lax.broadcasted_iota(jnp.int32, (G, 128), 1)
    squares = jnp.where(qj == qi + t * G, squares, 0.0)
    q_in[t] = jnp.broadcast_to(jnp.sum(squares, axis=0, keepdims=True), (8, 128))
    pend_q = [push({"tp": g}, q_in.at[t], q_in.at[t], spread_slots) for g in tp_peers]

    def take(span):
        for i in range(*span):
            blks = [d_in[g, :, i * 128 : (i + 1) * 128].astype(f32) for g in range(T)]
            for side in (0, 1):
                cols = slice(i * 256 + side * 128, i * 256 + side * 128 + 128)
                x_buf[:, cols] = jnp.concatenate(
                    [blk[side * G : side * G + G] for blk in blks], axis=0
                ).astype(bf16)

    mate = {"sec": at_step(0, 1)}
    Fh = Fs // NH
    parts = range(NH)
    ready = set()

    def need(step):
        for part in "gu":
            if (part, step) not in ready:
                copies[(part, step)].wait()
                ready.add((part, step))

    def widen(step, h, depth, base=None):
        need(step)
        c = at_step(*step)
        value = [
            jnp.dot(
                x_buf[:, depth],
                weight[c, depth, h * Fh : (h + 1) * Fh],
                preferred_element_type=f32,
            )
            for weight in (wg, wu)
        ]
        value = jnp.concatenate(value, axis=1)
        return value if base is None else base + value

    def unit_cols(h):
        return slice(h * 2 * Fh, (h + 1) * 2 * Fh)

    first, second = [slice(lo * 256, hi * 256) for lo, hi in spans]
    whole = slice(0, Dl)
    far = list(range(1, half))
    arrived(pend_d[0])
    take(spans[0])
    for n, dx in enumerate(far):
        for dc in (0, 1):
            for h in parts:
                far_acc[2 * n + dc, :, unit_cols(h)] = widen((dx, dc), h, first)
    arrived(pend_d[1])
    take(spans[1])
    arrived(pend_q)
    squares = q_in[0]
    for g in range(1, T):
        squares = squares + q_in[g]
    s_in[s] = squares
    pend_s = [push({"sec": c}, s_in.at[s], s_in.at[s], query_slots) for c in sec_peers]
    pair, far_sums = {}, {}
    for n, dx in enumerate(far):
        fx = (sx + dx) % half
        c = at_step(dx, 0)
        for h in parts:
            e_out[c, :, unit_cols(h)] = widen(
                (dx, 0), h, second, far_acc[2 * n, :, unit_cols(h)]
            ).astype(bf16)
            pair[(dx, h)] = push(
                mate, e_out.at[c, :, unit_cols(h)], pair_in.at[fx, :, unit_cols(h)], hop_slots
            )
        for h in parts:
            far_acc[2 * n + 1, :, unit_cols(h)] = widen(
                (dx, 1), h, second, far_acc[2 * n + 1, :, unit_cols(h)]
            )

    def near_mate(h):
        c = at_step(0, 1)
        e_out[c, :, unit_cols(h)] = widen((0, 1), h, whole).astype(bf16)
        pair[(0, h)] = push(mate, e_out.at[c, :, unit_cols(h)], pair_in.at[sx, :, unit_cols(h)], hop_slots)

    near_mate(0)
    for h in parts:
        for n, dx in enumerate(far):
            fx = (sx + dx) % half
            c = at_step(dx, 1)
            pair[(dx, h)].wait_recv()
            e_out[c, :, unit_cols(h)] = (
                far_acc[2 * n + 1, :, unit_cols(h)] + pair_in[fx, :, unit_cols(h)].astype(f32)
            ).astype(bf16)
            far_sums[(dx, h)] = push(
                {"sec": c}, e_out.at[c, :, unit_cols(h)], e_in.at[sx, :, unit_cols(h)], hop_slots
            )
    for h in parts[1:]:
        near_mate(h)
    for h in parts:
        near_acc[:, unit_cols(h)] = widen((0, 0), h, whole)
    arrived(pend_s)
    squares = s_in[0]
    for c in range(1, S):
        squares = squares + s_in[c]
    inverse = lax.rsqrt(squares[0:1, :] / D + 1e-06)
    ni = lax.broadcasted_iota(jnp.int32, (N, 128), 0)
    nj = lax.broadcasted_iota(jnp.int32, (N, 128), 1)
    inverse = jnp.sum(jnp.where(ni == nj, inverse, 0.0), axis=1, keepdims=True)
    to_mate, from_far = [], {}
    for h in parts:
        pair[(0, h)].wait_recv()
        for dx in far:
            far_sums[(dx, h)].wait_recv()
        for j in range(0, Fh, 128):
            both = []
            for lo in (h * 2 * Fh + j, h * 2 * Fh + Fh + j):
                value = near_acc[:, lo : lo + 128] + pair_in[sx, :, lo : lo + 128].astype(f32)
                for dx in far:
                    value = value + e_in[(sx + dx) % half, :, lo : lo + 128].astype(f32)
                both.append(value * inverse)
            gate, upper = both
            f_in[s, :, h * Fh + j : h * Fh + j + 128] = (
                gate / (1.0 + jnp.exp(-gate)) * upper
            ).astype(bf16)
        piece = f_in.at[s, :, h * Fh : (h + 1) * Fh]
        for dx in far:
            from_far[(half - dx, h)] = push({"sec": at_step(dx, 1)}, piece, piece, unit_slots)
        to_mate.append(push(mate, piece, piece, unit_slots))

    def lower(step, units, first=False):
        c = at_step(*step)
        for i in range(tiles):
            cols = slice(i * 256, (i + 1) * 256)
            value = jnp.dot(f_in[c, :, units], wd[c, units, cols], preferred_element_type=f32)
            acc[:, cols] = value if first else acc[:, cols] + value

    for step in order:
        copies[("d", step)].wait()
    all_units = slice(0, Fs)
    lower((0, 0), all_units, True)
    arrived(to_mate)
    lower((0, 1), all_units)
    relayed = {}
    for h in parts:
        for dx in far:
            from_far[(dx, h)].wait_recv()
            piece = f_in.at[at_step(dx, 1), :, h * Fh : (h + 1) * Fh]
            relayed[(dx, h)] = push(mate, piece, piece, unit_slots)
    for dx in far:
        lower((dx, 1), all_units)
    early = slice(0, (NH - 1) * Fh)
    late = slice((NH - 1) * Fh, Fs)
    for dx in far:
        for h in parts[:-1]:
            relayed[(dx, h)].wait_recv()
        lower((dx, 0), early)
    for dx in far[:-1]:
        relayed[(dx, NH - 1)].wait_recv()
        lower((dx, 0), late)
    relayed[(far[-1], NH - 1)].wait_recv()
    c = at_step(far[-1], 0)
    pend = []
    for span in spans:
        for i in range(*span):
            cols = slice(i * 256, (i + 1) * 256)
            value = jnp.dot(f_in[c, :, late], wd[c, late, cols], preferred_element_type=f32)
            deal(g_out, i, acc[:, cols] + value)
        pend.append(tp_round(g_out, g_in, span, sum_slots))
    for span, copies_in in zip(spans, pend):
        arrived(copies_in)
        total = stream_buf[:, lanes(span)] + tp_sum(g_out, g_in, span)
        out[:, span[0] * 256 : span[1] * 256] = unfold(total).astype(bf16)
    for copy in started[-sends:]:
        copy.wait_send()


def local(
    resid,
    query,
    new_kv,
    key_cache,
    cached_value_rows,
    cache_len,
    assign,
    out_weight,
    norm_gain,
    gate_weight,
    up_weight,
    down_weight,
):
    group = query.shape[0]
    per_device = key_cache.shape[0]
    tp_index = lax.axis_index("tp")
    sec_index = lax.axis_index("sec")
    tp_count = lax.axis_size("tp")
    local_slots = lax.dynamic_slice_in_dim(assign, tp_index * group, group)
    full_query, full_pairs = (
        lax.all_gather(query, "sec", axis=1, tiled=True),
        lax.all_gather(new_kv, "sec", axis=1, tiled=True),
    )
    wanted = sec_index * per_device + lax.iota(jnp.int32, per_device)
    picker = (local_slots[None, :] == wanted[:, None]).astype(jnp.bfloat16)
    my_query = jnp.dot(picker, full_query, preferred_element_type=jnp.float32).astype(jnp.bfloat16)
    my_pairs = jnp.dot(picker, full_pairs, preferred_element_type=jnp.float32).astype(jnp.bfloat16)
    attended = attend_slots(my_query, my_pairs, key_cache, cached_value_rows, cache_len)
    request_ids = lax.iota(jnp.int32, group * tp_count)
    slot_block = lax.all_gather(attended, "sec", axis=0, tiled=True)
    received = lax.all_to_all(slot_block, "tp", split_axis=1, concat_axis=0, tiled=True)
    position = request_ids // group * group + assign
    ordered = jnp.take(received, position, axis=0)
    block = ordered
    attn_out = lax.psum_scatter(
        jnp.dot(block, out_weight, preferred_element_type=jnp.float32).astype(jnp.bfloat16),
        "tp",
        scatter_dimension=0,
        tiled=True,
    ).astype(jnp.float32)
    stream = resid.astype(jnp.float32) + attn_out
    squares = lax.psum(jnp.sum(stream * stream, axis=1), "sec")
    inverse = lax.rsqrt(squares / D + 1e-06)
    normed = (stream * inverse[:, None] * norm_gain.astype(jnp.float32)[None, :]).astype(
        jnp.bfloat16
    )
    piece = lax.all_gather(normed, "tp", axis=0, tiled=True)
    gate_part = jnp.dot(piece, gate_weight, preferred_element_type=jnp.float32)
    up_part = jnp.dot(piece, up_weight, preferred_element_type=jnp.float32)
    projected = jnp.concatenate([gate_part, up_part], axis=1)
    width = gate_weight.shape[1]
    share = lax.psum_scatter(
        projected.astype(jnp.bfloat16), "sec", scatter_dimension=0, tiled=True
    ).astype(jnp.float32)
    hidden = lax.all_gather(gated_units(share, width), "sec", axis=0, tiled=True)
    block = hidden
    ff_out = lax.psum_scatter(
        jnp.dot(block, down_weight, preferred_element_type=jnp.float32).astype(jnp.bfloat16),
        "tp",
        scatter_dimension=0,
        tiled=True,
    ).astype(jnp.float32)
    return (stream + ff_out).astype(jnp.bfloat16)


def fused(
    resid,
    query,
    new_kv,
    key_cache,
    cached_value_rows,
    cache_len,
    assign,
    out_weight,
    norm_gain,
    gate_weight,
    up_weight,
    down_weight,
):
    S, T = lax.axis_size("sec"), lax.axis_size("tp")
    G, R = query.shape[0], key_cache.shape[0]
    N = G * T
    RH = up_to(R * (QUERY_HEADS // T), ROWS16)
    RQ = up_to(R * (QUERY_HEADS // S), ROWS16)
    Dl, Hl, F, kvl = resid.shape[1], out_weight.shape[0], gate_weight.shape[1], new_kv.shape[1]
    Fs = F // S
    NH = HIDDEN_PARTS
    landed = 4 * (S - 1) - (S - 1) + T + 2 * (T - 1) + NH * (S - 1)
    spread = max(3 * (T - 1), 2 * (S - 1) + T)
    landed = landed + spread - 2 * (S - 1) - T + max(0, NH * (S - 1) - spread)
    bf16, f32 = jnp.bfloat16, jnp.float32
    V = pltpu.VMEM
    vm = pl.BlockSpec(memory_space=pltpu.VMEM)
    hbm = pl.BlockSpec(memory_space=pl.ANY)
    scratch = [
        V(resid.shape, bf16),
        V(query.shape, bf16),
        V(new_kv.shape, bf16),
        V((1, N), jnp.int32),
        V(norm_gain.shape, bf16),
        pltpu.SMEM(cache_len.shape, jnp.int32),
        V(key_cache.shape, bf16),
        V(cached_value_rows.shape, bf16),
        V((Hl, Dl), bf16),
        V((S, Dl, Fs), bf16),
        V((S, Dl, Fs), bf16),
        V((S, Fs, Dl), bf16),
        V((S, RQ, HEAD_WIDTH), bf16),
        V((S, 8, kvl), bf16),
        V((S, RQ, HEAD_WIDTH), bf16),
        V((S, 8, kvl), bf16),
        V((R, QUERY_HEADS, HEAD_WIDTH), f32),
        V((T, RH, HEAD_WIDTH), f32),
        V((T, RH, HEAD_WIDTH), bf16),
        V((S, T, RH, HEAD_WIDTH), bf16),
        V((QUERY_HEADS // T * N, S * T * RH), bf16),
        V((N, Hl), bf16),
        V((T, 2 * G, Dl // 2), bf16),
        V((T, 2 * G, Dl // 2), bf16),
        V((T, 2 * G, Dl // 2), bf16),
        V((T, 8, 128), f32),
        V((N, Dl), bf16),
        V((S, 8, 128), f32),
        V((S, N, 2 * Fs), bf16),
        V((S // 2, N, 2 * Fs), bf16),
        V((S // 2, N, 2 * Fs), bf16),
        V((S, N, Fs), bf16),
        V((N, Dl), f32),
        V((2 * (S // 2 - 1), N, 2 * Fs), f32),
        V((N, 2 * Fs), f32),
        V((T, 2 * G, Dl // 2), bf16),
        V((T, 2 * G, Dl // 2), bf16),
        V((2 * G, Dl // 2), f32),
        pltpu.SemaphoreType.DMA((2 * R + 4 + 2 * S + max(0, S - 2 * R),)),
        pltpu.SemaphoreType.DMA((SENDS,)),
        pltpu.SemaphoreType.DMA((landed,)),
    ]
    return pl.pallas_call(
        functools.partial(fused_kernel, (S, T, G, R, NH)),
        out_shape=pltpu.VMEM(resid.shape, bf16),
        in_specs=[hbm] * 12,
        out_specs=vm,
        scratch_shapes=scratch,
        compiler_params=pltpu.CompilerParams(
            collective_id=0, has_side_effects=True, vmem_limit_bytes=54 * 2**20
        ),
    )(
        resid,
        query,
        new_kv,
        assign.reshape(1, N),
        norm_gain,
        cache_len,
        key_cache,
        cached_value_rows,
        out_weight,
        gate_weight,
        up_weight,
        down_weight,
    )


def layer(*args):
    query, key_cache, out_weight, gate_weight = args[1], args[3], args[7], args[9]
    shapes = (
        query.shape[0],
        key_cache.shape[0],
        out_weight.shape[0],
        gate_weight.shape[1],
        lax.axis_size("sec"),
        lax.axis_size("tp"),
    )
    return fused(*args) if fits_kernel(shapes) else local(*args)


def solution(mesh):
    return jax.shard_map(
        layer,
        mesh=mesh,
        in_specs=(
            P(("rep", "tp"), "sec"),
            P(("rep", "tp"), "sec"),
            P(("rep", "tp"), "sec"),
            P(("rep", "sec", "tp"), None, None),
            P(("rep", "sec", "tp"), None, None),
            P(("rep", "sec", "tp")),
            P("rep"),
            P("tp", "sec"),
            P("sec"),
            P("sec", "tp"),
            P("sec", "tp"),
            P("tp", "sec"),
        ),
        out_specs=P(("rep", "tp"), "sec"),
        check_vma=False,
    )
```
